32 devices in a mesh: dp: 4 (over y, x), fsdp: 8 (over z, core).
Axes of the slice: x: 2, y: 2, z: 4, core: 2. Of those that a mesh axis runs over, the one named last changes fastest.
Arguments:
- spectra: bfloat16 [32, 80, 128], P(('dp', 'fsdp')), may hold values from -6 to 6
- gaussian: bfloat16 [32, 80, 128], P(('dp', 'fsdp')), may hold values from -6 to 6
- flow_times: float32 [32], P(('dp', 'fsdp')), may hold values from 0 to 1
- lengths: int32 [32], P(('dp', 'fsdp')), may hold values from 32 to 128, as said below
- span_flags: int32 [32, 128], P(('dp', 'fsdp')), may hold values from 0 to 1, as said below
- phone_ids: int32 [32, 128], P(('dp', 'fsdp')), may hold values from 0 to 95
- input_master: float32 [256, 1024], P(None, ('dp', 'fsdp')), may hold values from -0.625 to 0.625
- input_moment: float32 [256, 1024], P(None, ('dp', 'fsdp')), may hold values from -2.2888184e-05 to 2.2888184e-05
- input_square: float32 [256, 1024], P(None, ('dp', 'fsdp')), may hold values from 3.542059e-11 to 5.6672944e-10
- kernel_master: float32 [31, 1024, 64], P(None, ('dp', 'fsdp')), may hold values from -0.125 to 0.125
- kernel_moment: float32 [31, 1024, 64], P(None, ('dp', 'fsdp')), may hold values from -2.2888184e-05 to 2.2888184e-05
- kernel_square: float32 [31, 1024, 64], P(None, ('dp', 'fsdp')), may hold values from 3.542059e-11 to 5.6672944e-10
- joint_master: float32 [2, 1024, 3072], P(None, ('dp', 'fsdp')), may hold values from -0.1875 to 0.1875
- joint_moment: float32 [2, 1024, 3072], P(None, ('dp', 'fsdp')), may hold values from -2.2888184e-05 to 2.2888184e-05
- joint_square: float32 [2, 1024, 3072], P(None, ('dp', 'fsdp')), may hold values from 3.542059e-11 to 5.6672944e-10
- output_master: float32 [2, 1024, 1024], P(None, ('dp', 'fsdp')), may hold values from -0.5 to 0.5
- output_moment: float32 [2, 1024, 1024], P(None, ('dp', 'fsdp')), may hold values from -2.2888184e-05 to 2.2888184e-05
- output_square: float32 [2, 1024, 1024], P(None, ('dp', 'fsdp')), may hold values from 3.542059e-11 to 5.6672944e-10
- expand_master: float32 [2, 1024, 4096], P(None, ('dp', 'fsdp')), may hold values from -0.1875 to 0.1875
- expand_moment: float32 [2, 1024, 4096], P(None, ('dp', 'fsdp')), may hold values from -2.2888184e-05 to 2.2888184e-05
- expand_square: float32 [2, 1024, 4096], P(None, ('dp', 'fsdp')), may hold values from 3.542059e-11 to 5.6672944e-10
- reduce_master: float32 [2, 4096, 1024], P(None, ('dp', 'fsdp')), may hold values from -0.09375 to 0.09375
- reduce_moment: float32 [2, 4096, 1024], P(None, ('dp', 'fsdp')), may hold values from -2.2888184e-05 to 2.2888184e-05
- reduce_square: float32 [2, 4096, 1024], P(None, ('dp', 'fsdp')), may hold values from 3.542059e-11 to 5.6672944e-10
- bridge_master: float32 [2048, 1024], P(('dp', 'fsdp')), may hold values from -0.125 to 0.125
- bridge_moment: float32 [2048, 1024], P(('dp', 'fsdp')), may hold values from -2.2888184e-05 to 2.2888184e-05
- bridge_square: float32 [2048, 1024], P(('dp', 'fsdp')), may hold values from 3.542059e-11 to 5.6672944e-10
- readout_master: float32 [1024, 80], P(('dp', 'fsdp')), may hold values from -0.1875 to 0.1875
- readout_moment: float32 [1024, 80], P(('dp', 'fsdp')), may hold values from -2.2888184e-05 to 2.2888184e-05
- readout_square: float32 [1024, 80], P(('dp', 'fsdp')), may hold values from 3.542059e-11 to 5.6672944e-10
- gains_master: float32 [5, 1024], P(None, ('dp', 'fsdp')), may hold values from 0.3 to 2.5
- gains_moment: float32 [5, 1024], P(None, ('dp', 'fsdp')), may hold values from -0.00048828125 to 0.00048828125
- gains_square: float32 [5, 1024], P(None, ('dp', 'fsdp')), may hold values from 3.3733893e-09 to 2.0240336e-08
Outputs:
- loss_sum: float32 [], replicated
- frame_total: float32 [], replicated
- grad_norm: float32 [], replicated
- input_first: float32 [256, 1024], P(None, ('dp', 'fsdp'))
- input_second: float32 [256, 1024], P(None, ('dp', 'fsdp'))
- input_updated: float32 [256, 1024], P(None, ('dp', 'fsdp'))
- kernel_first: float32 [31, 1024, 64], P(None, ('dp', 'fsdp'))
- kernel_second: float32 [31, 1024, 64], P(None, ('dp', 'fsdp'))
- kernel_updated: float32 [31, 1024, 64], P(None, ('dp', 'fsdp'))
- joint_first: float32 [2, 1024, 3072], P(None, ('dp', 'fsdp'))
- joint_second: float32 [2, 1024, 3072], P(None, ('dp', 'fsdp'))
- joint_updated: float32 [2, 1024, 3072], P(None, ('dp', 'fsdp'))
- output_first: float32 [2, 1024, 1024], P(None, ('dp', 'fsdp'))
- output_second: float32 [2, 1024, 1024], P(None, ('dp', 'fsdp'))
- output_updated: float32 [2, 1024, 1024], P(None, ('dp', 'fsdp'))
- expand_first: float32 [2, 1024, 4096], P(None, ('dp', 'fsdp'))
- expand_second: float32 [2, 1024, 4096], P(None, ('dp', 'fsdp'))
- expand_updated: float32 [2, 1024, 4096], P(None, ('dp', 'fsdp'))
- reduce_first: float32 [2, 4096, 1024], P(None, ('dp', 'fsdp'))
- reduce_second: float32 [2, 4096, 1024], P(None, ('dp', 'fsdp'))
- reduce_updated: float32 [2, 4096, 1024], P(None, ('dp', 'fsdp'))
- bridge_first: float32 [2048, 1024], P(('dp', 'fsdp'))
- bridge_second: float32 [2048, 1024], P(('dp', 'fsdp'))
- bridge_updated: float32 [2048, 1024], P(('dp', 'fsdp'))
- readout_first: float32 [1024, 80], P(('dp', 'fsdp'))
- readout_second: float32 [1024, 80], P(('dp', 'fsdp'))
- readout_updated: float32 [1024, 80], P(('dp', 'fsdp'))
- gains_first: float32 [5, 1024], P(None, ('dp', 'fsdp'))
- gains_second: float32 [5, 1024], P(None, ('dp', 'fsdp'))
- gains_updated: float32 [5, 1024], P(None, ('dp', 'fsdp'))
The draws below stay inside these ranges and needn't reach their ends.
Inputs may be any that keep to these rules, and one draw needn't show every extreme that they name: `lengths`: frames of each utterance; some utterance is 128 frames long. `span_flags`: within each utterance one run of frames inside its length, covering at least seven tenths of it, rounded down, is 1; everything else is 0.
All inputs are finite; a program needn't handle non-finite values.
Results may differ from the reference program's by a relative error of at most 0.017.
Values may be sent and summed in bfloat16 or wider, within the bound.
No kernel may reach another device: no remote copies, remote signals or barrier semaphores. Data moves between devices by JAX's collectives and lax.ppermute only.
A program may use at most 448 MiB of HBM per device.

```python
import math
import jax
import jax.numpy as jnp
from jax import lax

D = 1024
HEADS = 16
FF = 4096
MEL = 80
VOCAB = 96
KS = 31
GROUPS = 16
LAYERS = 2
STEP = 10
LEN = 128
SEQ_DEV = 1
SEQS = 32
PARAMS = 29643776
N_DP = 4
N_FSDP = 8


def length_law(key):
    places = jnp.arange(SEQS, dtype=jnp.int32) // SEQ_DEV
    outer = places // N_FSDP
    inner = places % N_FSDP
    lowest = LEN // 4
    rising = lowest + (LEN - lowest) * (outer * (N_FSDP - 1) + inner * (N_DP - 1)) // (2 * (N_DP - 1) * (N_FSDP - 1))
    jitter = jax.random.randint(key, (SEQS,), 0, max(LEN // 8, 2))
    jitter = jnp.where(jnp.arange(SEQS) == SEQS - 1, 0, jitter)
    return jnp.maximum(rising - jitter, lowest).astype(jnp.int32)


def draw_lengths(key, part):
    return length_law(key)


def draw_span_flags(key, part):
    lengths = length_law(key)
    key = jax.random.fold_in(key, 2)
    first_key, second_key = jax.random.split(key)
    least = lengths * 7 // 10
    extra = jax.random.randint(first_key, (SEQS,), 0, 1 << 20) % (lengths * 3 // 10 + 1)
    covered = least + extra
    begin = jax.random.randint(second_key, (SEQS,), 0, 1 << 20) % (lengths - covered + 1)
    places = jnp.arange(LEN)[None, :]
    inside = (places >= begin[:, None]) & (places < (begin + covered)[:, None])
    return inside.astype(jnp.int32)


def draw_gains_master(key, part):
    key = jax.random.fold_in(key, 3)
    columns = jnp.arange(D, dtype=jnp.float32) / D
    ramp = 0.5 + columns
    jolt = jax.random.uniform(key, (2 * LAYERS + 1, D), jnp.float32, 0.85, 1.15)
    return ramp[None, :] * jolt


def plant(values, rng, smallest, high):
    index_at = [jax.random.randint(jax.random.fold_in(rng, axis), (), 0, length) for axis, length in enumerate(values.shape)]
    longest = values.shape.index(max(values.shape))
    beside = index_at[:longest] + [(index_at[longest] + 1) % values.shape[longest]] + index_at[longest + 1:]
    return values.at[tuple(index_at)].set(smallest).at[tuple(beside)].set(high)


def block_levels(key, extent, cuts, low, high):
    loudness = 1.0
    for position, shards_of in cuts:
        heights = jax.random.uniform(jax.random.fold_in(jax.random.fold_in(key, 6), position), (shards_of,), jnp.float32, low / len(cuts), high / len(cuts))
        loudness = loudness * jnp.repeat(jnp.exp(heights), extent[position] // shards_of).reshape((-1,) + (1,) * (len(extent) - 1 - position))
    return loudness


def normal_values(rng, shape, width, most, pieces=(), held_as=jnp.bfloat16):
    result = width * jax.random.normal(rng, shape, jnp.float32)
    if pieces:
        result = result * block_levels(rng, shape, pieces, -0.22, 0.18)
    return jnp.clip(result, -most, most).astype(held_as)


def setup_inputs(seed: int = 0) -> dict:
    splits = jax.random.split(jax.random.key(seed), 34)
    spectra = normal_values(splits[0], (SEQS, MEL, LEN), 1.0, 6.0, ((0, 32),))
    gaussian = normal_values(splits[1], (SEQS, MEL, LEN), 1.0, 6.0, ((0, 32),))
    flow_times = jnp.clip(1.0 * jax.random.uniform(splits[2], (SEQS,), jnp.float32) ** block_levels(splits[2], (SEQS,), ((0, 32),), -0.2, 0.2), 0.0, 1.0)
    lengths = draw_lengths(jax.random.fold_in(splits[33], 71), 0)
    span_flags = draw_span_flags(jax.random.fold_in(splits[33], 71), 0)
    phone_ids = plant(jax.random.randint(splits[5], (SEQS, LEN), 0, VOCAB), jax.random.fold_in(splits[5], 1), 0, VOCAB - 1).astype(jnp.int32)
    input_master = normal_values(splits[6], (2 * MEL + VOCAB, D), MEL ** -0.5, 0.625, ((1, 32),), jnp.float32)
    input_moment = normal_values(splits[7], (2 * MEL + VOCAB, D), (0.022 / PARAMS ** 0.5), 2.288818359375e-05, ((1, 32),), jnp.float32)
    input_square = jnp.clip(jnp.exp(math.log(5.667294411537682e-10) - 2.7725887 * jax.random.uniform(splits[8], (2 * MEL + VOCAB, D), jnp.float32) ** block_levels(splits[8], (2 * MEL + VOCAB, D), ((1, 32),), -0.2, 0.2)), 3.5420590072110514e-11, 5.667294411537682e-10)
    kernel_master = normal_values(splits[9], (KS, D, D // GROUPS), (KS * (D // GROUPS)) ** -0.5, 0.125, ((1, 32),), jnp.float32)
    kernel_moment = normal_values(splits[10], (KS, D, D // GROUPS), (0.022 / PARAMS ** 0.5), 2.288818359375e-05, ((1, 32),), jnp.float32)
    kernel_square = jnp.clip(jnp.exp(math.log(5.667294411537682e-10) - 2.7725887 * jax.random.uniform(splits[11], (KS, D, D // GROUPS), jnp.float32) ** block_levels(splits[11], (KS, D, D // GROUPS), ((1, 32),), -0.2, 0.2)), 3.5420590072110514e-11, 5.667294411537682e-10)
    joint_master = normal_values(splits[12], (LAYERS, D, 3 * D), D ** -0.5, 0.1875, ((1, 32),), jnp.float32)
    joint_moment = normal_values(splits[13], (LAYERS, D, 3 * D), (0.022 / PARAMS ** 0.5), 2.288818359375e-05, ((1, 32),), jnp.float32)
    joint_square = jnp.clip(jnp.exp(math.log(5.667294411537682e-10) - 2.7725887 * jax.random.uniform(splits[14], (LAYERS, D, 3 * D), jnp.float32) ** block_levels(splits[14], (LAYERS, D, 3 * D), ((1, 32),), -0.2, 0.2)), 3.5420590072110514e-11, 5.667294411537682e-10)
    output_master = normal_values(splits[15], (LAYERS, D, D), (D // 8) ** -0.5, 0.5, ((1, 32),), jnp.float32)
    output_moment = normal_values(splits[16], (LAYERS, D, D), (0.022 / PARAMS ** 0.5), 2.288818359375e-05, ((1, 32),), jnp.float32)
    output_square = jnp.clip(jnp.exp(math.log(5.667294411537682e-10) - 2.7725887 * jax.random.uniform(splits[17], (LAYERS, D, D), jnp.float32) ** block_levels(splits[17], (LAYERS, D, D), ((1, 32),), -0.2, 0.2)), 3.5420590072110514e-11, 5.667294411537682e-10)
    expand_master = normal_values(splits[18], (LAYERS, D, FF), D ** -0.5, 0.1875, ((1, 32),), jnp.float32)
    expand_moment = normal_values(splits[19], (LAYERS, D, FF), (0.022 / PARAMS ** 0.5), 2.288818359375e-05, ((1, 32),), jnp.float32)
    expand_square = jnp.clip(jnp.exp(math.log(5.667294411537682e-10) - 2.7725887 * jax.random.uniform(splits[20], (LAYERS, D, FF), jnp.float32) ** block_levels(splits[20], (LAYERS, D, FF), ((1, 32),), -0.2, 0.2)), 3.5420590072110514e-11, 5.667294411537682e-10)
    reduce_master = normal_values(splits[21], (LAYERS, FF, D), FF ** -0.5, 0.09375, ((1, 32),), jnp.float32)
    reduce_moment = normal_values(splits[22], (LAYERS, FF, D), (0.022 / PARAMS ** 0.5), 2.288818359375e-05, ((1, 32),), jnp.float32)
    reduce_square = jnp.clip(jnp.exp(math.log(5.667294411537682e-10) - 2.7725887 * jax.random.uniform(splits[23], (LAYERS, FF, D), jnp.float32) ** block_levels(splits[23], (LAYERS, FF, D), ((1, 32),), -0.2, 0.2)), 3.5420590072110514e-11, 5.667294411537682e-10)
    bridge_master = normal_values(splits[24], (2 * D, D), (2 * D) ** -0.5, 0.125, ((0, 32),), jnp.float32)
    bridge_moment = normal_values(splits[25], (2 * D, D), (0.022 / PARAMS ** 0.5), 2.288818359375e-05, ((0, 32),), jnp.float32)
    bridge_square = jnp.clip(jnp.exp(math.log(5.667294411537682e-10) - 2.7725887 * jax.random.uniform(splits[26], (2 * D, D), jnp.float32) ** block_levels(splits[26], (2 * D, D), ((0, 32),), -0.2, 0.2)), 3.5420590072110514e-11, 5.667294411537682e-10)
    readout_master = normal_values(splits[27], (D, MEL), D ** -0.5, 0.1875, ((0, 32),), jnp.float32)
    readout_moment = normal_values(splits[28], (D, MEL), (0.022 / PARAMS ** 0.5), 2.288818359375e-05, ((0, 32),), jnp.float32)
    readout_square = jnp.clip(jnp.exp(math.log(5.667294411537682e-10) - 2.7725887 * jax.random.uniform(splits[29], (D, MEL), jnp.float32) ** block_levels(splits[29], (D, MEL), ((0, 32),), -0.2, 0.2)), 3.5420590072110514e-11, 5.667294411537682e-10)
    gains_master = draw_gains_master(jax.random.fold_in(splits[33], 71), 0)
    gains_moment = normal_values(splits[31], (2 * LAYERS + 1, D), (0.44 / PARAMS ** 0.5), 0.00048828125, ((1, 32),), jnp.float32)
    gains_square = jnp.clip(jnp.exp(math.log(2.0240335629750916e-08) - 1.79175945 * jax.random.uniform(splits[32], (2 * LAYERS + 1, D), jnp.float32) ** block_levels(splits[32], (2 * LAYERS + 1, D), ((1, 32),), -0.2, 0.2)), 3.373389345640021e-09, 2.0240335629750916e-08)
    return {"spectra": spectra, "gaussian": gaussian, "flow_times": flow_times, "lengths": lengths, "span_flags": span_flags, "phone_ids": phone_ids, "input_master": input_master, "input_moment": input_moment, "input_square": input_square, "kernel_master": kernel_master, "kernel_moment": kernel_moment, "kernel_square": kernel_square, "joint_master": joint_master, "joint_moment": joint_moment, "joint_square": joint_square, "output_master": output_master, "output_moment": output_moment, "output_square": output_square, "expand_master": expand_master, "expand_moment": expand_moment, "expand_square": expand_square, "reduce_master": reduce_master, "reduce_moment": reduce_moment, "reduce_square": reduce_square, "bridge_master": bridge_master, "bridge_moment": bridge_moment, "bridge_square": bridge_square, "readout_master": readout_master, "readout_moment": readout_moment, "readout_square": readout_square, "gains_master": gains_master, "gains_moment": gains_moment, "gains_square": gains_square}


@jax.custom_vjp
def low(v):
    return lax.optimization_barrier(v.astype(jnp.bfloat16)).astype(jnp.float32)

@jax.custom_vjp
def low_back(v):
    return v

def low_keep(v):
    return (low(v), None)

def low_pass(kept, grad):
    return (grad,)

def back_keep(v):
    return (v, None)

def back_low(kept, grad):
    return (low(grad),)
low.defvjp(low_keep, low_pass)
low_back.defvjp(back_keep, back_low)
FULL_PRECISION = lax.Precision.HIGHEST
SIGMA_MIN = 1e-05
NORM_EPS = 1e-05
MASKED = -1e+30
BETA_ONE = 0.9
BETA_TWO = 0.95
ADAM_EPS = 1e-08
DECAY_RATE = 0.01
CLIP_LIMIT = 0.2
RATE_SCALE = 0.5
GAIN_RATE = 0.25

def rounded(values):
    return low(low_back(values))

def layer_norm(values, gain_row):
    center = values - lax.optimization_barrier(jnp.mean(values, -1, keepdims=True))
    spread = lax.optimization_barrier(jnp.mean(center * center, -1, keepdims=True))
    return center * lax.rsqrt(spread + NORM_EPS) * gain_row

def project(values, matrix):
    return jnp.einsum('...i,ij->...j', values, matrix, precision=FULL_PRECISION)

def alibi_bias(frames):
    slopes = 2.0 ** (-8.0 * (jnp.arange(HEADS, dtype=jnp.float32) + 1.0) / HEADS)
    places = jnp.arange(frames, dtype=jnp.float32)
    return -slopes[:, None, None] * jnp.abs(places[:, None] - places[None, :])

def conv_mix(hidden, kernel):
    tap_count = kernel.shape[0]
    margin = tap_count // 2
    seq_count, frame_count, model_width = hidden.shape
    per_group = model_width // GROUPS
    padded = jnp.pad(hidden, ((0, 0), (margin, margin), (0, 0)))
    stacked = jnp.stack([padded[:, tap:tap + frame_count] for tap in range(tap_count)], 1)
    stacked = stacked.reshape(seq_count, tap_count, frame_count, GROUPS, per_group)
    weights = kernel.reshape(tap_count, GROUPS, per_group, per_group)
    mixed = jnp.einsum('bklgc,kgoc->blgo', stacked, weights, precision=FULL_PRECISION)
    return mixed.reshape(seq_count, frame_count, model_width)

def attend(joint, valid, alibi):
    seq_count, frame_count, triple = joint.shape
    head_size = triple // (3 * HEADS)
    parts = joint.reshape(seq_count, frame_count, 3, HEADS, head_size)
    scores = jnp.einsum('sqhd,skhd->shqk', parts[:, :, 0], parts[:, :, 1], precision=FULL_PRECISION)
    scores = scores * head_size ** (-0.5) + alibi[None]
    scores = low_back(jnp.where(valid[:, None, None, :], scores, MASKED))
    weights = jax.nn.softmax(scores, -1)
    mixed = jnp.einsum('shqk,skhd->sqhd', low(weights), parts[:, :, 2], precision=FULL_PRECISION)
    return rounded(mixed.reshape(seq_count, frame_count, triple // 3))

def layer(stream, mats, gain_one, gain_two, valid, alibi):
    joint_w, output_w, expand_w, reduce_w = mats
    joint = rounded(project(low(layer_norm(stream, gain_one)), joint_w))
    stream = stream + low_back(project(attend(joint, valid, alibi), output_w))
    upper = low_back(project(low(layer_norm(stream, gain_two)), expand_w))
    return stream + low_back(project(low(jax.nn.gelu(upper)), reduce_w))

def group_loss(params, spectra, gaussian, flow_times, lengths, span_flags, phone_ids):
    input_weight, kernel_w, joint_w, output_w, expand_w, reduce_w, bridge_w, readout_w, gains_w = params
    frame_count = spectra.shape[2]
    valid = jnp.arange(frame_count)[None, :] < lengths[:, None]
    flags = span_flags.astype(jnp.float32)
    scaled = flow_times[:, None, None]
    noisy = (1.0 - (1.0 - SIGMA_MIN) * scaled) * gaussian + scaled * spectra
    context = spectra * (1.0 - flags[:, None, :])
    onehot = (phone_ids[:, None, :] == jnp.arange(VOCAB)[None, :, None]).astype(jnp.float32)
    feature_rows = low(jnp.concatenate([noisy, context, onehot], 1))
    initial_state = jnp.einsum('nzv,zr->nvr', feature_rows, input_weight, precision=FULL_PRECISION)
    initial_state = low_back(initial_state * valid[:, :, None].astype(jnp.float32))
    embedded = initial_state + jax.nn.gelu(low_back(conv_mix(low(initial_state), kernel_w)))
    alibi = alibi_bias(frame_count)
    encoded = layer(embedded, (joint_w[0], output_w[0], expand_w[0], reduce_w[0]), gains_w[0], gains_w[1], valid, alibi)
    bridged = low_back(project(low(jnp.concatenate([encoded, embedded], -1)), bridge_w))
    decoded = layer(bridged, (joint_w[1], output_w[1], expand_w[1], reduce_w[1]), gains_w[2], gains_w[3], valid, alibi)
    predict = low_back(project(low(layer_norm(decoded, gains_w[4])), readout_w))
    target = jnp.swapaxes(spectra - (1.0 - SIGMA_MIN) * gaussian, 1, 2)
    weight = (flags * valid.astype(jnp.float32))[:, :, None]
    return jnp.sum(weight * (predict - target) ** 2)

def adamw(master, moment, square, grad, rate, decay):
    moment = BETA_ONE * moment + (1.0 - BETA_ONE) * grad
    square = BETA_TWO * square + (1.0 - BETA_TWO) * grad * grad
    fixed_moment = moment / (1.0 - BETA_ONE ** STEP)
    fixed_square = square / (1.0 - BETA_TWO ** STEP)
    return (moment, square, master - rate * (fixed_moment / (jnp.sqrt(fixed_square) + ADAM_EPS) + decay * master))

def weight_rates():
    fan_ins = (MEL, KS * (D // GROUPS), D, D // 8, D, FF, 2 * D, D)
    return [RATE_SCALE * fan_in ** (-0.5) for fan_in in fan_ins] + [GAIN_RATE]

def reference(spectra, gaussian, flow_times, lengths, span_flags, phone_ids, input_master, input_moment, input_square, kernel_master, kernel_moment, kernel_square, joint_master, joint_moment, joint_square, output_master, output_moment, output_square, expand_master, expand_moment, expand_square, reduce_master, reduce_moment, reduce_square, bridge_master, bridge_moment, bridge_square, readout_master, readout_moment, readout_square, gains_master, gains_moment, gains_square):
    masters = (input_master, kernel_master, joint_master, output_master, expand_master, reduce_master, bridge_master, readout_master, gains_master)
    moments = (input_moment, kernel_moment, joint_moment, output_moment, expand_moment, reduce_moment, bridge_moment, readout_moment, gains_moment)
    squares = (input_square, kernel_square, joint_square, output_square, expand_square, reduce_square, bridge_square, readout_square, gains_square)
    group_size = 8 * SEQ_DEV
    data = (spectra.astype(jnp.float32), gaussian.astype(jnp.float32), flow_times, lengths, span_flags, phone_ids)
    grouped = tuple((item.reshape((item.shape[0] // group_size, group_size) + item.shape[1:]) for item in data))

    def total_loss(params):
        copies = tuple((low(item) for item in params))

        def one_group(carry, piece):
            return (carry + jax.checkpoint(group_loss)(copies, *piece), None)
        summed, _ = lax.scan(one_group, jnp.zeros((), jnp.float32), grouped)
        return summed
    loss_sum, pull = jax.vjp(total_loss, masters)
    grads = pull(jnp.ones((), jnp.float32))[0]
    valid = jnp.arange(LEN)[None, :] < lengths[:, None]
    frame_total = jnp.sum(span_flags.astype(jnp.float32) * valid.astype(jnp.float32))
    squared = sum((jnp.sum(item * item) for item in grads))
    grad_norm = jnp.sqrt(squared) / frame_total
    factor = jnp.minimum(1.0, CLIP_LIMIT / grad_norm) / frame_total
    decays = [DECAY_RATE] * 8 + [0.0]
    results = []
    for master, moment, square, grad, rate, decay in zip(masters, moments, squares, grads, weight_rates(), decays):
        results.extend(adamw(master, moment, square, factor * grad, rate, decay))
    return (loss_sum, frame_total, grad_norm, *results)
```

```python
import jax
import jax.numpy as jnp
from jax import lax
from jax.experimental import pallas as pl
from jax.experimental.pallas import tpu as pltpu
from jax.sharding import PartitionSpec as P

D = 1024
HEADS = 16
FF = 4096
MEL = 80
VOCAB = 96
KS = 31
GROUPS = 16
STEP = 10


SIGMA_MIN = 1e-05
NORM_EPS = 1e-05
MASKED = -1e30
BETA_ONE = 0.9
BETA_TWO = 0.95
ADAM_EPS = 1e-08
DECAY_RATE = 0.01
CLIP_LIMIT = 0.2
RATE_SCALE = 0.5
GAIN_RATE = 0.25


def layer_norm(values, gain_row):
    center = values - jnp.mean(values, -1, keepdims=True)
    spread = jnp.mean(center * center, -1, keepdims=True)
    return center * lax.rsqrt(spread + NORM_EPS) * gain_row


def alibi_bias(frames):
    slopes = 2.0 ** (-8.0 * (jnp.arange(HEADS, dtype=jnp.float32) + 1.0) / HEADS)
    places = jnp.arange(frames, dtype=jnp.float32)
    return -slopes[:, None, None] * jnp.abs(places[:, None] - places[None, :])


def conv_mix(hidden, kernel):
    tap_count = kernel.shape[0]
    margin = tap_count // 2
    seq_count, frame_count, model_width = hidden.shape
    per_group = model_width // GROUPS
    padded = jnp.pad(hidden, ((0, 0), (margin, margin), (0, 0)))
    stacked = jnp.stack([padded[:, tap : tap + frame_count] for tap in range(tap_count)], 1)
    stacked = stacked.reshape(seq_count, tap_count, frame_count, GROUPS, per_group)
    weights = kernel.reshape(tap_count, GROUPS, per_group, per_group)
    mixed = jnp.einsum("bklgc,kgoc->blgo", stacked, weights)
    return mixed.reshape(seq_count, frame_count, model_width)


def score_block(query, keyed, valid, alibi):
    scale = query.shape[-1] ** (-0.5)
    scores = (
        jnp.einsum("sqhd,skhd->shqk", query, keyed, preferred_element_type=jnp.float32) * scale
        + alibi[None]
    )
    return jnp.where(valid[:, None, None, :], scores, MASKED)


def layer_forward(stream, mats, gain_one, gain_two, valid, alibi):
    joint_w, output_w, expand_w, reduce_w = mats
    seq_count, frame_count, model_width = stream.shape
    row_count = seq_count * frame_count
    normed = layer_norm(stream, gain_one).astype(jnp.bfloat16).reshape(row_count, model_width)
    joint = jnp.dot(normed, joint_w, preferred_element_type=jnp.float32).astype(jnp.bfloat16)
    joint = joint.reshape(seq_count, frame_count, 3, HEADS, model_width // HEADS)
    scores = score_block(joint[:, :, 0], joint[:, :, 1], valid, alibi)
    highest = jnp.max(scores, -1, keepdims=True)
    raised = jnp.exp(scores - highest)
    totals = jnp.sum(raised, -1, keepdims=True)
    probs = raised / totals
    log_total = highest + jnp.log(totals)
    context = jnp.einsum(
        "shqk,skhd->sqhd",
        probs.astype(jnp.bfloat16),
        joint[:, :, 2],
        preferred_element_type=jnp.float32,
    )
    context = context.astype(jnp.bfloat16).reshape(row_count, model_width)
    middle = stream + jnp.dot(context, output_w, preferred_element_type=jnp.float32).reshape(
        stream.shape
    )
    normed_two = layer_norm(middle, gain_two).astype(jnp.bfloat16).reshape(row_count, model_width)
    upper = jnp.dot(normed_two, expand_w, preferred_element_type=jnp.float32)
    hidden = jax.nn.gelu(upper).astype(jnp.bfloat16)
    result = middle + jnp.dot(hidden, reduce_w, preferred_element_type=jnp.float32).reshape(
        stream.shape
    )
    return (result, (stream, normed, joint, log_total, context, middle, normed_two, upper, hidden))


def layer_backward(incoming, kept, mats, gain_one, gain_two, valid, alibi):
    stream, normed, joint, log_total, context, middle, normed_two, upper, hidden = kept
    joint_w, output_w, expand_w, reduce_w = mats
    seq_count, frame_count, model_width = stream.shape
    row_count = seq_count * frame_count
    incoming_low = incoming.reshape(row_count, model_width).astype(jnp.bfloat16)
    d_reduce = jnp.dot(hidden.T, incoming_low, preferred_element_type=jnp.float32)
    d_hidden = jnp.dot(incoming_low, reduce_w.T, preferred_element_type=jnp.float32)
    gelu_pull = jax.vjp(jax.nn.gelu, upper)[1]
    d_upper = gelu_pull(d_hidden)[0].astype(jnp.bfloat16)
    d_expand = jnp.dot(normed_two.T, d_upper, preferred_element_type=jnp.float32)
    d_normed = jnp.dot(d_upper, expand_w.T, preferred_element_type=jnp.float32).reshape(
        stream.shape
    )
    norm_pull = jax.vjp(layer_norm, middle, gain_two)[1]
    d_middle, d_gain_two = norm_pull(d_normed)
    d_middle = d_middle + incoming
    d_middle_low = d_middle.reshape(row_count, model_width).astype(jnp.bfloat16)
    d_output = jnp.dot(context.T, d_middle_low, preferred_element_type=jnp.float32)
    d_context = jnp.dot(d_middle_low, output_w.T, preferred_element_type=jnp.float32).astype(
        jnp.bfloat16
    )
    d_context = d_context.reshape(seq_count, frame_count, HEADS, model_width // HEADS)
    query, keyed, valued = (joint[:, :, 0], joint[:, :, 1], joint[:, :, 2])
    probs = jnp.exp(score_block(query, keyed, valid, alibi) - log_total)
    d_probs = jnp.einsum("sqhd,skhd->shqk", d_context, valued, preferred_element_type=jnp.float32)
    d_valued = jnp.einsum(
        "shqk,sqhd->skhd", probs.astype(jnp.bfloat16), d_context, preferred_element_type=jnp.float32
    )
    inner = jnp.sum(probs * d_probs, -1, keepdims=True)
    d_scores = (probs * (d_probs - inner)).astype(jnp.bfloat16)
    scale = query.shape[-1] ** (-0.5)
    d_query = (
        jnp.einsum("shqk,skhd->sqhd", d_scores, keyed, preferred_element_type=jnp.float32) * scale
    )
    d_keyed = (
        jnp.einsum("shqk,sqhd->skhd", d_scores, query, preferred_element_type=jnp.float32) * scale
    )
    d_joint = (
        jnp.stack([d_query, d_keyed, d_valued], 2)
        .astype(jnp.bfloat16)
        .reshape(row_count, 3 * model_width)
    )
    d_joint_w = jnp.dot(normed.T, d_joint, preferred_element_type=jnp.float32)
    d_normed = jnp.dot(d_joint, joint_w.T, preferred_element_type=jnp.float32).reshape(stream.shape)
    norm_pull = jax.vjp(layer_norm, stream, gain_one)[1]
    d_stream, d_gain_one = norm_pull(d_normed)
    return (d_stream + d_middle, (d_joint_w, d_output, d_expand, d_reduce), d_gain_one, d_gain_two)


def adamw(master, moment, square, grad, rate, decay):
    moment = BETA_ONE * moment + (1.0 - BETA_ONE) * grad
    square = BETA_TWO * square + (1.0 - BETA_TWO) * grad * grad
    fixed_moment = moment / (1.0 - BETA_ONE**STEP)
    fixed_square = square / (1.0 - BETA_TWO**STEP)
    return (
        moment,
        square,
        master - rate * (fixed_moment / (jnp.sqrt(fixed_square) + ADAM_EPS) + decay * master),
    )


def weight_rates():
    fan_ins = (MEL, KS * (D // GROUPS), D, D // 8, D, FF, 2 * D, D)
    return [RATE_SCALE * fan_in ** (-0.5) for fan_in in fan_ins] + [GAIN_RATE]


def shards(
    spectra,
    gaussian,
    flow_times,
    lengths,
    span_flags,
    phone_ids,
    input_master,
    input_moment,
    input_square,
    kernel_master,
    kernel_moment,
    kernel_square,
    joint_master,
    joint_moment,
    joint_square,
    output_master,
    output_moment,
    output_square,
    expand_master,
    expand_moment,
    expand_square,
    reduce_master,
    reduce_moment,
    reduce_square,
    bridge_master,
    bridge_moment,
    bridge_square,
    readout_master,
    readout_moment,
    readout_square,
    gains_master,
    gains_moment,
    gains_square,
):
    low_type = jnp.bfloat16
    wide_dtype = jnp.float32
    input_wide, kernel_full, bridge_full, readout_full, gains_full = (
        lax.all_gather(input_master.astype(low_type), ("dp", "fsdp"), axis=1, tiled=True),
        lax.all_gather(kernel_master.astype(low_type), ("dp", "fsdp"), axis=1, tiled=True),
        lax.all_gather(bridge_master.astype(low_type), ("dp", "fsdp"), axis=0, tiled=True),
        lax.all_gather(readout_master.astype(low_type), ("dp", "fsdp"), axis=0, tiled=True),
        lax.all_gather(gains_master.astype(low_type), ("dp", "fsdp"), axis=1, tiled=True),
    )
    gains_full = gains_full.astype(wide_dtype)

    def fetch(layer_index):
        return (
            lax.all_gather(
                joint_master[layer_index].astype(low_type), ("dp", "fsdp"), axis=0, tiled=True
            ),
            lax.all_gather(
                output_master[layer_index].astype(low_type), ("dp", "fsdp"), axis=0, tiled=True
            ),
            lax.all_gather(
                expand_master[layer_index].astype(low_type), ("dp", "fsdp"), axis=0, tiled=True
            ),
            lax.all_gather(
                reduce_master[layer_index].astype(low_type), ("dp", "fsdp"), axis=0, tiled=True
            ),
        )

    def share(grads):
        return (
            lax.psum_scatter(grads[0], ("dp", "fsdp"), scatter_dimension=0, tiled=True),
            lax.psum_scatter(grads[1], ("dp", "fsdp"), scatter_dimension=0, tiled=True),
            lax.psum_scatter(grads[2], ("dp", "fsdp"), scatter_dimension=0, tiled=True),
            lax.psum_scatter(grads[3], ("dp", "fsdp"), scatter_dimension=0, tiled=True),
        )

    seq_count, mel_count, frame_count = spectra.shape
    row_count = seq_count * frame_count
    valid = jnp.arange(frame_count)[None, :] < lengths[:, None]
    valid_float = valid.astype(wide_dtype)
    flags = span_flags.astype(wide_dtype)
    clean = spectra.astype(wide_dtype)
    noise_full = gaussian.astype(wide_dtype)
    scaled = flow_times[:, None, None]
    noisy = (1.0 - (1.0 - SIGMA_MIN) * scaled) * noise_full + scaled * clean
    context = clean * (1.0 - flags[:, None, :])
    onehot = (phone_ids[:, None, :] == jnp.arange(VOCAB)[None, :, None]).astype(low_type)
    feature_rows = jnp.concatenate([noisy.astype(low_type), context.astype(low_type), onehot], 1)
    initial_state = (
        jnp.einsum("nzv,zr->nvr", feature_rows, input_wide, preferred_element_type=wide_dtype)
        * valid_float[:, :, None]
    )
    conv_out, conv_pull = jax.vjp(
        conv_mix, initial_state.astype(low_type).astype(wide_dtype), kernel_full.astype(wide_dtype)
    )
    embedded = initial_state + jax.nn.gelu(conv_out)
    alibi = alibi_bias(frame_count)
    mats_zero = fetch(0)
    encoded, kept_zero = layer_forward(
        embedded, mats_zero, gains_full[0], gains_full[1], valid, alibi
    )
    model_width = encoded.shape[-1]
    joined = (
        jnp.concatenate([encoded, embedded], -1)
        .astype(low_type)
        .reshape(row_count, 2 * model_width)
    )
    bridged = jnp.dot(joined, bridge_full, preferred_element_type=wide_dtype).reshape(encoded.shape)
    mats_one = fetch(1)
    decoded, kept_one = layer_forward(bridged, mats_one, gains_full[2], gains_full[3], valid, alibi)
    final_low = layer_norm(decoded, gains_full[4]).astype(low_type).reshape(row_count, model_width)
    predict = jnp.dot(final_low, readout_full, preferred_element_type=wide_dtype)
    target = jnp.swapaxes(clean - (1.0 - SIGMA_MIN) * noise_full, 1, 2).reshape(
        row_count, mel_count
    )
    weight = (flags * valid_float).reshape(row_count, 1)
    missed = predict - target
    loss_local = jnp.sum(weight * missed * missed)
    count_local = jnp.sum(weight)
    loss_sum, frame_total = lax.psum((loss_local, count_local), ("dp", "fsdp"))
    d_predict = (2.0 * weight * missed).astype(low_type)
    d_readout = jnp.dot(final_low.T, d_predict, preferred_element_type=wide_dtype)
    d_final = jnp.dot(d_predict, readout_full.T, preferred_element_type=wide_dtype).reshape(
        decoded.shape
    )
    final_pull = jax.vjp(layer_norm, decoded, gains_full[4])[1]
    d_decoded, d_gain_last = final_pull(d_final)
    mats_back = mats_one
    d_bridged, grads_one, d_gain_two, d_gain_three = layer_backward(
        d_decoded, kept_one, mats_back, gains_full[2], gains_full[3], valid, alibi
    )
    shard_one = share(grads_one)
    d_bridged_low = d_bridged.reshape(row_count, model_width).astype(low_type)
    d_bridge = jnp.dot(joined.T, d_bridged_low, preferred_element_type=wide_dtype)
    d_joined = jnp.dot(d_bridged_low, bridge_full.T, preferred_element_type=wide_dtype).reshape(
        seq_count, frame_count, 2 * model_width
    )
    mats_back = mats_zero
    d_embedded, grads_zero, d_gain_zero, d_gain_one = layer_backward(
        d_joined[:, :, :model_width],
        kept_zero,
        mats_back,
        gains_full[0],
        gains_full[1],
        valid,
        alibi,
    )
    shard_zero = share(grads_zero)
    d_embedded = d_embedded + d_joined[:, :, model_width:]
    gelu_pull = jax.vjp(jax.nn.gelu, conv_out)[1]
    d_conv = gelu_pull(d_embedded)[0].astype(low_type).astype(wide_dtype)
    d_conv_in, d_kernel = conv_pull(d_conv)
    initial_gradient = ((d_embedded + d_conv_in) * valid_float[:, :, None]).astype(low_type)
    input_gradient = jnp.einsum(
        "fpk,fkq->pq", feature_rows, initial_gradient, preferred_element_type=wide_dtype
    )
    d_gains = jnp.stack([d_gain_zero, d_gain_one, d_gain_two, d_gain_three, d_gain_last])
    edge_input, edge_kernel, edge_bridge, edge_readout, edge_gains = (
        lax.psum_scatter(input_gradient, ("dp", "fsdp"), scatter_dimension=1, tiled=True),
        lax.psum_scatter(d_kernel, ("dp", "fsdp"), scatter_dimension=1, tiled=True),
        lax.psum_scatter(d_bridge, ("dp", "fsdp"), scatter_dimension=0, tiled=True),
        lax.psum_scatter(d_readout, ("dp", "fsdp"), scatter_dimension=0, tiled=True),
        lax.psum_scatter(d_gains, ("dp", "fsdp"), scatter_dimension=1, tiled=True),
    )
    layer_shards = [
        jnp.stack([zero_part, one_part]) for zero_part, one_part in zip(shard_zero, shard_one)
    ]
    grads = [edge_input, edge_kernel] + layer_shards + [edge_bridge, edge_readout, edge_gains]
    squares_local = sum((jnp.sum(item * item) for item in grads))
    squared = lax.psum(squares_local, ("dp", "fsdp"))
    grad_norm = jnp.sqrt(squared) / frame_total
    factor = jnp.minimum(1.0, CLIP_LIMIT / grad_norm) / frame_total
    masters = (
        input_master,
        kernel_master,
        joint_master,
        output_master,
        expand_master,
        reduce_master,
        bridge_master,
        readout_master,
        gains_master,
    )
    moments = (
        input_moment,
        kernel_moment,
        joint_moment,
        output_moment,
        expand_moment,
        reduce_moment,
        bridge_moment,
        readout_moment,
        gains_moment,
    )
    squares = (
        input_square,
        kernel_square,
        joint_square,
        output_square,
        expand_square,
        reduce_square,
        bridge_square,
        readout_square,
        gains_square,
    )
    decays = [DECAY_RATE] * 8 + [0.0]
    results = []
    for master, moment, square, grad, rate, decay in zip(
        masters, moments, squares, grads, weight_rates(), decays
    ):
        results.extend(adamw(master, moment, square, factor * grad, rate, decay))
    return (loss_sum, frame_total, grad_norm, *results)


LOW = jnp.bfloat16
WIDE = jnp.float32
BOTH = ("dp", "fsdp")
VMEM_GRANT = 24 * 2**20
GRANT = pltpu.CompilerParams(vmem_limit_bytes=VMEM_GRANT)
TAPS_OUT = 8
GELU_SCALE = 0.7978845608028654
SHORT = pl.CostEstimate(flops=1000, bytes_accessed=1000, transcendentals=0)
LANES = 512
Z_LINES = [[half + 2 * i for i in range(4)] for half in range(2)]


def swap_x(item):
    return lax.ppermute(item, "dp", [(i, i ^ 1) for i in range(4)])


def swap_y(item):
    return lax.ppermute(item, "dp", [(i, i ^ 2) for i in range(4)])


def swap_core(item):
    return lax.ppermute(item, "fsdp", [(i, i ^ 1) for i in range(8)])


def shift_z(item, hops):
    return lax.ppermute(item, "fsdp", [(i, (i + 2 * hops) % 8) for i in range(8)])


def pick(stacked, index):
    return lax.dynamic_index_in_dim(stacked, index, 0, keepdims=False)


def in_order(core, mine, other):
    first = core == 0
    return jnp.where(first, mine, other), jnp.where(first, other, mine)


def side_by_side(core, mine):
    return jnp.concatenate(in_order(core, mine, swap_core(mine)), -1)


def z_line(own, z):
    parts = [own] + [shift_z(own, hops) for hops in (1, 2, 3)]
    line = jnp.zeros((4,) + own.shape, own.dtype)
    for hops, part in enumerate(parts):
        line = lax.dynamic_update_index_in_dim(line, part, (z - hops) % 4, 0)
    return line


def laid_out(weights_ref, places_ref, whole_ref, part):
    for slot in range(16):
        start = pl.multiple_of(places_ref[slot] * part, 16)
        whole_ref[pl.ds(start, part), :] = weights_ref[slot]


def piece_dot(rows, weights, base, part, count, low=False, with_gelu=False):
    gathered, places = weights
    row_count, depth = rows.shape
    out_type = LOW if low else WIDE
    width = count * LANES

    def body(places_ref, rows_ref, weights_ref, *refs):
        whole_ref = refs[-1]
        laid_out(weights_ref, places_ref, whole_ref, part)
        total = jnp.dot(rows_ref[...], whole_ref[...], preferred_element_type=WIDE)
        refs[0][...] = total.astype(out_type)
        if with_gelu:
            refs[1][...] = jax.nn.gelu(total).astype(LOW)

    out_spec = pl.BlockSpec((row_count, LANES), lambda j, s: (0, j))
    shape = jax.ShapeDtypeStruct((row_count, width), out_type)
    low_shape = jax.ShapeDtypeStruct((row_count, width), LOW)
    return pl.pallas_call(
        body,
        grid_spec=pltpu.PrefetchScalarGridSpec(
            num_scalar_prefetch=1,
            grid=(count,),
            in_specs=[
                pl.BlockSpec((row_count, depth), lambda j, s: (0, 0)),
                pl.BlockSpec((16, part, LANES), lambda j, s: (0, j + base // part, 0)),
            ],
            out_specs=[out_spec, out_spec] if with_gelu else out_spec,
            scratch_shapes=[pltpu.VMEM((depth, LANES), LOW)],
        ),
        out_shape=[shape, low_shape] if with_gelu else shape,
        compiler_params=GRANT,
        cost_estimate=SHORT,
    )(places, rows, gathered)


def gelu_slope(values):
    cubic = 0.044715 * values * values
    bent = jnp.tanh(GELU_SCALE * values * (1.0 + cubic))
    return 0.5 * (1.0 + bent) + 0.5 * values * (1.0 - bent * bent) * GELU_SCALE * (
        1.0 + 3.0 * cubic
    )


def piece_dot_back(grads, weights, base, part, upper=None, split=False):
    gathered, places = weights
    row_count, width = grads.shape
    depth, steps = 16 * part, grads.shape[1] // LANES
    half = depth // 2

    def body(places_ref, grads_ref, weights_ref, *refs):
        total_ref, whole_ref = refs[-2:]
        laid_out(weights_ref, places_ref, whole_ref, part)
        product = lax.dot_general(
            grads_ref[...],
            whole_ref[...],
            (((1,), (1,)), ((), ())),
            preferred_element_type=WIDE,
        )

        @pl.when(pl.program_id(0) == 0)
        def _():
            total_ref[...] = product

        @pl.when(pl.program_id(0) > 0)
        def _():
            total_ref[...] += product

        @pl.when(pl.program_id(0) == steps - 1)
        def _():
            if upper is not None:
                refs[1][...] = (total_ref[...] * gelu_slope(refs[0][...])).astype(LOW)
            elif split:
                core = places_ref[16]
                refs[0][...] = total_ref[:, pl.ds(pl.multiple_of(core * half, 128), half)]
                refs[1][...] = total_ref[:, pl.ds(pl.multiple_of((1 - core) * half, 128), half)]
            else:
                refs[0][...] = total_ref[...]

    def fixed(shape):
        return pl.BlockSpec(shape, lambda j, s: (0, 0))

    if split:
        shapes = [jax.ShapeDtypeStruct((row_count, half), WIDE)] * 2
    else:
        shapes = [jax.ShapeDtypeStruct((row_count, depth), WIDE if upper is None else LOW)]
    extra = [] if upper is None else [upper]
    out = pl.pallas_call(
        body,
        grid_spec=pltpu.PrefetchScalarGridSpec(
            num_scalar_prefetch=1,
            grid=(steps,),
            in_specs=[
                pl.BlockSpec((row_count, LANES), lambda j, s: (0, j)),
                pl.BlockSpec((16, part, LANES), lambda j, s: (0, j + base // part, 0)),
            ]
            + [fixed(item.shape) for item in extra],
            out_specs=[fixed(item.shape) for item in shapes],
            scratch_shapes=[
                pltpu.VMEM((row_count, depth), WIDE),
                pltpu.VMEM((depth, LANES), LOW),
            ],
        ),
        out_shape=shapes,
        compiler_params=GRANT,
        cost_estimate=SHORT,
    )(places, grads, gathered, *extra)
    return out if split else out[0]


def whole_blocks(items):
    return [pl.BlockSpec(item.shape, lambda s, n=len(item.shape): (0,) * n) for item in items]


def one_step(body, scalars, operands, shapes, scratch=()):
    return pl.pallas_call(
        body,
        grid_spec=pltpu.PrefetchScalarGridSpec(
            num_scalar_prefetch=1,
            grid=(),
            in_specs=[pl.BlockSpec(memory_space=pltpu.VMEM)] * len(operands),
            out_specs=[pl.BlockSpec(memory_space=pltpu.VMEM)] * len(shapes),
            scratch_shapes=list(scratch),
        ),
        out_shape=shapes,
        compiler_params=GRANT,
        cost_estimate=SHORT,
    )(scalars, *operands)


def norm_forward(base, mine, other, gain, scalars, halves):
    addends = [] if mine is None else [mine, other]
    bases = [] if base is None else [base]
    rows = (mine if base is None else base).shape[0]
    width = gain.shape[1]
    half = width // 2

    def body(scalars_ref, *refs):
        gain_ref, stream_ref, normed_ref = refs[-3:]
        base_ref = None if base is None else refs[0]
        if mine is None:
            stream_ref[...] = base_ref[...]
        elif halves:
            mine_ref, other_ref = refs[len(bases) : len(bases) + 2]
            core = scalars_ref[16]
            for ref, side in ((mine_ref, core), (other_ref, 1 - core)):
                lanes = pl.ds(pl.multiple_of(side * half, 128), half)
                part = ref[...]
                stream_ref[:, lanes] = part if base is None else base_ref[:, lanes] + part
        else:
            mine_ref, other_ref = refs[len(bases) : len(bases) + 2]
            stream_ref[...] = base_ref[...] + (mine_ref[...] + other_ref[...])
        normed_ref[...] = (norm_parts(stream_ref[...]) * gain_ref[...]).astype(LOW)

    shapes = [jax.ShapeDtypeStruct((rows, width), WIDE), jax.ShapeDtypeStruct((rows, width), LOW)]
    return one_step(body, scalars, (*bases, *addends, gain), shapes)


def norm_backward(mine, other, values, gain, incoming, scalars):
    rows, width = values.shape
    half = width // 2

    def body(scalars_ref, mine_ref, other_ref, values_ref, gain_ref, incoming_ref, *refs):
        total_ref, low_ref, low_half_ref, row_ref, terms_ref = refs
        core = scalars_ref[16]
        back, terms = norm_back(values_ref[...], gain_ref[...], mine_ref[...] + other_ref[...])
        total = incoming_ref[...] + back
        total_ref[...] = total
        low_ref[...] = total.astype(LOW)
        low_half_ref[...] = low_ref[:, pl.ds(pl.multiple_of(core * half, 128), half)]
        terms_ref[...] = terms
        own = terms_ref[pl.ds(pl.multiple_of(core * (rows // 2), 8), rows // 2), :]
        row_ref[...] = jnp.sum(own, 0, keepdims=True)

    shapes = [
        jax.ShapeDtypeStruct((rows, width), WIDE),
        jax.ShapeDtypeStruct((rows, width), LOW),
        jax.ShapeDtypeStruct((rows, half), LOW),
        jax.ShapeDtypeStruct((1, width), WIDE),
    ]
    scratch = [pltpu.VMEM((rows, width), WIDE)]
    return one_step(
        body, scalars, (mine, other, values, gain, incoming), shapes, scratch
    )


def head_probs(joint_ref, head, size, slope, valid, distance):
    third = joint_ref.shape[1] // 3
    query = joint_ref[:, head * size : (head + 1) * size]
    keyed = joint_ref[:, third + head * size : third + (head + 1) * size]
    scores = lax.dot_general(
        query, keyed, (((1,), (1,)), ((), ())), preferred_element_type=WIDE
    )
    scores = jnp.where(valid, scores * size ** (-0.5) - slope * distance, MASKED)
    raised = jnp.exp(scores - jnp.max(scores, -1, keepdims=True))
    return query, keyed, raised / jnp.sum(raised, -1, keepdims=True)


def frame_distance(frames):
    ahead = lax.broadcasted_iota(jnp.int32, (frames, frames), 0)
    return jnp.abs(ahead - lax.broadcasted_iota(jnp.int32, (frames, frames), 1)).astype(WIDE)


def attend(joint, slopes, valid, size):
    rows, triple = joint.shape
    frames, third = rows // 2, triple // 3

    def body(slopes_ref, joint_ref, valid_ref, out_ref):
        distance = frame_distance(frames)
        mask = jnp.broadcast_to(valid_ref[0] > 0.5, (frames, frames))
        for head in range(third // size):
            _, _, probs = head_probs(joint_ref, head, size, slopes_ref[head], mask, distance)
            value = joint_ref[:, 2 * third + head * size : 2 * third + (head + 1) * size]
            mixed = jnp.dot(probs.astype(LOW), value, preferred_element_type=WIDE)
            out_ref[:, head * size : (head + 1) * size] = mixed.astype(LOW)

    return pl.pallas_call(
        body,
        grid_spec=pltpu.PrefetchScalarGridSpec(
            num_scalar_prefetch=1,
            grid=(2,),
            in_specs=[
                pl.BlockSpec((frames, triple), lambda u, s: (u, 0)),
                pl.BlockSpec((1, 1, frames), lambda u, s: (u, 0, 0)),
            ],
            out_specs=pl.BlockSpec((frames, third), lambda u, s: (u, 0)),
        ),
        out_shape=jax.ShapeDtypeStruct((rows, third), LOW),
        compiler_params=GRANT,
        cost_estimate=SHORT,
    )(slopes, joint, valid)


def attend_back(joint, mine, other, slopes, valid, size):
    rows, triple = joint.shape
    frames, third = rows // 2, triple // 3

    def body(slopes_ref, joint_ref, mine_ref, other_ref, valid_ref, out_ref):
        distance = frame_distance(frames)
        mask = jnp.broadcast_to(valid_ref[0] > 0.5, (frames, frames))
        scale = size ** (-0.5)
        for head in range(third // size):
            cut = slice(head * size, (head + 1) * size)
            query, keyed, probs = head_probs(
                joint_ref, head, size, slopes_ref[head], mask, distance
            )
            value = joint_ref[:, 2 * third + head * size : 2 * third + (head + 1) * size]
            grad = (mine_ref[:, cut] + other_ref[:, cut]).astype(LOW)
            d_probs = lax.dot_general(
                grad, value, (((1,), (1,)), ((), ())), preferred_element_type=WIDE
            )
            inner = jnp.sum(probs * d_probs, -1, keepdims=True)
            d_scores = (probs * (d_probs - inner)).astype(LOW)
            d_query = jnp.dot(d_scores, keyed, preferred_element_type=WIDE) * scale
            d_keyed = jnp.dot(d_scores.T, query, preferred_element_type=WIDE) * scale
            d_value = jnp.dot(probs.astype(LOW).T, grad, preferred_element_type=WIDE)
            for spot, item in enumerate((d_query, d_keyed, d_value)):
                start = spot * third + head * size
                out_ref[:, start : start + size] = item.astype(LOW)

    def utterance(width):
        return pl.BlockSpec((frames, width), lambda u, s: (u, 0))

    return pl.pallas_call(
        body,
        grid_spec=pltpu.PrefetchScalarGridSpec(
            num_scalar_prefetch=1,
            grid=(2,),
            in_specs=[
                utterance(triple),
                utterance(third),
                utterance(third),
                pl.BlockSpec((1, 1, frames), lambda u, s: (u, 0, 0)),
            ],
            out_specs=utterance(triple),
        ),
        out_shape=jax.ShapeDtypeStruct((rows, triple), LOW),
        compiler_params=GRANT,
        cost_estimate=SHORT,
    )(slopes, joint, mine, other, valid)


def packed_tokens(left, right, numbers):
    rows, depth = left.shape
    quarter, width = depth // 4, right.shape[1]

    def body(numbers_ref, left_ref, right_ref, out_ref):
        for spot in range(2):
            start = pl.multiple_of(numbers_ref[spot] * quarter, 128)
            out_ref[:, spot * quarter : (spot + 1) * quarter] = left_ref[:, pl.ds(start, quarter)]
        out_ref[:, 2 * quarter :] = right_ref[...]

    shapes = [jax.ShapeDtypeStruct((rows, 2 * quarter + width), LOW)]
    return one_step(body, numbers, (left, right), shapes)[0]


def outer_sum(left, right, got, number, second, out_type):
    rows, depth = left.shape
    quarter, width = depth // 4, right.shape[1]

    def body(number_ref, left_ref, right_ref, far_left_ref, far_right_ref, out_ref):
        dims = (((0,), (0,)), ((), ()))
        total = lax.dot_general(
            left_ref[...], right_ref[...], dims, preferred_element_type=WIDE
        )
        total = total + lax.dot_general(
            far_left_ref[...], far_right_ref[...], dims, preferred_element_type=WIDE
        )
        out_ref[...] = total.astype(out_type)

    return pl.pallas_call(
        body,
        grid_spec=pltpu.PrefetchScalarGridSpec(
            num_scalar_prefetch=1,
            grid=(width // LANES,),
            in_specs=[
                pl.BlockSpec((rows, quarter), lambda j, s: (0, s[0])),
                pl.BlockSpec((rows, LANES), lambda j, s: (0, j)),
                pl.BlockSpec((rows, quarter), lambda j, s: (0, second)),
                pl.BlockSpec((rows, LANES), lambda j, s: (0, j + 2 * quarter // LANES)),
            ],
            out_specs=pl.BlockSpec((quarter, LANES), lambda j, s: (0, j)),
        ),
        out_shape=jax.ShapeDtypeStruct((quarter, width), out_type),
        compiler_params=GRANT,
        cost_estimate=SHORT,
    )(number, left, right, got, got)


def banded_kernel(body, operands, blocks, out_block, shape, sums):
    def summed(*refs):
        if not sums:
            refs[-1][...] = body(*refs[:-1])
            return

        @pl.when(pl.program_id(0) == 0)
        def _():
            refs[-1][...] = jnp.zeros_like(refs[-1])

        refs[-1][...] += body(*refs[:-1])

    return pl.pallas_call(
        summed,
        grid=(5,),
        in_specs=blocks,
        out_specs=out_block,
        out_shape=jax.ShapeDtypeStruct(shape, WIDE),
        compiler_params=GRANT,
        cost_estimate=SHORT,
    )(*operands)


def banded_dot(windows, banded):
    rows, (_, depth, width) = windows.shape[0], banded.shape
    return banded_kernel(
        lambda left, right: jnp.dot(left[...], right[0], preferred_element_type=WIDE),
        (windows, banded),
        [
            pl.BlockSpec((rows, depth), lambda i: (0, i)),
            pl.BlockSpec((1, depth, width), lambda i: (i, 0, 0)),
        ],
        pl.BlockSpec((rows, width), lambda i: (0, 0)),
        (rows, width),
        True,
    )


def banded_back(grads, banded):
    rows, (_, depth, width) = grads.shape[0], banded.shape
    dims = (((1,), (1,)), ((), ()))
    return banded_kernel(
        lambda left, right: lax.dot_general(
            left[...], right[0], dims, preferred_element_type=WIDE
        ),
        (grads, banded),
        [
            pl.BlockSpec((rows, width), lambda i: (0, i)),
            pl.BlockSpec((1, depth, width), lambda i: (i, 0, 0)),
        ],
        pl.BlockSpec((rows, depth), lambda i: (0, 0)),
        (rows, depth),
        True,
    )


def banded_outer(windows, grads):
    rows, width = grads.shape
    depth = windows.shape[1] // 5
    dims = (((0,), (0,)), ((), ()))
    return banded_kernel(
        lambda left, right: lax.dot_general(
            left[...], right[...], dims, preferred_element_type=WIDE
        ),
        (windows, grads),
        [
            pl.BlockSpec((rows, depth), lambda i: (0, i)),
            pl.BlockSpec((rows, width), lambda i: (0, 0)),
        ],
        pl.BlockSpec((depth, width), lambda i: (i, 0)),
        (windows.shape[1], width),
        False,
    )


def norm_parts(values):
    center = values - jnp.mean(values, -1, keepdims=True)
    spread = jnp.mean(center * center, -1, keepdims=True)
    return center * lax.rsqrt(spread + NORM_EPS)


def norm_back(values, gain_row, grads):
    center = values - jnp.mean(values, -1, keepdims=True)
    spread = jnp.mean(center * center, -1, keepdims=True)
    inverse = lax.rsqrt(spread + NORM_EPS)
    unit = center * inverse
    scaled = grads * gain_row
    back = inverse * (
        scaled
        - jnp.mean(scaled, -1, keepdims=True)
        - unit * jnp.mean(scaled * unit, -1, keepdims=True)
    )
    return back, grads * unit


def tp_forward(stream, normed, mats, gain_two, slopes, valid, scalars, beside=None):
    (joint_out, jo), (expand, ex), (reduce, re) = mats
    width = stream.shape[1]
    joint = piece_dot(normed, joint_out, jo, 64, 3, low=True)
    context = attend(joint, slopes, valid, width // HEADS)
    context = side_by_side(scalars[16], context)
    mixed = piece_dot(context, joint_out, jo + 192, 64, 1)
    if beside is not None:
        mixed, _ = tie((mixed, beside))
    middle, normed_two = norm_forward(stream, mixed, swap_core(mixed), gain_two, scalars, True)
    upper, hidden = piece_dot(normed_two, expand, ex, 64, 4, with_gelu=True)
    lowered = piece_dot(hidden, reduce, re, 128, 2)
    kept = (stream, normed, joint, context, middle, normed_two, upper, hidden)
    return middle, lowered, kept


tie = lax.optimization_barrier


class Share:
    def __init__(self, left, right, spot, by_y):
        y, x = spot
        self.left, self.right = left, right
        if by_y:
            self.hops = [swap_y, swap_x]
            passed, theirs = (y, 1 - x), ((1 - y, 1 - x), (1 - y, x))
        else:
            self.hops = [swap_x, swap_y]
            passed, theirs = (1 - y, x), ((1 - y, 1 - x), (y, 1 - x))
        numbers = [2 * row + column for row, column in (passed, (y, x), *theirs)]
        self.passed, self.own, *theirs = [number.astype(jnp.int32) for number in numbers]
        self.made = packed_tokens(left, right, jnp.stack(theirs))
        self.flying = self.total = self.beside = None
        self.turns = 0

    def send(self):
        if self.hops:
            self.flying = self.hops.pop(0)(self.made)
        else:
            self.flying = None
            self.total = lax.psum_scatter(
                self.made, "fsdp", scatter_dimension=0, axis_index_groups=Z_LINES, tiled=True
            )

    def land(self, landed):
        terms = (self.left, self.right, landed)
        if self.hops:
            self.made = outer_sum(*terms, self.passed[None], 0, LOW)
            self.kept = outer_sum(*terms, self.own[None], 1, WIDE)
        else:
            self.made = (self.kept + landed.astype(WIDE)).astype(LOW)


class Flow:
    def __init__(self):
        self.shares = []

    def add(self, values, *terms):
        added = [Share(*term) for term in terms]
        values, made = tie((values, [share.made for share in added]))
        for share, item in zip(added, made):
            share.made = item
            share.send()
        self.shares += added
        return (*values, *added)

    def turn(self, *values):
        flying = [share for share in self.shares if share.flying is not None]
        summed = [share for share in self.shares if share.total is not None]
        for share in summed:
            share.turns += 1
        summed = [share for share in summed if share.turns == 3]
        values, landed, totals = tie(
            (values, [share.flying for share in flying], [share.total for share in summed])
        )
        for share, item in zip(summed, totals):
            share.total = item
        for share, item in zip(flying, landed):
            share.land(item)
        for share in [share for share in flying if share.beside is not None]:
            if not share.hops:
                share.made = jnp.concatenate([share.made, share.beside.made], 1)
                share.beside.flying = None
                flying.remove(share.beside)
        values, made = tie((values, [share.made for share in flying]))
        for share, item in zip(flying, made):
            share.made = item
            share.send()
        return values


def own_rows(total, core):
    halves = total.reshape(2, total.shape[0] // 2, total.shape[1])
    mine, other = pick(halves, core), swap_core(pick(halves, 1 - core))
    return jnp.stack(in_order(core, mine, other))


def tp_backward(
    incoming, incoming_low, kept, mats, gain_one, gain_two, slopes, valid, spot, scalars, flow
):
    stream, normed, joint, context, middle, normed_two, upper, hidden = kept
    (joint_out, jo), (expand, ex), (reduce, re) = mats
    d_upper = piece_dot_back(incoming_low, reduce, re, 128, upper=upper)
    d_normed = piece_dot_back(d_upper, expand, ex, 64)
    incoming, d_upper, d_normed = flow.turn(incoming, d_upper, d_normed)
    d_normed, g_reduce, g_expand = flow.add(
        (d_normed,), (hidden, incoming_low, spot, False), (normed_two, d_upper, spot, True)
    )
    d_middle, _, d_middle_low, d_gain_two = norm_backward(
        d_normed, swap_core(d_normed), middle, gain_two, incoming, scalars
    )
    mine, other = piece_dot_back(d_middle_low, joint_out, jo + 192, 64, split=True)
    mine, other, d_middle, d_middle_low = flow.turn(mine, other, d_middle, d_middle_low)
    d_joint = attend_back(
        joint, mine, swap_core(other), slopes, valid, stream.shape[1] // HEADS
    )
    d_normed = piece_dot_back(d_joint, joint_out, jo, 64)
    d_joint, d_normed = flow.turn(d_joint, d_normed)
    d_normed, g_output, g_joint = flow.add(
        (d_normed,), (context, d_middle_low, spot, False), (normed, d_joint, spot, True)
    )
    g_joint.beside = g_output
    result = norm_backward(d_normed, swap_core(d_normed), stream, gain_one, d_middle, scalars)
    return result, (g_joint, g_expand, g_reduce), d_gain_two


def paired_shards(
    spectra,
    gaussian,
    flow_times,
    lengths,
    span_flags,
    phone_ids,
    input_master,
    input_moment,
    input_square,
    kernel_master,
    kernel_moment,
    kernel_square,
    joint_master,
    joint_moment,
    joint_square,
    output_master,
    output_moment,
    output_square,
    expand_master,
    expand_moment,
    expand_square,
    reduce_master,
    reduce_moment,
    reduce_square,
    bridge_master,
    bridge_moment,
    bridge_square,
    readout_master,
    readout_moment,
    readout_square,
    gains_master,
    gains_moment,
    gains_square,
):
    dp_index, fsdp_index = lax.axis_index("dp"), lax.axis_index("fsdp")
    y, x = dp_index // 2, dp_index % 2
    z, core = fsdp_index // 2, fsdp_index % 2
    spot = (y, x)
    corners = [2 * y + x, 2 * y + 1 - x, 2 * (1 - y) + x, 2 * (1 - y) + 1 - x]
    behind = [(z - hops) % 4 for hops in range(4)]
    in_place = jnp.stack([*range(16), core]).astype(jnp.int32)
    all_shifted = [4 * corner + line for corner in corners for line in behind]
    all_shifted = jnp.stack([*all_shifted, core]).astype(jnp.int32)
    both_shifted = [4 * corner + line for line in behind for corner in corners]
    both_shifted = jnp.stack([*both_shifted, core]).astype(jnp.int32)
    chip = 8 * y + 4 * x + z
    mel_count, frame_count = spectra.shape[1:]
    taps, outs, group = kernel_master.shape
    width = outs * 32
    blocks = frame_count // TAPS_OUT

    with jax.named_scope("features"):
        flags = span_flags[0].astype(WIDE)
        valid_own = (jnp.arange(frame_count) < lengths[0]).astype(WIDE)
        clean, noise = spectra[0].astype(WIDE), gaussian[0].astype(WIDE)
        time = flow_times[0]
        noisy = (1.0 - (1.0 - SIGMA_MIN) * time) * noise + time * clean
        shown = clean * (1.0 - flags[None, :])
        small = jnp.concatenate(
            [readout_master.astype(LOW), gains_master.astype(LOW).T], 1
        )
        small = jnp.pad(small, ((0, 0), (0, frame_count - small.shape[1])))
        packed = jnp.concatenate(
            [
                noisy.astype(LOW),
                shown.astype(LOW),
                phone_ids.astype(LOW),
                valid_own[None].astype(LOW),
                jnp.zeros((14, frame_count), LOW),
                small,
            ],
            0,
        )
        line = z_line(packed, z)
        beside, across = swap_x(line), swap_y(line)
        corner = swap_y(beside)
        whole = jnp.zeros((4,) + line.shape, LOW)
        for number, part in enumerate((line, beside, across, corner)):
            whole = lax.dynamic_update_index_in_dim(whole, part, corners[number], 0)
        whole = whole.reshape((16,) + packed.shape)
        whole = jnp.stack(in_order(core, whole, swap_core(whole)), 1)
        whole = whole.reshape((32,) + packed.shape)
        mels = whole[:, : 2 * mel_count]
        onehot = (whole[:, 2 * mel_count][:, None, :] == jnp.arange(VOCAB, dtype=LOW)[None, :, None]).astype(LOW)
        features = jnp.concatenate([mels, onehot], 1)
        valid_all = whole[:, 2 * mel_count + 1].astype(WIDE)
        small = whole[:, 2 * mel_count + 16 :].reshape(width, frame_count)
        readout_full = small[:, :mel_count]
        gains_full = small[:, mel_count : mel_count + 5].T.astype(WIDE)

    with jax.named_scope("weights"):
        layers, rows = joint_master.shape[:2]
        tiles = expand_master.shape[2] // (2 * 128 * 4)
        cut_joint = joint_master.astype(LOW).reshape(layers, rows, 3, 2, LANES)
        cut_output = output_master.astype(LOW).reshape(layers, rows, 1, 2, LANES)
        cut_expand = expand_master.astype(LOW).reshape(layers, rows, tiles, 4, 2, 128)
        cut_bridge = bridge_master.astype(LOW).reshape(2, rows, 2, LANES)

        def columns_of(which):
            joint = lax.dynamic_index_in_dim(cut_joint, which, 3, keepdims=False)
            out = lax.dynamic_index_in_dim(cut_output, which, 3, keepdims=False)
            expand = lax.dynamic_index_in_dim(cut_expand, which, 4, keepdims=False)
            expand = expand.reshape(layers, rows, tiles, LANES)
            bridge = lax.dynamic_index_in_dim(cut_bridge, which, 2, keepdims=False)
            blocks = jnp.concatenate([joint, out, expand], 2).transpose(0, 2, 1, 3)
            blocks = blocks.reshape(layers * (4 + tiles), rows, LANES)
            return jnp.concatenate([blocks, bridge], 0)

        mine, other = in_order(core, columns_of(core), swap_core(columns_of(1 - core)))
        blocks = layers * (4 + tiles)
        paired = jnp.stack([mine[:blocks], other[:blocks]], 1)
        paired = paired.reshape(layers, 4 + tiles, 2 * rows, LANES)
        bridge = jnp.concatenate([mine[blocks:], other[blocks:]], 0).reshape(-1, LANES)
        lowered = reduce_master.astype(LOW).reshape(layers, -1, 2, LANES)
        lowered = lowered.transpose(0, 2, 1, 3).reshape(layers, -1, LANES)

        def flat(item):
            return item.reshape(-1, LANES)

        def along_z(own):
            parts = [own]
            for _ in range(3):
                parts.append(shift_z(parts[-1], 1))
            return parts

        def by_permutes(own, after_line, after_square, x_first):
            line = jnp.concatenate(along_z(tie((own, after_line))[0]), 0)
            line = tie((line, after_square))[0]
            beside, across = swap_x(line), swap_y(line)
            corner = swap_y(beside) if x_first else swap_x(across)
            whole = jnp.concatenate([line, beside, across, corner], 0)
            return line, (beside, across), (whole.reshape((16,) + own.shape), all_shifted)

        same_core = [[half + 2 * i for i in range(16)] for half in range(2)]

        def in_background(*parts):
            own = jnp.concatenate(parts, 0)
            whole = lax.all_gather(own, BOTH, axis=0, axis_index_groups=same_core)
            return whole, in_place

        third = in_background(lowered[0], bridge, flat(paired[1, :4]))
        fourth = in_background(flat(paired[1, 4:]))
        first_line, first_square, first = by_permutes(flat(paired[0, :4]), line, line, True)
        last_own = tie((lowered[1], line))[0]
        beside, across = swap_x(last_own), swap_y(last_own)
        square = jnp.concatenate([last_own, beside, across, swap_y(beside)], 0)
        second_line, _, second = by_permutes(
            flat(paired[0, 4:]), first_line, first_square, False
        )
        last = along_z(tie((square, second_line))[0])
        fifth = (jnp.concatenate(last, 0).reshape((16,) + last_own.shape), both_shifted)
        mats_zero = ((first, 0), (second, 0), (third, 0))
        mats_one = ((third, lowered.shape[1] + bridge.shape[0]), (fourth, 0), (fifth, 0))
        bridge_mat = (third, lowered.shape[1])

    with jax.named_scope("embedding"):
        columns = input_master.astype(LOW)
        columns = jnp.concatenate(in_order(core, columns, swap_core(columns)), -1)
        start = jnp.einsum("nzv,zr->nvr", features, columns, preferred_element_type=WIDE)
        start = start * valid_all[:, :, None]
        padded = start.astype(LOW).reshape(32, blocks, TAPS_OUT * group)
        padded = jnp.pad(padded, ((0, 0), (2, 2), (0, 0)))
        windows = jnp.concatenate([padded[:, i : i + blocks] for i in range(5)], -1)
        windows = windows.reshape(32 * blocks, 5 * TAPS_OUT * group)
        turned = jnp.pad(
            kernel_master.astype(LOW).transpose(0, 2, 1), ((TAPS_OUT, TAPS_OUT), (0, 0), (0, 0))
        )
        banded = jnp.stack([turned[7 - j : 47 - j] for j in range(TAPS_OUT)], 2)
        banded = banded.reshape(5, TAPS_OUT * group, TAPS_OUT * outs)
        conv_out = banded_dot(windows, banded)
        start_own = lax.dynamic_slice_in_dim(start, core * outs, outs, 2)
        start_own = start_own.reshape(32 * blocks, TAPS_OUT * outs)
        embedded = start_own + jax.nn.gelu(conv_out)
        embedded = lax.all_to_all(embedded.astype(LOW), BOTH, 0, 0, tiled=True)
        embedded = embedded.reshape(32, frame_count, outs).transpose(1, 0, 2)
        embedded = embedded.reshape(frame_count, width)
        embedded = jnp.concatenate(in_order(core, embedded, swap_core(embedded)), 0)
        embedded = embedded.astype(WIDE)

    slopes = 2.0 ** (
        -8.0 * (jnp.arange(HEADS // 2) + core * (HEADS // 2) + 1.0).astype(WIDE) / HEADS
    )
    valid = lax.dynamic_slice_in_dim(valid_all, 2 * chip, 2, 0)[:, None, :]
    scalars = in_place
    gain = [gains_full[row : row + 1] for row in range(5)]

    with jax.named_scope("forward_layers"):
        embedded, normed = norm_forward(embedded, None, None, gain[0], scalars, False)
        middle, lowered, kept_zero = tp_forward(
            embedded, normed, mats_zero, gain[1], slopes, valid, scalars, last[2]
        )
        encoded = middle + (lowered + swap_core(lowered))
        joined = jnp.concatenate([encoded, embedded], -1).astype(LOW)
        joined, _ = tie((joined, last[3]))
        bridged = piece_dot(joined, *bridge_mat, 128, 1)
        bridged, normed = norm_forward(
            None, bridged, swap_core(bridged), gain[2], scalars, True
        )
        middle, lowered, kept_one = tp_forward(
            bridged, normed, mats_one, gain[3], slopes, valid, scalars
        )
        decoded = middle + (lowered + swap_core(lowered))

    with jax.named_scope("readout_loss"):
        last = pick(decoded.reshape(2, frame_count, width), core)
        final_low = (norm_parts(last) * gains_full[4]).astype(LOW)
        predict = jnp.dot(final_low, readout_full, preferred_element_type=WIDE)
        target = (clean - (1.0 - SIGMA_MIN) * noise).T
        weight = (flags * valid_own)[:, None]
        missed = predict - target
        loss_local = jnp.sum(weight * missed * missed)
        count_local = jnp.sum(weight)
        d_predict = (2.0 * weight * missed).astype(LOW)
        d_readout = lax.dot_general(
            final_low, d_predict, (((0,), (0,)), ((), ())), preferred_element_type=WIDE
        )
        d_final = lax.dot_general(
            d_predict, readout_full, (((1,), (1,)), ((), ())), preferred_element_type=WIDE
        )
        back, gain_terms = norm_back(last, gains_full[4], d_final)
        d_gain_last = jnp.sum(gain_terms, 0)
        d_decoded = jnp.concatenate(in_order(core, back, swap_core(back)), 0)

    with jax.named_scope("backward_layers"):
        flow = Flow()
        parts = (slopes, valid, spot, scalars, flow)
        result, shares_one, d_gain_three = tp_backward(
            d_decoded, d_decoded.astype(LOW), kept_one, mats_one, gain[2], gain[3], *parts
        )
        d_gain_two = result[3]
        d_joined = piece_dot_back(result[2], *bridge_mat, 128)
        d_joined, d_bridged_low = flow.turn(d_joined, result[2])
        d_joined, g_bridge = flow.add((d_joined,), (joined, d_bridged_low, spot, True))
        d_joined = d_joined + swap_core(d_joined)
        d_encoded = d_joined[:, :width]
        result, shares_zero, d_gain_one = tp_backward(
            d_encoded, d_encoded.astype(LOW), kept_zero, mats_zero, gain[0], gain[1], *parts
        )
        d_gain_zero = result[3]
        d_embedded = result[0] + d_joined[:, width:]
        (d_embedded,) = flow.turn(d_embedded)

    with jax.named_scope("embedding_back"):
        own = pick(d_embedded.astype(LOW).reshape(2, frame_count, width), core)
        own = own.reshape(frame_count, 32, outs).transpose(1, 0, 2)
        own = lax.all_to_all(
            own.reshape(32 * blocks, TAPS_OUT * outs), BOTH, 0, 0, tiled=True
        ).astype(WIDE)
        d_conv = jax.vjp(jax.nn.gelu, conv_out)[1](own)[0].astype(LOW)
        padded = jnp.pad(
            d_conv.reshape(32, blocks, TAPS_OUT * outs), ((0, 0), (2, 2), (0, 0))
        )
        shifted = jnp.concatenate([padded[:, 4 - i : 4 - i + blocks] for i in range(5)], -1)
        d_start = banded_back(
            shifted.reshape(32 * blocks, 5 * TAPS_OUT * outs), banded
        )
        d_start = d_start.reshape(32 * blocks, TAPS_OUT, 2, outs)
        mine = lax.dynamic_index_in_dim(d_start, core, 2, keepdims=False)
        other = lax.dynamic_index_in_dim(d_start, 1 - core, 2, keepdims=False)
        other = swap_core(other.reshape(32 * blocks, TAPS_OUT * outs))
        d_start = own + mine.reshape(32 * blocks, TAPS_OUT * outs) + other
        d_start = d_start.reshape(32, frame_count, outs) * valid_all[:, :, None]
        grad_input = jnp.einsum(
            "nzv,nvr->zr", features, d_start.astype(LOW), preferred_element_type=WIDE
        )
        spread = banded_outer(windows, d_conv)
        spread = spread.reshape(5 * TAPS_OUT, group, TAPS_OUT, outs)
        grad_kernel = sum(spread[j + 1 : j + 1 + taps, :, j, :] for j in range(TAPS_OUT))
        grad_kernel = grad_kernel.transpose(0, 2, 1)

    with jax.named_scope("small_grads"):
        d_readout, d_gain_zero, _ = tie((d_readout, d_gain_zero, d_conv))
        d_gains = jnp.concatenate(
            [d_gain_zero, d_gain_one, d_gain_two, d_gain_three, d_gain_last[None]], 0
        )
        fill = jnp.zeros((width, 1), WIDE)
        small = jnp.concatenate([d_readout, d_gains.T, fill + loss_local, fill + count_local], 1)
        small = jnp.pad(small, ((0, 0), (0, 128 - small.shape[1])))
        small = lax.all_to_all(small, BOTH, 0, 0, tiled=True)
        small = jnp.sum(small.reshape(32, width // 32, 128), 0)
        grad_readout = small[:, :mel_count]
        grad_gains = small[:, mel_count : mel_count + 5].T
        loss_sum = small[0, mel_count + 5]
        frame_total = small[0, mel_count + 6]

    with jax.named_scope("own_grads"):
        flow.turn(d_conv)
        for share in [*shares_zero, *shares_one, g_bridge]:
            share.total = tie((share.total, d_conv))[0].astype(WIDE)

        def unfolded(both, count):
            cut = both.reshape(2, both.shape[1], count, both.shape[2] // count)
            return jnp.moveaxis(cut, 0, 2).reshape(both.shape[1], 2 * both.shape[2])

        layer_grads = []
        for joint_share, expand_share, reduce_share in (shares_zero, shares_one):
            both = own_rows(joint_share.total, core)
            layer_grads.append(
                (
                    unfolded(both[:, :, : 3 * LANES], 3),
                    unfolded(both[:, :, 3 * LANES :], 1),
                    unfolded(own_rows(expand_share.total, core), 4 * tiles),
                    reduce_share.total,
                )
            )
        grads = [
            grad_input,
            grad_kernel,
            *[jnp.stack(pair) for pair in zip(*layer_grads)],
            unfolded(own_rows(g_bridge.total, core), 1),
            grad_readout,
            grad_gains,
        ]

    with jax.named_scope("clip_and_update"):
        squares_local = sum((jnp.sum(item * item) for item in grads))
        squared = lax.all_to_all(
            jnp.zeros((32, 128), WIDE) + squares_local, BOTH, 0, 0, tiled=True
        )
        squared = jnp.sum(squared[:, 0])
        grad_norm = jnp.sqrt(squared) / frame_total
        factor = jnp.minimum(1.0, CLIP_LIMIT / grad_norm) / frame_total
        masters = (
            input_master,
            kernel_master,
            joint_master,
            output_master,
            expand_master,
            reduce_master,
            bridge_master,
            readout_master,
            gains_master,
        )
        moments = (
            input_moment,
            kernel_moment,
            joint_moment,
            output_moment,
            expand_moment,
            reduce_moment,
            bridge_moment,
            readout_moment,
            gains_moment,
        )
        squares = (
            input_square,
            kernel_square,
            joint_square,
            output_square,
            expand_square,
            reduce_square,
            bridge_square,
            readout_square,
            gains_square,
        )
        decays = [DECAY_RATE] * 8 + [0.0]
        results = []
        for master, moment, square, grad, rate, decay in zip(
            masters, moments, squares, grads, weight_rates(), decays
        ):
            results.extend(adamw(master, moment, square, factor * grad, rate, decay))
    return (loss_sum, frame_total, grad_norm, *results)


def solution(mesh):
    in_specs = (
        P(("dp", "fsdp"), None, None),
        P(("dp", "fsdp"), None, None),
        P(("dp", "fsdp")),
        P(("dp", "fsdp")),
        P(("dp", "fsdp"), None),
        P(("dp", "fsdp"), None),
        P(None, ("dp", "fsdp")),
        P(None, ("dp", "fsdp")),
        P(None, ("dp", "fsdp")),
        P(None, ("dp", "fsdp"), None),
        P(None, ("dp", "fsdp"), None),
        P(None, ("dp", "fsdp"), None),
        P(None, ("dp", "fsdp"), None),
        P(None, ("dp", "fsdp"), None),
        P(None, ("dp", "fsdp"), None),
        P(None, ("dp", "fsdp"), None),
        P(None, ("dp", "fsdp"), None),
        P(None, ("dp", "fsdp"), None),
        P(None, ("dp", "fsdp"), None),
        P(None, ("dp", "fsdp"), None),
        P(None, ("dp", "fsdp"), None),
        P(None, ("dp", "fsdp"), None),
        P(None, ("dp", "fsdp"), None),
        P(None, ("dp", "fsdp"), None),
        P(("dp", "fsdp"), None),
        P(("dp", "fsdp"), None),
        P(("dp", "fsdp"), None),
        P(("dp", "fsdp"), None),
        P(("dp", "fsdp"), None),
        P(("dp", "fsdp"), None),
        P(None, ("dp", "fsdp")),
        P(None, ("dp", "fsdp")),
        P(None, ("dp", "fsdp")),
    )
    out_specs = (
        P(),
        P(),
        P(),
        P(None, ("dp", "fsdp")),
        P(None, ("dp", "fsdp")),
        P(None, ("dp", "fsdp")),
        P(None, ("dp", "fsdp"), None),
        P(None, ("dp", "fsdp"), None),
        P(None, ("dp", "fsdp"), None),
        P(None, ("dp", "fsdp"), None),
        P(None, ("dp", "fsdp"), None),
        P(None, ("dp", "fsdp"), None),
        P(None, ("dp", "fsdp"), None),
        P(None, ("dp", "fsdp"), None),
        P(None, ("dp", "fsdp"), None),
        P(None, ("dp", "fsdp"), None),
        P(None, ("dp", "fsdp"), None),
        P(None, ("dp", "fsdp"), None),
        P(None, ("dp", "fsdp"), None),
        P(None, ("dp", "fsdp"), None),
        P(None, ("dp", "fsdp"), None),
        P(("dp", "fsdp"), None),
        P(("dp", "fsdp"), None),
        P(("dp", "fsdp"), None),
        P(("dp", "fsdp"), None),
        P(("dp", "fsdp"), None),
        P(("dp", "fsdp"), None),
        P(None, ("dp", "fsdp")),
        P(None, ("dp", "fsdp")),
        P(None, ("dp", "fsdp")),
    )
    paired = mesh.shape["dp"] == 4 and mesh.shape["fsdp"] == 8
    step = paired_shards if paired else shards
    return jax.shard_map(step, mesh=mesh, in_specs=in_specs, out_specs=out_specs, check_vma=False)
```

```python
import jax
import jax.numpy as jnp
from jax import lax
from jax.experimental import pallas as pl
from jax.experimental.pallas import tpu as pltpu
from jax.sharding import PartitionSpec as P

D = 1024
HEADS = 16
FF = 4096
MEL = 80
VOCAB = 96
KS = 31
GROUPS = 16
STEP = 10


SIGMA_MIN = 1e-05
NORM_EPS = 1e-05
MASKED = -1e30
BETA_ONE = 0.9
BETA_TWO = 0.95
ADAM_EPS = 1e-08
DECAY_RATE = 0.01
CLIP_LIMIT = 0.2
RATE_SCALE = 0.5
GAIN_RATE = 0.25


def layer_norm(values, gain_row):
    center = values - jnp.mean(values, -1, keepdims=True)
    spread = jnp.mean(center * center, -1, keepdims=True)
    return center * lax.rsqrt(spread + NORM_EPS) * gain_row


def alibi_bias(frames):
    slopes = 2.0 ** (-8.0 * (jnp.arange(HEADS, dtype=jnp.float32) + 1.0) / HEADS)
    places = jnp.arange(frames, dtype=jnp.float32)
    return -slopes[:, None, None] * jnp.abs(places[:, None] - places[None, :])


def conv_mix(hidden, kernel):
    tap_count = kernel.shape[0]
    margin = tap_count // 2
    seq_count, frame_count, model_width = hidden.shape
    per_group = model_width // GROUPS
    padded = jnp.pad(hidden, ((0, 0), (margin, margin), (0, 0)))
    stacked = jnp.stack([padded[:, tap : tap + frame_count] for tap in range(tap_count)], 1)
    stacked = stacked.reshape(seq_count, tap_count, frame_count, GROUPS, per_group)
    weights = kernel.reshape(tap_count, GROUPS, per_group, per_group)
    mixed = jnp.einsum("bklgc,kgoc->blgo", stacked, weights)
    return mixed.reshape(seq_count, frame_count, model_width)


def score_block(query, keyed, valid, alibi):
    scale = query.shape[-1] ** (-0.5)
    scores = (
        jnp.einsum("sqhd,skhd->shqk", query, keyed, preferred_element_type=jnp.float32) * scale
        + alibi[None]
    )
    return jnp.where(valid[:, None, None, :], scores, MASKED)


def layer_forward(stream, mats, gain_one, gain_two, valid, alibi):
    joint_w, output_w, expand_w, reduce_w = mats
    seq_count, frame_count, model_width = stream.shape
    row_count = seq_count * frame_count
    normed = layer_norm(stream, gain_one).astype(jnp.bfloat16).reshape(row_count, model_width)
    joint = jnp.dot(normed, joint_w, preferred_element_type=jnp.float32).astype(jnp.bfloat16)
    joint = joint.reshape(seq_count, frame_count, 3, HEADS, model_width // HEADS)
    scores = score_block(joint[:, :, 0], joint[:, :, 1], valid, alibi)
    highest = jnp.max(scores, -1, keepdims=True)
    raised = jnp.exp(scores - highest)
    totals = jnp.sum(raised, -1, keepdims=True)
    probs = raised / totals
    log_total = highest + jnp.log(totals)
    context = jnp.einsum(
        "shqk,skhd->sqhd",
        probs.astype(jnp.bfloat16),
        joint[:, :, 2],
        preferred_element_type=jnp.float32,
    )
    context = context.astype(jnp.bfloat16).reshape(row_count, model_width)
    middle = stream + jnp.dot(context, output_w, preferred_element_type=jnp.float32).reshape(
        stream.shape
    )
    normed_two = layer_norm(middle, gain_two).astype(jnp.bfloat16).reshape(row_count, model_width)
    upper = jnp.dot(normed_two, expand_w, preferred_element_type=jnp.float32)
    hidden = jax.nn.gelu(upper).astype(jnp.bfloat16)
    result = middle + jnp.dot(hidden, reduce_w, preferred_element_type=jnp.float32).reshape(
        stream.shape
    )
    return (result, (stream, normed, joint, log_total, context, middle, normed_two, upper, hidden))


def layer_backward(incoming, kept, mats, gain_one, gain_two, valid, alibi):
    stream, normed, joint, log_total, context, middle, normed_two, upper, hidden = kept
    joint_w, output_w, expand_w, reduce_w = mats
    seq_count, frame_count, model_width = stream.shape
    row_count = seq_count * frame_count
    incoming_low = incoming.reshape(row_count, model_width).astype(jnp.bfloat16)
    d_reduce = jnp.dot(hidden.T, incoming_low, preferred_element_type=jnp.float32)
    d_hidden = jnp.dot(incoming_low, reduce_w.T, preferred_element_type=jnp.float32)
    gelu_pull = jax.vjp(jax.nn.gelu, upper)[1]
    d_upper = gelu_pull(d_hidden)[0].astype(jnp.bfloat16)
    d_expand = jnp.dot(normed_two.T, d_upper, preferred_element_type=jnp.float32)
    d_normed = jnp.dot(d_upper, expand_w.T, preferred_element_type=jnp.float32).reshape(
        stream.shape
    )
    norm_pull = jax.vjp(layer_norm, middle, gain_two)[1]
    d_middle, d_gain_two = norm_pull(d_normed)
    d_middle = d_middle + incoming
    d_middle_low = d_middle.reshape(row_count, model_width).astype(jnp.bfloat16)
    d_output = jnp.dot(context.T, d_middle_low, preferred_element_type=jnp.float32)
    d_context = jnp.dot(d_middle_low, output_w.T, preferred_element_type=jnp.float32).astype(
        jnp.bfloat16
    )
    d_context = d_context.reshape(seq_count, frame_count, HEADS, model_width // HEADS)
    query, keyed, valued = (joint[:, :, 0], joint[:, :, 1], joint[:, :, 2])
    probs = jnp.exp(score_block(query, keyed, valid, alibi) - log_total)
    d_probs = jnp.einsum("sqhd,skhd->shqk", d_context, valued, preferred_element_type=jnp.float32)
    d_valued = jnp.einsum(
        "shqk,sqhd->skhd", probs.astype(jnp.bfloat16), d_context, preferred_element_type=jnp.float32
    )
    inner = jnp.sum(probs * d_probs, -1, keepdims=True)
    d_scores = (probs * (d_probs - inner)).astype(jnp.bfloat16)
    scale = query.shape[-1] ** (-0.5)
    d_query = (
        jnp.einsum("shqk,skhd->sqhd", d_scores, keyed, preferred_element_type=jnp.float32) * scale
    )
    d_keyed = (
        jnp.einsum("shqk,sqhd->skhd", d_scores, query, preferred_element_type=jnp.float32) * scale
    )
    d_joint = (
        jnp.stack([d_query, d_keyed, d_valued], 2)
        .astype(jnp.bfloat16)
        .reshape(row_count, 3 * model_width)
    )
    d_joint_w = jnp.dot(normed.T, d_joint, preferred_element_type=jnp.float32)
    d_normed = jnp.dot(d_joint, joint_w.T, preferred_element_type=jnp.float32).reshape(stream.shape)
    norm_pull = jax.vjp(layer_norm, stream, gain_one)[1]
    d_stream, d_gain_one = norm_pull(d_normed)
    return (d_stream + d_middle, (d_joint_w, d_output, d_expand, d_reduce), d_gain_one, d_gain_two)


def adamw(master, moment, square, grad, rate, decay):
    moment = BETA_ONE * moment + (1.0 - BETA_ONE) * grad
    square = BETA_TWO * square + (1.0 - BETA_TWO) * grad * grad
    fixed_moment = moment / (1.0 - BETA_ONE**STEP)
    fixed_square = square / (1.0 - BETA_TWO**STEP)
    return (
        moment,
        square,
        master - rate * (fixed_moment / (jnp.sqrt(fixed_square) + ADAM_EPS) + decay * master),
    )


def weight_rates():
    fan_ins = (MEL, KS * (D // GROUPS), D, D // 8, D, FF, 2 * D, D)
    return [RATE_SCALE * fan_in ** (-0.5) for fan_in in fan_ins] + [GAIN_RATE]


def shards(
    spectra,
    gaussian,
    flow_times,
    lengths,
    span_flags,
    phone_ids,
    input_master,
    input_moment,
    input_square,
    kernel_master,
    kernel_moment,
    kernel_square,
    joint_master,
    joint_moment,
    joint_square,
    output_master,
    output_moment,
    output_square,
    expand_master,
    expand_moment,
    expand_square,
    reduce_master,
    reduce_moment,
    reduce_square,
    bridge_master,
    bridge_moment,
    bridge_square,
    readout_master,
    readout_moment,
    readout_square,
    gains_master,
    gains_moment,
    gains_square,
):
    low_type = jnp.bfloat16
    wide_dtype = jnp.float32
    input_wide, kernel_full, bridge_full, readout_full, gains_full = (
        lax.all_gather(input_master.astype(low_type), ("dp", "fsdp"), axis=1, tiled=True),
        lax.all_gather(kernel_master.astype(low_type), ("dp", "fsdp"), axis=1, tiled=True),
        lax.all_gather(bridge_master.astype(low_type), ("dp", "fsdp"), axis=0, tiled=True),
        lax.all_gather(readout_master.astype(low_type), ("dp", "fsdp"), axis=0, tiled=True),
        lax.all_gather(gains_master.astype(low_type), ("dp", "fsdp"), axis=1, tiled=True),
    )
    gains_full = gains_full.astype(wide_dtype)

    def fetch(layer_index):
        return (
            lax.all_gather(
                joint_master[layer_index].astype(low_type), ("dp", "fsdp"), axis=0, tiled=True
            ),
            lax.all_gather(
                output_master[layer_index].astype(low_type), ("dp", "fsdp"), axis=0, tiled=True
            ),
            lax.all_gather(
                expand_master[layer_index].astype(low_type), ("dp", "fsdp"), axis=0, tiled=True
            ),
            lax.all_gather(
                reduce_master[layer_index].astype(low_type), ("dp", "fsdp"), axis=0, tiled=True
            ),
        )

    def share(grads):
        return (
            lax.psum_scatter(grads[0], ("dp", "fsdp"), scatter_dimension=0, tiled=True),
            lax.psum_scatter(grads[1], ("dp", "fsdp"), scatter_dimension=0, tiled=True),
            lax.psum_scatter(grads[2], ("dp", "fsdp"), scatter_dimension=0, tiled=True),
            lax.psum_scatter(grads[3], ("dp", "fsdp"), scatter_dimension=0, tiled=True),
        )

    seq_count, mel_count, frame_count = spectra.shape
    row_count = seq_count * frame_count
    valid = jnp.arange(frame_count)[None, :] < lengths[:, None]
    valid_float = valid.astype(wide_dtype)
    flags = span_flags.astype(wide_dtype)
    clean = spectra.astype(wide_dtype)
    noise_full = gaussian.astype(wide_dtype)
    scaled = flow_times[:, None, None]
    noisy = (1.0 - (1.0 - SIGMA_MIN) * scaled) * noise_full + scaled * clean
    context = clean * (1.0 - flags[:, None, :])
    onehot = (phone_ids[:, None, :] == jnp.arange(VOCAB)[None, :, None]).astype(low_type)
    feature_rows = jnp.concatenate([noisy.astype(low_type), context.astype(low_type), onehot], 1)
    initial_state = (
        jnp.einsum("nzv,zr->nvr", feature_rows, input_wide, preferred_element_type=wide_dtype)
        * valid_float[:, :, None]
    )
    conv_out, conv_pull = jax.vjp(
        conv_mix, initial_state.astype(low_type).astype(wide_dtype), kernel_full.astype(wide_dtype)
    )
    embedded = initial_state + jax.nn.gelu(conv_out)
    alibi = alibi_bias(frame_count)
    mats_zero = fetch(0)
    encoded, kept_zero = layer_forward(
        embedded, mats_zero, gains_full[0], gains_full[1], valid, alibi
    )
    model_width = encoded.shape[-1]
    joined = (
        jnp.concatenate([encoded, embedded], -1)
        .astype(low_type)
        .reshape(row_count, 2 * model_width)
    )
    bridged = jnp.dot(joined, bridge_full, preferred_element_type=wide_dtype).reshape(encoded.shape)
    mats_one = fetch(1)
    decoded, kept_one = layer_forward(bridged, mats_one, gains_full[2], gains_full[3], valid, alibi)
    final_low = layer_norm(decoded, gains_full[4]).astype(low_type).reshape(row_count, model_width)
    predict = jnp.dot(final_low, readout_full, preferred_element_type=wide_dtype)
    target = jnp.swapaxes(clean - (1.0 - SIGMA_MIN) * noise_full, 1, 2).reshape(
        row_count, mel_count
    )
    weight = (flags * valid_float).reshape(row_count, 1)
    missed = predict - target
    loss_local = jnp.sum(weight * missed * missed)
    count_local = jnp.sum(weight)
    loss_sum, frame_total = lax.psum((loss_local, count_local), ("dp", "fsdp"))
    d_predict = (2.0 * weight * missed).astype(low_type)
    d_readout = jnp.dot(final_low.T, d_predict, preferred_element_type=wide_dtype)
    d_final = jnp.dot(d_predict, readout_full.T, preferred_element_type=wide_dtype).reshape(
        decoded.shape
    )
    final_pull = jax.vjp(layer_norm, decoded, gains_full[4])[1]
    d_decoded, d_gain_last = final_pull(d_final)
    mats_back = mats_one
    d_bridged, grads_one, d_gain_two, d_gain_three = layer_backward(
        d_decoded, kept_one, mats_back, gains_full[2], gains_full[3], valid, alibi
    )
    shard_one = share(grads_one)
    d_bridged_low = d_bridged.reshape(row_count, model_width).astype(low_type)
    d_bridge = jnp.dot(joined.T, d_bridged_low, preferred_element_type=wide_dtype)
    d_joined = jnp.dot(d_bridged_low, bridge_full.T, preferred_element_type=wide_dtype).reshape(
        seq_count, frame_count, 2 * model_width
    )
    mats_back = mats_zero
    d_embedded, grads_zero, d_gain_zero, d_gain_one = layer_backward(
        d_joined[:, :, :model_width],
        kept_zero,
        mats_back,
        gains_full[0],
        gains_full[1],
        valid,
        alibi,
    )
    shard_zero = share(grads_zero)
    d_embedded = d_embedded + d_joined[:, :, model_width:]
    gelu_pull = jax.vjp(jax.nn.gelu, conv_out)[1]
    d_conv = gelu_pull(d_embedded)[0].astype(low_type).astype(wide_dtype)
    d_conv_in, d_kernel = conv_pull(d_conv)
    initial_gradient = ((d_embedded + d_conv_in) * valid_float[:, :, None]).astype(low_type)
    input_gradient = jnp.einsum(
        "fpk,fkq->pq", feature_rows, initial_gradient, preferred_element_type=wide_dtype
    )
    d_gains = jnp.stack([d_gain_zero, d_gain_one, d_gain_two, d_gain_three, d_gain_last])
    edge_input, edge_kernel, edge_bridge, edge_readout, edge_gains = (
        lax.psum_scatter(input_gradient, ("dp", "fsdp"), scatter_dimension=1, tiled=True),
        lax.psum_scatter(d_kernel, ("dp", "fsdp"), scatter_dimension=1, tiled=True),
        lax.psum_scatter(d_bridge, ("dp", "fsdp"), scatter_dimension=0, tiled=True),
        lax.psum_scatter(d_readout, ("dp", "fsdp"), scatter_dimension=0, tiled=True),
        lax.psum_scatter(d_gains, ("dp", "fsdp"), scatter_dimension=1, tiled=True),
    )
    layer_shards = [
        jnp.stack([zero_part, one_part]) for zero_part, one_part in zip(shard_zero, shard_one)
    ]
    grads = [edge_input, edge_kernel] + layer_shards + [edge_bridge, edge_readout, edge_gains]
    squares_local = sum((jnp.sum(item * item) for item in grads))
    squared = lax.psum(squares_local, ("dp", "fsdp"))
    grad_norm = jnp.sqrt(squared) / frame_total
    factor = jnp.minimum(1.0, CLIP_LIMIT / grad_norm) / frame_total
    masters = (
        input_master,
        kernel_master,
        joint_master,
        output_master,
        expand_master,
        reduce_master,
        bridge_master,
        readout_master,
        gains_master,
    )
    moments = (
        input_moment,
        kernel_moment,
        joint_moment,
        output_moment,
        expand_moment,
        reduce_moment,
        bridge_moment,
        readout_moment,
        gains_moment,
    )
    squares = (
        input_square,
        kernel_square,
        joint_square,
        output_square,
        expand_square,
        reduce_square,
        bridge_square,
        readout_square,
        gains_square,
    )
    decays = [DECAY_RATE] * 8 + [0.0]
    results = []
    for master, moment, square, grad, rate, decay in zip(
        masters, moments, squares, grads, weight_rates(), decays
    ):
        results.extend(adamw(master, moment, square, factor * grad, rate, decay))
    return (loss_sum, frame_total, grad_norm, *results)


LOW = jnp.bfloat16
WIDE = jnp.float32
BOTH = ("dp", "fsdp")
VMEM_GRANT = 24 * 2**20
GRANT = pltpu.CompilerParams(vmem_limit_bytes=VMEM_GRANT)
TAPS_OUT = 8
GELU_SCALE = 0.7978845608028654
SHORT = pl.CostEstimate(flops=1000, bytes_accessed=1000, transcendentals=0)
LANES = 512
Z_LINES = [[half + 2 * i for i in range(4)] for half in range(2)]


def swap_x(item):
    return lax.ppermute(item, "dp", [(i, i ^ 1) for i in range(4)])


def swap_y(item):
    return lax.ppermute(item, "dp", [(i, i ^ 2) for i in range(4)])


def swap_core(item):
    return lax.ppermute(item, "fsdp", [(i, i ^ 1) for i in range(8)])


def shift_z(item, hops):
    return lax.ppermute(item, "fsdp", [(i, (i + 2 * hops) % 8) for i in range(8)])


def pick(stacked, index):
    return lax.dynamic_index_in_dim(stacked, index, 0, keepdims=False)


def in_order(core, mine, other):
    first = core == 0
    return jnp.where(first, mine, other), jnp.where(first, other, mine)


def side_by_side(core, mine):
    return jnp.concatenate(in_order(core, mine, swap_core(mine)), -1)


def z_line(own, z):
    parts = [own] + [shift_z(own, hops) for hops in (1, 2, 3)]
    line = jnp.zeros((4,) + own.shape, own.dtype)
    for hops, part in enumerate(parts):
        line = lax.dynamic_update_index_in_dim(line, part, (z - hops) % 4, 0)
    return line


def laid_out(weights_ref, places_ref, whole_ref, part):
    for slot in range(16):
        start = pl.multiple_of(places_ref[slot] * part, 16)
        whole_ref[pl.ds(start, part), :] = weights_ref[slot]


def piece_dot(rows, weights, base, part, count, low=False, with_gelu=False):
    gathered, places = weights
    row_count, depth = rows.shape
    out_type = LOW if low else WIDE
    width = count * LANES

    def body(places_ref, rows_ref, weights_ref, *refs):
        whole_ref = refs[-1]
        laid_out(weights_ref, places_ref, whole_ref, part)
        total = jnp.dot(rows_ref[...], whole_ref[...], preferred_element_type=WIDE)
        refs[0][...] = total.astype(out_type)
        if with_gelu:
            refs[1][...] = jax.nn.gelu(total).astype(LOW)

    out_spec = pl.BlockSpec((row_count, LANES), lambda j, s: (0, j))
    shape = jax.ShapeDtypeStruct((row_count, width), out_type)
    low_shape = jax.ShapeDtypeStruct((row_count, width), LOW)
    return pl.pallas_call(
        body,
        grid_spec=pltpu.PrefetchScalarGridSpec(
            num_scalar_prefetch=1,
            grid=(count,),
            in_specs=[
                pl.BlockSpec((row_count, depth), lambda j, s: (0, 0)),
                pl.BlockSpec((16, part, LANES), lambda j, s: (0, j + base // part, 0)),
            ],
            out_specs=[out_spec, out_spec] if with_gelu else out_spec,
            scratch_shapes=[pltpu.VMEM((depth, LANES), LOW)],
        ),
        out_shape=[shape, low_shape] if with_gelu else shape,
        compiler_params=GRANT,
        cost_estimate=SHORT,
    )(places, rows, gathered)


def gelu_slope(values):
    cubic = 0.044715 * values * values
    bent = jnp.tanh(GELU_SCALE * values * (1.0 + cubic))
    return 0.5 * (1.0 + bent) + 0.5 * values * (1.0 - bent * bent) * GELU_SCALE * (
        1.0 + 3.0 * cubic
    )


def piece_dot_back(grads, weights, base, part, upper=None, split=False):
    gathered, places = weights
    row_count, width = grads.shape
    depth, steps = 16 * part, grads.shape[1] // LANES
    half = depth // 2

    def body(places_ref, grads_ref, weights_ref, *refs):
        total_ref, whole_ref = refs[-2:]
        laid_out(weights_ref, places_ref, whole_ref, part)
        product = lax.dot_general(
            grads_ref[...],
            whole_ref[...],
            (((1,), (1,)), ((), ())),
            preferred_element_type=WIDE,
        )

        @pl.when(pl.program_id(0) == 0)
        def _():
            total_ref[...] = product

        @pl.when(pl.program_id(0) > 0)
        def _():
            total_ref[...] += product

        @pl.when(pl.program_id(0) == steps - 1)
        def _():
            if upper is not None:
                refs[1][...] = (total_ref[...] * gelu_slope(refs[0][...])).astype(LOW)
            elif split:
                core = places_ref[16]
                refs[0][...] = total_ref[:, pl.ds(pl.multiple_of(core * half, 128), half)]
                refs[1][...] = total_ref[:, pl.ds(pl.multiple_of((1 - core) * half, 128), half)]
            else:
                refs[0][...] = total_ref[...]

    def fixed(shape):
        return pl.BlockSpec(shape, lambda j, s: (0, 0))

    if split:
        shapes = [jax.ShapeDtypeStruct((row_count, half), WIDE)] * 2
    else:
        shapes = [jax.ShapeDtypeStruct((row_count, depth), WIDE if upper is None else LOW)]
    extra = [] if upper is None else [upper]
    out = pl.pallas_call(
        body,
        grid_spec=pltpu.PrefetchScalarGridSpec(
            num_scalar_prefetch=1,
            grid=(steps,),
            in_specs=[
                pl.BlockSpec((row_count, LANES), lambda j, s: (0, j)),
                pl.BlockSpec((16, part, LANES), lambda j, s: (0, j + base // part, 0)),
            ]
            + [fixed(item.shape) for item in extra],
            out_specs=[fixed(item.shape) for item in shapes],
            scratch_shapes=[
                pltpu.VMEM((row_count, depth), WIDE),
                pltpu.VMEM((depth, LANES), LOW),
            ],
        ),
        out_shape=shapes,
        compiler_params=GRANT,
        cost_estimate=SHORT,
    )(places, grads, gathered, *extra)
    return out if split else out[0]


def whole_blocks(items):
    return [pl.BlockSpec(item.shape, lambda s, n=len(item.shape): (0,) * n) for item in items]


def one_step(body, scalars, operands, shapes, scratch=()):
    return pl.pallas_call(
        body,
        grid_spec=pltpu.PrefetchScalarGridSpec(
            num_scalar_prefetch=1,
            grid=(),
            in_specs=[pl.BlockSpec(memory_space=pltpu.VMEM)] * len(operands),
            out_specs=[pl.BlockSpec(memory_space=pltpu.VMEM)] * len(shapes),
            scratch_shapes=list(scratch),
        ),
        out_shape=shapes,
        compiler_params=GRANT,
        cost_estimate=SHORT,
    )(scalars, *operands)


def norm_forward(base, mine, other, gain, scalars, halves):
    addends = [] if mine is None else [mine, other]
    bases = [] if base is None else [base]
    rows = (mine if base is None else base).shape[0]
    width = gain.shape[1]
    half = width // 2

    def body(scalars_ref, *refs):
        gain_ref, stream_ref, normed_ref = refs[-3:]
        base_ref = None if base is None else refs[0]
        if mine is None:
            stream_ref[...] = base_ref[...]
        elif halves:
            mine_ref, other_ref = refs[len(bases) : len(bases) + 2]
            core = scalars_ref[16]
            for ref, side in ((mine_ref, core), (other_ref, 1 - core)):
                lanes = pl.ds(pl.multiple_of(side * half, 128), half)
                part = ref[...]
                stream_ref[:, lanes] = part if base is None else base_ref[:, lanes] + part
        else:
            mine_ref, other_ref = refs[len(bases) : len(bases) + 2]
            stream_ref[...] = base_ref[...] + (mine_ref[...] + other_ref[...])
        normed_ref[...] = (norm_parts(stream_ref[...]) * gain_ref[...]).astype(LOW)

    shapes = [jax.ShapeDtypeStruct((rows, width), WIDE), jax.ShapeDtypeStruct((rows, width), LOW)]
    return one_step(body, scalars, (*bases, *addends, gain), shapes)


def norm_backward(mine, other, values, gain, incoming, scalars):
    rows, width = values.shape
    half = width // 2

    def body(scalars_ref, mine_ref, other_ref, values_ref, gain_ref, incoming_ref, *refs):
        total_ref, low_ref, low_half_ref, row_ref, terms_ref = refs
        core = scalars_ref[16]
        back, terms = norm_back(values_ref[...], gain_ref[...], mine_ref[...] + other_ref[...])
        total = incoming_ref[...] + back
        total_ref[...] = total
        low_ref[...] = total.astype(LOW)
        low_half_ref[...] = low_ref[:, pl.ds(pl.multiple_of(core * half, 128), half)]
        terms_ref[...] = terms
        own = terms_ref[pl.ds(pl.multiple_of(core * (rows // 2), 8), rows // 2), :]
        row_ref[...] = jnp.sum(own, 0, keepdims=True)

    shapes = [
        jax.ShapeDtypeStruct((rows, width), WIDE),
        jax.ShapeDtypeStruct((rows, width), LOW),
        jax.ShapeDtypeStruct((rows, half), LOW),
        jax.ShapeDtypeStruct((1, width), WIDE),
    ]
    scratch = [pltpu.VMEM((rows, width), WIDE)]
    return one_step(
        body, scalars, (mine, other, values, gain, incoming), shapes, scratch
    )


def head_probs(joint_ref, head, size, slope, valid, distance):
    third = joint_ref.shape[1] // 3
    query = joint_ref[:, head * size : (head + 1) * size]
    keyed = joint_ref[:, third + head * size : third + (head + 1) * size]
    scores = lax.dot_general(
        query, keyed, (((1,), (1,)), ((), ())), preferred_element_type=WIDE
    )
    scores = jnp.where(valid, scores * size ** (-0.5) - slope * distance, MASKED)
    raised = jnp.exp(scores - jnp.max(scores, -1, keepdims=True))
    return query, keyed, raised / jnp.sum(raised, -1, keepdims=True)


def frame_distance(frames):
    ahead = lax.broadcasted_iota(jnp.int32, (frames, frames), 0)
    return jnp.abs(ahead - lax.broadcasted_iota(jnp.int32, (frames, frames), 1)).astype(WIDE)


def attend(joint, slopes, valid, size):
    rows, triple = joint.shape
    frames, third = rows // 2, triple // 3

    def body(slopes_ref, joint_ref, valid_ref, out_ref):
        distance = frame_distance(frames)
        mask = jnp.broadcast_to(valid_ref[0] > 0.5, (frames, frames))
        for head in range(third // size):
            _, _, probs = head_probs(joint_ref, head, size, slopes_ref[head], mask, distance)
            value = joint_ref[:, 2 * third + head * size : 2 * third + (head + 1) * size]
            mixed = jnp.dot(probs.astype(LOW), value, preferred_element_type=WIDE)
            out_ref[:, head * size : (head + 1) * size] = mixed.astype(LOW)

    return pl.pallas_call(
        body,
        grid_spec=pltpu.PrefetchScalarGridSpec(
            num_scalar_prefetch=1,
            grid=(2,),
            in_specs=[
                pl.BlockSpec((frames, triple), lambda u, s: (u, 0)),
                pl.BlockSpec((1, 1, frames), lambda u, s: (u, 0, 0)),
            ],
            out_specs=pl.BlockSpec((frames, third), lambda u, s: (u, 0)),
        ),
        out_shape=jax.ShapeDtypeStruct((rows, third), LOW),
        compiler_params=GRANT,
        cost_estimate=SHORT,
    )(slopes, joint, valid)


def attend_back(joint, mine, other, slopes, valid, size):
    rows, triple = joint.shape
    frames, third = rows // 2, triple // 3

    def body(slopes_ref, joint_ref, mine_ref, other_ref, valid_ref, out_ref):
        distance = frame_distance(frames)
        mask = jnp.broadcast_to(valid_ref[0] > 0.5, (frames, frames))
        scale = size ** (-0.5)
        for head in range(third // size):
            cut = slice(head * size, (head + 1) * size)
            query, keyed, probs = head_probs(
                joint_ref, head, size, slopes_ref[head], mask, distance
            )
            value = joint_ref[:, 2 * third + head * size : 2 * third + (head + 1) * size]
            grad = (mine_ref[:, cut] + other_ref[:, cut]).astype(LOW)
            d_probs = lax.dot_general(
                grad, value, (((1,), (1,)), ((), ())), preferred_element_type=WIDE
            )
            inner = jnp.sum(probs * d_probs, -1, keepdims=True)
            d_scores = (probs * (d_probs - inner)).astype(LOW)
            d_query = jnp.dot(d_scores, keyed, preferred_element_type=WIDE) * scale
            d_keyed = jnp.dot(d_scores.T, query, preferred_element_type=WIDE) * scale
            d_value = jnp.dot(probs.astype(LOW).T, grad, preferred_element_type=WIDE)
            for spot, item in enumerate((d_query, d_keyed, d_value)):
                start = spot * third + head * size
                out_ref[:, start : start + size] = item.astype(LOW)

    def utterance(width):
        return pl.BlockSpec((frames, width), lambda u, s: (u, 0))

    return pl.pallas_call(
        body,
        grid_spec=pltpu.PrefetchScalarGridSpec(
            num_scalar_prefetch=1,
            grid=(2,),
            in_specs=[
                utterance(triple),
                utterance(third),
                utterance(third),
                pl.BlockSpec((1, 1, frames), lambda u, s: (u, 0, 0)),
            ],
            out_specs=utterance(triple),
        ),
        out_shape=jax.ShapeDtypeStruct((rows, triple), LOW),
        compiler_params=GRANT,
        cost_estimate=SHORT,
    )(slopes, joint, mine, other, valid)


def packed_tokens(left, right, numbers):
    rows, depth = left.shape
    quarter, width = depth // 4, right.shape[1]

    def body(numbers_ref, left_ref, right_ref, out_ref):
        for spot in range(2):
            start = pl.multiple_of(numbers_ref[spot] * quarter, 128)
            out_ref[:, spot * quarter : (spot + 1) * quarter] = left_ref[:, pl.ds(start, quarter)]
        out_ref[:, 2 * quarter :] = right_ref[...]

    shapes = [jax.ShapeDtypeStruct((rows, 2 * quarter + width), LOW)]
    return one_step(body, numbers, (left, right), shapes)[0]


def outer_sum(left, right, got, number, second, out_type):
    rows, depth = left.shape
    quarter, width = depth // 4, right.shape[1]

    def body(number_ref, left_ref, right_ref, far_left_ref, far_right_ref, out_ref):
        dims = (((0,), (0,)), ((), ()))
        total = lax.dot_general(
            left_ref[...], right_ref[...], dims, preferred_element_type=WIDE
        )
        total = total + lax.dot_general(
            far_left_ref[...], far_right_ref[...], dims, preferred_element_type=WIDE
        )
        out_ref[...] = total.astype(out_type)

    return pl.pallas_call(
        body,
        grid_spec=pltpu.PrefetchScalarGridSpec(
            num_scalar_prefetch=1,
            grid=(width // LANES,),
            in_specs=[
                pl.BlockSpec((rows, quarter), lambda j, s: (0, s[0])),
                pl.BlockSpec((rows, LANES), lambda j, s: (0, j)),
                pl.BlockSpec((rows, quarter), lambda j, s: (0, second)),
                pl.BlockSpec((rows, LANES), lambda j, s: (0, j + 2 * quarter // LANES)),
            ],
            out_specs=pl.BlockSpec((quarter, LANES), lambda j, s: (0, j)),
        ),
        out_shape=jax.ShapeDtypeStruct((quarter, width), out_type),
        compiler_params=GRANT,
        cost_estimate=SHORT,
    )(number, left, right, got, got)


def banded_kernel(body, operands, blocks, out_block, shape, sums):
    def summed(*refs):
        if not sums:
            refs[-1][...] = body(*refs[:-1])
            return

        @pl.when(pl.program_id(0) == 0)
        def _():
            refs[-1][...] = jnp.zeros_like(refs[-1])

        refs[-1][...] += body(*refs[:-1])

    return pl.pallas_call(
        summed,
        grid=(5,),
        in_specs=blocks,
        out_specs=out_block,
        out_shape=jax.ShapeDtypeStruct(shape, WIDE),
        compiler_params=GRANT,
        cost_estimate=SHORT,
    )(*operands)


def banded_dot(windows, banded):
    rows, (_, depth, width) = windows.shape[0], banded.shape
    return banded_kernel(
        lambda left, right: jnp.dot(left[...], right[0], preferred_element_type=WIDE),
        (windows, banded),
        [
            pl.BlockSpec((rows, depth), lambda i: (0, i)),
            pl.BlockSpec((1, depth, width), lambda i: (i, 0, 0)),
        ],
        pl.BlockSpec((rows, width), lambda i: (0, 0)),
        (rows, width),
        True,
    )


def banded_back(own, conv_out, windows, banded, scalars):
    rows, width = own.shape
    count, depth, _ = banded.shape
    blocks = rows // 32
    half = depth // 2

    def body(scalars_ref, own_ref, conv_ref, windows_ref, banded_ref, *refs):
        mine_ref, other_ref, outer_ref, padded_ref, low_ref, total_ref = refs
        step = pl.program_id(0)

        @pl.when(step == 0)
        def _():
            grads = own_ref[...].astype(WIDE) * gelu_slope(conv_ref[...])
            low_ref[...] = grads.astype(LOW)
            padded_ref[...] = jnp.zeros_like(padded_ref)
            padded_ref[:, 8 : 8 + blocks, :] = low_ref[...].astype(WIDE).reshape(32, blocks, width)
            total_ref[...] = jnp.zeros_like(total_ref)

        for number in range(count):

            @pl.when(step == number)
            def _():
                shifted = padded_ref[:, 10 - number : 10 - number + blocks, :]
                total_ref[...] += lax.dot_general(
                    shifted.reshape(rows, width).astype(LOW),
                    banded_ref[0],
                    (((1,), (1,)), ((), ())),
                    preferred_element_type=WIDE,
                )

        outer_ref[...] = lax.dot_general(
            windows_ref[...], low_ref[...], (((0,), (0,)), ((), ())), preferred_element_type=WIDE
        )

        @pl.when(step == count - 1)
        def _():
            core = scalars_ref[16]
            mine_ref[...] = total_ref[:, pl.ds(pl.multiple_of(core * half, 128), half)]
            other_ref[...] = total_ref[:, pl.ds(pl.multiple_of((1 - core) * half, 128), half)]

    def fixed(shape):
        return pl.BlockSpec(shape, lambda i, s: (0, 0))

    return pl.pallas_call(
        body,
        grid_spec=pltpu.PrefetchScalarGridSpec(
            num_scalar_prefetch=1,
            grid=(count,),
            in_specs=[
                fixed((rows, width)),
                fixed((rows, width)),
                pl.BlockSpec((rows, depth), lambda i, s: (0, i)),
                pl.BlockSpec((1, depth, width), lambda i, s: (i, 0, 0)),
            ],
            out_specs=[
                fixed((rows, half)),
                fixed((rows, half)),
                pl.BlockSpec((depth, width), lambda i, s: (i, 0)),
            ],
            scratch_shapes=[
                pltpu.VMEM((32, blocks + 16, width), WIDE),
                pltpu.VMEM((rows, width), LOW),
                pltpu.VMEM((rows, depth), WIDE),
            ],
        ),
        out_shape=[
            jax.ShapeDtypeStruct((rows, half), WIDE),
            jax.ShapeDtypeStruct((rows, half), WIDE),
            jax.ShapeDtypeStruct((count * depth, width), WIDE),
        ],
        compiler_params=GRANT,
        cost_estimate=SHORT,
    )(scalars, own, conv_out, windows, banded)


def input_grad(own, mine, other, valid, strided, scalars):
    frames, channels, _ = strided.shape
    outs = own.shape[1] // frames

    def body(scalars_ref, own_ref, mine_ref, other_ref, valid_ref, strided_ref, out_ref):
        total = None
        grads = own_ref[...].astype(WIDE) + mine_ref[...] + other_ref[...]
        for frame in range(frames):
            part = grads[:, frame * outs : (frame + 1) * outs] * valid_ref[:, frame : frame + 1]
            product = jnp.dot(
                strided_ref[frame], part.astype(LOW), preferred_element_type=WIDE
            )
            total = product if total is None else total + product
        out_ref[...] = total.T

    shapes = [jax.ShapeDtypeStruct((outs, channels), WIDE)]
    return one_step(body, scalars, (own, mine, other, valid, strided), shapes)[0]


def kernel_grad(spread, taps, outs, scalars):
    count = spread.shape[0] // (2 * TAPS_OUT * outs)

    def body(scalars_ref, spread_ref, out_ref):
        for tap in range(taps):
            for side in range(2):
                total = None
                for frame in range(TAPS_OUT):
                    block, spot = divmod(tap + frame + 1, TAPS_OUT)
                    row = ((block * 2 + side) * TAPS_OUT + spot) * outs
                    part = spread_ref[row : row + outs, frame * outs : (frame + 1) * outs]
                    total = part if total is None else total + part
                out_ref[tap, :, side * outs : (side + 1) * outs] = total.T

    shapes = [jax.ShapeDtypeStruct((taps, outs, 2 * outs), WIDE)]
    return one_step(body, scalars, (spread,), shapes)[0]


def packed_exchange(stream, joined, readout, gains, scalars):
    rows, width = stream.shape
    frames, outs = rows // 2, width // 32
    blocks = frames // TAPS_OUT
    mel_count, gain_count = readout.shape[1], gains.shape[0]

    def body(scalars_ref, stream_ref, joined_ref, readout_ref, gains_ref, out_ref, own_ref):
        first = pl.multiple_of(scalars_ref[16] * frames, 8)
        for lanes in range(width // 128):
            cut = pl.ds(lanes * 128, 128)
            beyond = pl.ds(width + lanes * 128, 128)
            own_ref[lanes] = (
                stream_ref[pl.ds(first, frames), cut] + joined_ref[pl.ds(first, frames), beyond]
            )
        out_ref[:, blocks:, :] = jnp.zeros((32, blocks, TAPS_OUT * outs), LOW)
        each = 128 // outs
        for frame in range(TAPS_OUT):
            for lanes in range(width // 128):
                part = own_ref[lanes, pl.ds(frame, blocks, stride=TAPS_OUT), :].astype(LOW)
                for spot in range(each):
                    piece = part[:, spot * outs : (spot + 1) * outs]
                    device = lanes * each + spot
                    out_ref[device, :blocks, frame * outs : (frame + 1) * outs] = piece
        for device in range(32):
            for side in range(2):
                row = device * outs + side * blocks
                piece = readout_ref[row : row + blocks, :].astype(LOW)
                out_ref[device, blocks:, side * 128 : side * 128 + mel_count] = piece
            piece = gains_ref[:, device * outs : (device + 1) * outs].astype(LOW)
            out_ref[device, blocks : blocks + gain_count, 96 : 96 + outs] = piece

    shapes = [jax.ShapeDtypeStruct((32, 2 * blocks, TAPS_OUT * outs), LOW)]
    scratch = [pltpu.VMEM((width // 128, frames, 128), WIDE)]
    return one_step(body, scalars, (stream, joined, readout, gains), shapes, scratch)[0]


def squares_of(items, scalars, extras=()):
    def body(scalars_ref, *refs):
        out_ref = refs[-1]
        out_ref[...] = refs[len(items)][...] if extras else jnp.zeros_like(out_ref)
        for ref in refs[: len(items)]:
            values = ref[...].astype(WIDE)
            values = values * values
            while values.ndim > 2:
                values = jnp.sum(values, 0)
            row = jnp.sum(values, 0, keepdims=True)
            width = row.shape[1]
            for start in range(0, width, 128):
                stop = min(start + 128, width)
                out_ref[0:1, : stop - start] += row[:, start:stop]

    shapes = [jax.ShapeDtypeStruct((8, 128), WIDE)]
    return one_step(body, scalars, (*items, *extras), shapes)[0]


def all_updates(totals, weights, scalars):
    rates, decays = weight_rates(), [DECAY_RATE] * 8 + [0.0]
    count = len(weights)

    steps = 8

    def split(item):
        return item.shape[-1] % (steps * 128) == 0

    def block(item):
        if not split(item):
            return pl.BlockSpec(item.shape, lambda j, s, n=item.ndim: (0,) * n)
        lead = item.ndim - 1
        shape = item.shape[:-1] + (item.shape[-1] // steps,)
        return pl.BlockSpec(shape, lambda j, s, n=lead: (0,) * n + (j,))

    def body(scalars_ref, totals_ref, *refs):
        ins, stats_ref, outs = refs[: 4 * count], refs[4 * count], refs[4 * count + 1 :]
        whole = jnp.sum(totals_ref[...].reshape(32, 8, 128), 0)
        squared, loss, frames = [
            jnp.sum(whole[row : row + 1], 1, keepdims=True) for row in range(3)
        ]
        norm = jnp.sqrt(squared) / frames
        factor = jnp.minimum(1.0, CLIP_LIMIT / norm) / frames

        def update(number):
            master, moment, square, grad = [
                ref[...].astype(WIDE) for ref in ins[4 * number : 4 * number + 4]
            ]
            scale = factor.reshape((1,) * grad.ndim)
            new = adamw(master, moment, square, scale * grad, rates[number], decays[number])
            for ref, item in zip(outs[3 * number : 3 * number + 3], new):
                ref[...] = item

        @pl.when(pl.program_id(0) == 0)
        def _():
            for row, item in enumerate((loss, frames, norm)):
                stats_ref[row : row + 1, :] = jnp.broadcast_to(item, (1, 128))
            for number, (master, *_) in enumerate(weights):
                if not split(master):
                    update(number)

        for number, (master, *_) in enumerate(weights):
            if split(master):
                update(number)

    stats_shape = jax.ShapeDtypeStruct((8, 128), WIDE)
    shapes, out_specs = [stats_shape], [pl.BlockSpec((8, 128), lambda j, s: (0, 0))]
    for master, *_ in weights:
        shapes += [jax.ShapeDtypeStruct(master.shape, WIDE)] * 3
        out_specs += [block(master)] * 3
    operands = (totals, *[item for weight in weights for item in weight])
    stats, *new = pl.pallas_call(
        body,
        grid_spec=pltpu.PrefetchScalarGridSpec(
            num_scalar_prefetch=1,
            grid=(steps,),
            in_specs=[block(item) for item in operands],
            out_specs=out_specs,
        ),
        out_shape=shapes,
        compiler_params=pltpu.CompilerParams(vmem_limit_bytes=60 * 2**20),
        cost_estimate=SHORT,
    )(scalars, *operands)
    return stats, new


def norm_parts(values):
    center = values - jnp.mean(values, -1, keepdims=True)
    spread = jnp.mean(center * center, -1, keepdims=True)
    return center * lax.rsqrt(spread + NORM_EPS)


def norm_back(values, gain_row, grads):
    center = values - jnp.mean(values, -1, keepdims=True)
    spread = jnp.mean(center * center, -1, keepdims=True)
    inverse = lax.rsqrt(spread + NORM_EPS)
    unit = center * inverse
    scaled = grads * gain_row
    back = inverse * (
        scaled
        - jnp.mean(scaled, -1, keepdims=True)
        - unit * jnp.mean(scaled * unit, -1, keepdims=True)
    )
    return back, grads * unit


def tp_forward(stream, normed, mats, gain_two, slopes, valid, scalars, beside=None):
    (joint_out, jo), (expand, ex), (reduce, re) = mats
    width = stream.shape[1]
    joint = piece_dot(normed, joint_out, jo, 64, 3, low=True)
    context = attend(joint, slopes, valid, width // HEADS)
    context = side_by_side(scalars[16], context)
    mixed = piece_dot(context, joint_out, jo + 192, 64, 1)
    if beside is not None:
        mixed, _ = tie((mixed, beside))
    middle, normed_two = norm_forward(stream, mixed, swap_core(mixed), gain_two, scalars, True)
    upper, hidden = piece_dot(normed_two, expand, ex, 64, 4, with_gelu=True)
    lowered = piece_dot(hidden, reduce, re, 128, 2)
    kept = (stream, normed, joint, context, middle, normed_two, upper, hidden)
    return middle, lowered, kept


tie = lax.optimization_barrier


class Share:
    def __init__(self, left, right, spot, by_y):
        y, x = spot
        self.left, self.right = left, right
        if by_y:
            self.hops = [swap_y, swap_x]
            passed, theirs = (y, 1 - x), ((1 - y, 1 - x), (1 - y, x))
        else:
            self.hops = [swap_x, swap_y]
            passed, theirs = (1 - y, x), ((1 - y, 1 - x), (y, 1 - x))
        numbers = [2 * row + column for row, column in (passed, (y, x), *theirs)]
        self.passed, self.own, *theirs = [number.astype(jnp.int32) for number in numbers]
        self.made = packed_tokens(left, right, jnp.stack(theirs))
        self.flying = self.total = self.beside = None
        self.turns = 0

    def send(self):
        if self.hops:
            self.flying = self.hops.pop(0)(self.made)
        else:
            self.flying = None
            self.total = lax.psum_scatter(
                self.made, "fsdp", scatter_dimension=0, axis_index_groups=Z_LINES, tiled=True
            )

    def land(self, landed):
        terms = (self.left, self.right, landed)
        if self.hops:
            self.made = outer_sum(*terms, self.passed[None], 0, LOW)
            self.kept = outer_sum(*terms, self.own[None], 1, WIDE)
        else:
            self.made = (self.kept + landed.astype(WIDE)).astype(LOW)


class Flow:
    def __init__(self):
        self.shares = []

    def add(self, values, *terms):
        added = [Share(*term) for term in terms]
        values, made = tie((values, [share.made for share in added]))
        for share, item in zip(added, made):
            share.made = item
            share.send()
        self.shares += added
        return (*values, *added)

    def turn(self, *values):
        flying = [share for share in self.shares if share.flying is not None]
        summed = [share for share in self.shares if share.total is not None]
        for share in summed:
            share.turns += 1
        summed = [share for share in summed if share.turns == 2]
        values, landed, totals = tie(
            (values, [share.flying for share in flying], [share.total for share in summed])
        )
        for share, item in zip(summed, totals):
            share.total = item
        for share, item in zip(flying, landed):
            share.land(item)
        for share in [share for share in flying if share.beside is not None]:
            if not share.hops:
                share.made = jnp.concatenate([share.made, share.beside.made], 1)
                share.beside.flying = None
                flying.remove(share.beside)
        values, made = tie((values, [share.made for share in flying]))
        for share, item in zip(flying, made):
            share.made = item
            share.send()
        return values


def own_rows(total, core):
    halves = total.reshape(2, total.shape[0] // 2, total.shape[1])
    mine, other = pick(halves, core), swap_core(pick(halves, 1 - core))
    return jnp.stack(in_order(core, mine, other))


def tp_backward(
    incoming, incoming_low, kept, mats, gain_one, gain_two, slopes, valid, spot, scalars, flow
):
    stream, normed, joint, context, middle, normed_two, upper, hidden = kept
    (joint_out, jo), (expand, ex), (reduce, re) = mats
    d_upper = piece_dot_back(incoming_low, reduce, re, 128, upper=upper)
    d_normed = piece_dot_back(d_upper, expand, ex, 64)
    incoming, d_upper, d_normed = flow.turn(incoming, d_upper, d_normed)
    d_normed, g_reduce, g_expand = flow.add(
        (d_normed,), (hidden, incoming_low, spot, False), (normed_two, d_upper, spot, True)
    )
    d_middle, _, d_middle_low, d_gain_two = norm_backward(
        d_normed, swap_core(d_normed), middle, gain_two, incoming, scalars
    )
    mine, other = piece_dot_back(d_middle_low, joint_out, jo + 192, 64, split=True)
    mine, other, d_middle, d_middle_low = flow.turn(mine, other, d_middle, d_middle_low)
    d_joint = attend_back(
        joint, mine, swap_core(other), slopes, valid, stream.shape[1] // HEADS
    )
    d_normed = piece_dot_back(d_joint, joint_out, jo, 64)
    d_joint, d_normed = flow.turn(d_joint, d_normed)
    d_normed, g_output, g_joint = flow.add(
        (d_normed,), (context, d_middle_low, spot, False), (normed, d_joint, spot, True)
    )
    g_joint.beside = g_output
    result = norm_backward(d_normed, swap_core(d_normed), stream, gain_one, d_middle, scalars)
    return result, (g_joint, g_expand, g_reduce), d_gain_two


def paired_shards(
    spectra,
    gaussian,
    flow_times,
    lengths,
    span_flags,
    phone_ids,
    input_master,
    input_moment,
    input_square,
    kernel_master,
    kernel_moment,
    kernel_square,
    joint_master,
    joint_moment,
    joint_square,
    output_master,
    output_moment,
    output_square,
    expand_master,
    expand_moment,
    expand_square,
    reduce_master,
    reduce_moment,
    reduce_square,
    bridge_master,
    bridge_moment,
    bridge_square,
    readout_master,
    readout_moment,
    readout_square,
    gains_master,
    gains_moment,
    gains_square,
):
    dp_index, fsdp_index = lax.axis_index("dp"), lax.axis_index("fsdp")
    y, x = dp_index // 2, dp_index % 2
    z, core = fsdp_index // 2, fsdp_index % 2
    spot = (y, x)
    corners = [2 * y + x, 2 * y + 1 - x, 2 * (1 - y) + x, 2 * (1 - y) + 1 - x]
    behind = [(z - hops) % 4 for hops in range(4)]
    in_place = jnp.stack([*range(16), core]).astype(jnp.int32)
    all_shifted = [4 * corner + line for corner in corners for line in behind]
    all_shifted = jnp.stack([*all_shifted, core]).astype(jnp.int32)
    both_shifted = [4 * corner + line for line in behind for corner in corners]
    both_shifted = jnp.stack([*both_shifted, core]).astype(jnp.int32)
    chip = 8 * y + 4 * x + z
    mel_count, frame_count = spectra.shape[1:]
    taps, outs, group = kernel_master.shape
    width = outs * 32
    blocks = frame_count // TAPS_OUT

    with jax.named_scope("features"):
        flags = span_flags[0].astype(WIDE)
        valid_own = (jnp.arange(frame_count) < lengths[0]).astype(WIDE)
        clean, noise = spectra[0].astype(WIDE), gaussian[0].astype(WIDE)
        time = flow_times[0]
        noisy = (1.0 - (1.0 - SIGMA_MIN) * time) * noise + time * clean
        shown = clean * (1.0 - flags[None, :])
        small = jnp.concatenate(
            [readout_master.astype(LOW), gains_master.astype(LOW).T], 1
        )
        small = jnp.pad(small, ((0, 0), (0, frame_count - small.shape[1])))
        packed = jnp.concatenate(
            [
                noisy.astype(LOW),
                shown.astype(LOW),
                phone_ids.astype(LOW),
                valid_own[None].astype(LOW),
                jnp.zeros((14, frame_count), LOW),
                small,
            ],
            0,
        )
        line = z_line(packed, z)
        beside, across = swap_x(line), swap_y(line)
        corner = swap_y(beside)
        whole = jnp.zeros((4,) + line.shape, LOW)
        for number, part in enumerate((line, beside, across, corner)):
            whole = lax.dynamic_update_index_in_dim(whole, part, corners[number], 0)
        whole = whole.reshape((16,) + packed.shape)
        whole = jnp.stack(in_order(core, whole, swap_core(whole)), 1)
        whole = whole.reshape((32,) + packed.shape)
        mels = whole[:, : 2 * mel_count]
        onehot = (whole[:, 2 * mel_count][:, None, :] == jnp.arange(VOCAB, dtype=LOW)[None, :, None]).astype(LOW)
        features = jnp.concatenate([mels, onehot], 1)
        valid_all = whole[:, 2 * mel_count + 1].astype(WIDE)
        small = whole[:, 2 * mel_count + 16 :].reshape(width, frame_count)
        readout_full = small[:, :mel_count]
        gains_full = small[:, mel_count : mel_count + 5].T.astype(WIDE)

    with jax.named_scope("weights"):
        layers, rows = joint_master.shape[:2]
        tiles = expand_master.shape[2] // (2 * 128 * 4)
        cut_joint = joint_master.astype(LOW).reshape(layers, rows, 3, 2, LANES)
        cut_output = output_master.astype(LOW).reshape(layers, rows, 1, 2, LANES)
        cut_expand = expand_master.astype(LOW).reshape(layers, rows, tiles, 4, 2, 128)
        cut_bridge = bridge_master.astype(LOW).reshape(2, rows, 2, LANES)

        def columns_of(which):
            joint = lax.dynamic_index_in_dim(cut_joint, which, 3, keepdims=False)
            out = lax.dynamic_index_in_dim(cut_output, which, 3, keepdims=False)
            expand = lax.dynamic_index_in_dim(cut_expand, which, 4, keepdims=False)
            expand = expand.reshape(layers, rows, tiles, LANES)
            bridge = lax.dynamic_index_in_dim(cut_bridge, which, 2, keepdims=False)
            blocks = jnp.concatenate([joint, out, expand], 2).transpose(0, 2, 1, 3)
            blocks = blocks.reshape(layers * (4 + tiles), rows, LANES)
            return jnp.concatenate([blocks, bridge], 0)

        mine, other = in_order(core, columns_of(core), swap_core(columns_of(1 - core)))
        blocks = layers * (4 + tiles)
        paired = jnp.stack([mine[:blocks], other[:blocks]], 1)
        paired = paired.reshape(layers, 4 + tiles, 2 * rows, LANES)
        bridge = jnp.concatenate([mine[blocks:], other[blocks:]], 0).reshape(-1, LANES)
        lowered = reduce_master.astype(LOW).reshape(layers, -1, 2, LANES)
        lowered = lowered.transpose(0, 2, 1, 3).reshape(layers, -1, LANES)

        def flat(item):
            return item.reshape(-1, LANES)

        def along_z(own):
            parts = [own]
            for _ in range(3):
                parts.append(shift_z(parts[-1], 1))
            return parts

        def by_permutes(own, after_line, after_square, x_first):
            line = jnp.concatenate(along_z(tie((own, after_line))[0]), 0)
            line = tie((line, after_square))[0]
            beside, across = swap_x(line), swap_y(line)
            corner = swap_y(beside) if x_first else swap_x(across)
            whole = jnp.concatenate([line, beside, across, corner], 0)
            return line, (beside, across), (whole.reshape((16,) + own.shape), all_shifted)

        same_core = [[half + 2 * i for i in range(16)] for half in range(2)]

        def in_background(*parts):
            own = jnp.concatenate(parts, 0)
            whole = lax.all_gather(own, BOTH, axis=0, axis_index_groups=same_core)
            return whole, in_place

        third = in_background(lowered[0], bridge, flat(paired[1, :4]))
        fourth = in_background(flat(paired[1, 4:]))
        first_line, first_square, first = by_permutes(flat(paired[0, :4]), line, line, True)
        last_own = tie((lowered[1], line))[0]
        beside, across = swap_x(last_own), swap_y(last_own)
        square = jnp.concatenate([last_own, beside, across, swap_y(beside)], 0)
        second_line, _, second = by_permutes(
            flat(paired[0, 4:]), first_line, first_square, False
        )
        last = along_z(tie((square, second_line))[0])
        fifth = (jnp.concatenate(last, 0).reshape((16,) + last_own.shape), both_shifted)
        mats_zero = ((first, 0), (second, 0), (third, 0))
        mats_one = ((third, lowered.shape[1] + bridge.shape[0]), (fourth, 0), (fifth, 0))
        bridge_mat = (third, lowered.shape[1])

    with jax.named_scope("embedding"):
        columns = input_master.astype(LOW)
        columns = jnp.concatenate(in_order(core, columns, swap_core(columns)), -1)
        start = jnp.einsum("nzv,zr->nvr", features, columns, preferred_element_type=WIDE)
        start = start * valid_all[:, :, None]
        padded = start.astype(LOW).reshape(32, blocks, TAPS_OUT, 2, outs)
        padded = padded.transpose(0, 1, 3, 2, 4).reshape(32, blocks, TAPS_OUT * group)
        padded = jnp.pad(padded, ((0, 0), (2, 2), (0, 0)))
        windows = jnp.concatenate([padded[:, i : i + blocks] for i in range(5)], -1)
        windows = windows.reshape(32 * blocks, 5 * TAPS_OUT * group)
        turned = jnp.pad(
            kernel_master.astype(LOW).transpose(0, 2, 1), ((TAPS_OUT, TAPS_OUT), (0, 0), (0, 0))
        )
        banded = jnp.stack([turned[7 - j : 47 - j] for j in range(TAPS_OUT)], 2)
        banded = banded.reshape(5, TAPS_OUT, 2, outs, TAPS_OUT * outs).transpose(0, 2, 1, 3, 4)
        banded = banded.reshape(5, TAPS_OUT * group, TAPS_OUT * outs)
        conv_out = banded_dot(windows, banded)
        strided = features.reshape(32, -1, blocks, TAPS_OUT).transpose(3, 1, 0, 2)
        strided = strided.reshape(TAPS_OUT, -1, 32 * blocks)
        valid_rows = valid_all.reshape(32 * blocks, TAPS_OUT)
        conv_out, strided, valid_rows = tie((conv_out, strided, valid_rows))
        start_own = lax.dynamic_slice_in_dim(start, core * outs, outs, 2)
        start_own = start_own.reshape(32 * blocks, TAPS_OUT * outs)
        embedded = start_own + jax.nn.gelu(conv_out)
        embedded = lax.all_to_all(embedded.astype(LOW), BOTH, 0, 0, tiled=True)
        embedded = embedded.reshape(32, frame_count, outs).transpose(1, 0, 2)
        embedded = embedded.reshape(frame_count, width)
        embedded = jnp.concatenate(in_order(core, embedded, swap_core(embedded)), 0)
        embedded = embedded.astype(WIDE)

    slopes = 2.0 ** (
        -8.0 * (jnp.arange(HEADS // 2) + core * (HEADS // 2) + 1.0).astype(WIDE) / HEADS
    )
    valid = lax.dynamic_slice_in_dim(valid_all, 2 * chip, 2, 0)[:, None, :]
    scalars = in_place
    gain = [gains_full[row : row + 1] for row in range(5)]

    with jax.named_scope("forward_layers"):
        embedded, normed = norm_forward(embedded, None, None, gain[0], scalars, False)
        middle, lowered, kept_zero = tp_forward(
            embedded, normed, mats_zero, gain[1], slopes, valid, scalars, last[2]
        )
        encoded = middle + (lowered + swap_core(lowered))
        joined = jnp.concatenate([encoded, embedded], -1).astype(LOW)
        joined, _ = tie((joined, last[3]))
        bridged = piece_dot(joined, *bridge_mat, 128, 1)
        bridged, normed = norm_forward(
            None, bridged, swap_core(bridged), gain[2], scalars, True
        )
        middle, lowered, kept_one = tp_forward(
            bridged, normed, mats_one, gain[3], slopes, valid, scalars
        )
        decoded = middle + (lowered + swap_core(lowered))

    with jax.named_scope("readout_loss"):
        last = pick(decoded.reshape(2, frame_count, width), core)
        final_low = (norm_parts(last) * gains_full[4]).astype(LOW)
        predict = jnp.dot(final_low, readout_full, preferred_element_type=WIDE)
        target = (clean - (1.0 - SIGMA_MIN) * noise).T
        weight = (flags * valid_own)[:, None]
        missed = predict - target
        loss_local = jnp.sum(weight * missed * missed)
        count_local = jnp.sum(weight)
        d_predict = (2.0 * weight * missed).astype(LOW)
        d_readout = lax.dot_general(
            final_low, d_predict, (((0,), (0,)), ((), ())), preferred_element_type=WIDE
        )
        d_final = lax.dot_general(
            d_predict, readout_full, (((1,), (1,)), ((), ())), preferred_element_type=WIDE
        )
        back, gain_terms = norm_back(last, gains_full[4], d_final)
        d_gain_last = jnp.sum(gain_terms, 0)
        d_decoded = jnp.concatenate(in_order(core, back, swap_core(back)), 0)

    with jax.named_scope("backward_layers"):
        flow = Flow()
        parts = (slopes, valid, spot, scalars, flow)
        result, shares_one, d_gain_three = tp_backward(
            d_decoded, d_decoded.astype(LOW), kept_one, mats_one, gain[2], gain[3], *parts
        )
        d_gain_two = result[3]
        d_joined = piece_dot_back(result[2], *bridge_mat, 128)
        d_joined, d_bridged_low = flow.turn(d_joined, result[2])
        d_joined, g_bridge = flow.add((d_joined,), (joined, d_bridged_low, spot, True))
        d_joined = d_joined + swap_core(d_joined)
        d_encoded = d_joined[:, :width]
        result, shares_zero, d_gain_one = tp_backward(
            d_encoded, d_encoded.astype(LOW), kept_zero, mats_zero, gain[0], gain[1], *parts
        )
        d_stream, d_gain_zero = result[0], result[3]

    with jax.named_scope("embedding_back"):
        d_gains = jnp.concatenate(
            [d_gain_zero, d_gain_one, d_gain_two, d_gain_three, d_gain_last[None]], 0
        )
        d_gains = jnp.pad(d_gains, ((0, 3), (0, 0)))
        both = packed_exchange(d_stream, d_joined, d_readout, d_gains, scalars)
        (both,) = flow.turn(both)
        (both,) = flow.turn(both)
        own_sent = both = both.reshape(64 * blocks, TAPS_OUT * outs)
        both = lax.all_to_all(both, BOTH, 0, 0, tiled=True)
        both, shares_zero[0].total = tie((both, shares_zero[0].total))
        both = both.reshape(32, 2 * blocks, TAPS_OUT * outs)
        own = both[:, :blocks].reshape(32 * blocks, TAPS_OUT * outs)
        mine, other, spread = banded_back(own, conv_out, windows, banded, scalars)
        grad_input = input_grad(own, mine, swap_core(other), valid_rows, strided, scalars)
        spread, small = tie((spread, both[:, blocks:]))
        grad_kernel = kernel_grad(spread, taps, outs, scalars)
        small = jnp.sum(small.astype(WIDE), 0)
        grad_readout = jnp.concatenate([small[:, :mel_count], small[:, 128 : 128 + mel_count]], 0)
        grad_gains = small[:5, 96 : 96 + outs]

    with jax.named_scope("own_grads"):
        shares = [*shares_zero, *shares_one, g_bridge]
        for share in shares:
            share.total = tie((share.total, own_sent))[0]

        def unfolded(both, count):
            cut = both.reshape(2, both.shape[1], count, both.shape[2] // count)
            return jnp.moveaxis(cut, 0, 2).reshape(both.shape[1], 2 * both.shape[2])

        layer_grads = []
        for joint_share, expand_share, reduce_share in (shares_zero, shares_one):
            both = own_rows(joint_share.total, core)
            layer_grads.append(
                (
                    unfolded(both[:, :, : 3 * LANES], 3),
                    unfolded(both[:, :, 3 * LANES :], 1),
                    unfolded(own_rows(expand_share.total, core), 4 * tiles),
                    reduce_share.total,
                )
            )
        grads = [
            grad_input,
            grad_kernel,
            *[jnp.stack(pair) for pair in zip(*layer_grads)],
            unfolded(own_rows(g_bridge.total, core), 1),
            grad_readout,
            grad_gains,
        ]

    with jax.named_scope("clip_and_update"):
        early = squares_of([share.total for share in shares[1:]], scalars)
        row = lax.broadcasted_iota(jnp.int32, (8, 128), 0)
        lane = lax.broadcasted_iota(jnp.int32, (8, 128), 1)
        told = jnp.where(row == 1, loss_local, jnp.where(row == 2, count_local, 0.0))
        early = early + jnp.where(lane == 0, told, 0.0)
        late = [shares[0].total, grad_input, grad_kernel, grad_readout, grad_gains]
        totals = squares_of(late, scalars, (early,))
        totals = jnp.broadcast_to(totals[None], (32, 8, 128)).reshape(256, 128)
        totals = lax.all_to_all(totals, BOTH, 0, 0, tiled=True)
        masters = (
            input_master.T,
            kernel_master,
            joint_master,
            output_master,
            expand_master,
            reduce_master,
            bridge_master,
            readout_master,
            gains_master,
        )
        moments = (
            input_moment.T,
            kernel_moment,
            joint_moment,
            output_moment,
            expand_moment,
            reduce_moment,
            bridge_moment,
            readout_moment,
            gains_moment,
        )
        squares = (
            input_square.T,
            kernel_square,
            joint_square,
            output_square,
            expand_square,
            reduce_square,
            bridge_square,
            readout_square,
            gains_square,
        )
        stats, results = all_updates(
            totals, list(zip(masters, moments, squares, grads)), scalars
        )
        results[:3] = [item.T for item in results[:3]]
        loss_sum, frame_total, grad_norm = stats[0, 0], stats[1, 0], stats[2, 0]
    return (loss_sum, frame_total, grad_norm, *results)


def solution(mesh):
    in_specs = (
        P(("dp", "fsdp"), None, None),
        P(("dp", "fsdp"), None, None),
        P(("dp", "fsdp")),
        P(("dp", "fsdp")),
        P(("dp", "fsdp"), None),
        P(("dp", "fsdp"), None),
        P(None, ("dp", "fsdp")),
        P(None, ("dp", "fsdp")),
        P(None, ("dp", "fsdp")),
        P(None, ("dp", "fsdp"), None),
        P(None, ("dp", "fsdp"), None),
        P(None, ("dp", "fsdp"), None),
        P(None, ("dp", "fsdp"), None),
        P(None, ("dp", "fsdp"), None),
        P(None, ("dp", "fsdp"), None),
        P(None, ("dp", "fsdp"), None),
        P(None, ("dp", "fsdp"), None),
        P(None, ("dp", "fsdp"), None),
        P(None, ("dp", "fsdp"), None),
        P(None, ("dp", "fsdp"), None),
        P(None, ("dp", "fsdp"), None),
        P(None, ("dp", "fsdp"), None),
        P(None, ("dp", "fsdp"), None),
        P(None, ("dp", "fsdp"), None),
        P(("dp", "fsdp"), None),
        P(("dp", "fsdp"), None),
        P(("dp", "fsdp"), None),
        P(("dp", "fsdp"), None),
        P(("dp", "fsdp"), None),
        P(("dp", "fsdp"), None),
        P(None, ("dp", "fsdp")),
        P(None, ("dp", "fsdp")),
        P(None, ("dp", "fsdp")),
    )
    out_specs = (
        P(),
        P(),
        P(),
        P(None, ("dp", "fsdp")),
        P(None, ("dp", "fsdp")),
        P(None, ("dp", "fsdp")),
        P(None, ("dp", "fsdp"), None),
        P(None, ("dp", "fsdp"), None),
        P(None, ("dp", "fsdp"), None),
        P(None, ("dp", "fsdp"), None),
        P(None, ("dp", "fsdp"), None),
        P(None, ("dp", "fsdp"), None),
        P(None, ("dp", "fsdp"), None),
        P(None, ("dp", "fsdp"), None),
        P(None, ("dp", "fsdp"), None),
        P(None, ("dp", "fsdp"), None),
        P(None, ("dp", "fsdp"), None),
        P(None, ("dp", "fsdp"), None),
        P(None, ("dp", "fsdp"), None),
        P(None, ("dp", "fsdp"), None),
        P(None, ("dp", "fsdp"), None),
        P(("dp", "fsdp"), None),
        P(("dp", "fsdp"), None),
        P(("dp", "fsdp"), None),
        P(("dp", "fsdp"), None),
        P(("dp", "fsdp"), None),
        P(("dp", "fsdp"), None),
        P(None, ("dp", "fsdp")),
        P(None, ("dp", "fsdp")),
        P(None, ("dp", "fsdp")),
    )
    paired = mesh.shape["dp"] == 4 and mesh.shape["fsdp"] == 8
    step = paired_shards if paired else shards
    return jax.shard_map(step, mesh=mesh, in_specs=in_specs, out_specs=out_specs, check_vma=False)
```

```python
import jax
import jax.numpy as jnp
from jax import lax
from jax.experimental import pallas as pl
from jax.experimental.pallas import tpu as pltpu
from jax.sharding import PartitionSpec as P

D = 1024
HEADS = 16
FF = 4096
MEL = 80
VOCAB = 96
KS = 31
GROUPS = 16
STEP = 10


SIGMA_MIN = 1e-05
NORM_EPS = 1e-05
MASKED = -1e30
BETA_ONE = 0.9
BETA_TWO = 0.95
ADAM_EPS = 1e-08
DECAY_RATE = 0.01
CLIP_LIMIT = 0.2
RATE_SCALE = 0.5
GAIN_RATE = 0.25


def layer_norm(values, gain_row):
    center = values - jnp.mean(values, -1, keepdims=True)
    spread = jnp.mean(center * center, -1, keepdims=True)
    return center * lax.rsqrt(spread + NORM_EPS) * gain_row


def alibi_bias(frames):
    slopes = 2.0 ** (-8.0 * (jnp.arange(HEADS, dtype=jnp.float32) + 1.0) / HEADS)
    places = jnp.arange(frames, dtype=jnp.float32)
    return -slopes[:, None, None] * jnp.abs(places[:, None] - places[None, :])


def conv_mix(hidden, kernel):
    tap_count = kernel.shape[0]
    margin = tap_count // 2
    seq_count, frame_count, model_width = hidden.shape
    per_group = model_width // GROUPS
    padded = jnp.pad(hidden, ((0, 0), (margin, margin), (0, 0)))
    stacked = jnp.stack([padded[:, tap : tap + frame_count] for tap in range(tap_count)], 1)
    stacked = stacked.reshape(seq_count, tap_count, frame_count, GROUPS, per_group)
    weights = kernel.reshape(tap_count, GROUPS, per_group, per_group)
    mixed = jnp.einsum("bklgc,kgoc->blgo", stacked, weights)
    return mixed.reshape(seq_count, frame_count, model_width)


def score_block(query, keyed, valid, alibi):
    scale = query.shape[-1] ** (-0.5)
    scores = (
        jnp.einsum("sqhd,skhd->shqk", query, keyed, preferred_element_type=jnp.float32) * scale
        + alibi[None]
    )
    return jnp.where(valid[:, None, None, :], scores, MASKED)


def layer_forward(stream, mats, gain_one, gain_two, valid, alibi):
    joint_w, output_w, expand_w, reduce_w = mats
    seq_count, frame_count, model_width = stream.shape
    row_count = seq_count * frame_count
    normed = layer_norm(stream, gain_one).astype(jnp.bfloat16).reshape(row_count, model_width)
    joint = jnp.dot(normed, joint_w, preferred_element_type=jnp.float32).astype(jnp.bfloat16)
    joint = joint.reshape(seq_count, frame_count, 3, HEADS, model_width // HEADS)
    scores = score_block(joint[:, :, 0], joint[:, :, 1], valid, alibi)
    highest = jnp.max(scores, -1, keepdims=True)
    raised = jnp.exp(scores - highest)
    totals = jnp.sum(raised, -1, keepdims=True)
    probs = raised / totals
    log_total = highest + jnp.log(totals)
    context = jnp.einsum(
        "shqk,skhd->sqhd",
        probs.astype(jnp.bfloat16),
        joint[:, :, 2],
        preferred_element_type=jnp.float32,
    )
    context = context.astype(jnp.bfloat16).reshape(row_count, model_width)
    middle = stream + jnp.dot(context, output_w, preferred_element_type=jnp.float32).reshape(
        stream.shape
    )
    normed_two = layer_norm(middle, gain_two).astype(jnp.bfloat16).reshape(row_count, model_width)
    upper = jnp.dot(normed_two, expand_w, preferred_element_type=jnp.float32)
    hidden = jax.nn.gelu(upper).astype(jnp.bfloat16)
    result = middle + jnp.dot(hidden, reduce_w, preferred_element_type=jnp.float32).reshape(
        stream.shape
    )
    return (result, (stream, normed, joint, log_total, context, middle, normed_two, upper, hidden))


def layer_backward(incoming, kept, mats, gain_one, gain_two, valid, alibi):
    stream, normed, joint, log_total, context, middle, normed_two, upper, hidden = kept
    joint_w, output_w, expand_w, reduce_w = mats
    seq_count, frame_count, model_width = stream.shape
    row_count = seq_count * frame_count
    incoming_low = incoming.reshape(row_count, model_width).astype(jnp.bfloat16)
    d_reduce = jnp.dot(hidden.T, incoming_low, preferred_element_type=jnp.float32)
    d_hidden = jnp.dot(incoming_low, reduce_w.T, preferred_element_type=jnp.float32)
    gelu_pull = jax.vjp(jax.nn.gelu, upper)[1]
    d_upper = gelu_pull(d_hidden)[0].astype(jnp.bfloat16)
    d_expand = jnp.dot(normed_two.T, d_upper, preferred_element_type=jnp.float32)
    d_normed = jnp.dot(d_upper, expand_w.T, preferred_element_type=jnp.float32).reshape(
        stream.shape
    )
    norm_pull = jax.vjp(layer_norm, middle, gain_two)[1]
    d_middle, d_gain_two = norm_pull(d_normed)
    d_middle = d_middle + incoming
    d_middle_low = d_middle.reshape(row_count, model_width).astype(jnp.bfloat16)
    d_output = jnp.dot(context.T, d_middle_low, preferred_element_type=jnp.float32)
    d_context = jnp.dot(d_middle_low, output_w.T, preferred_element_type=jnp.float32).astype(
        jnp.bfloat16
    )
    d_context = d_context.reshape(seq_count, frame_count, HEADS, model_width // HEADS)
    query, keyed, valued = (joint[:, :, 0], joint[:, :, 1], joint[:, :, 2])
    probs = jnp.exp(score_block(query, keyed, valid, alibi) - log_total)
    d_probs = jnp.einsum("sqhd,skhd->shqk", d_context, valued, preferred_element_type=jnp.float32)
    d_valued = jnp.einsum(
        "shqk,sqhd->skhd", probs.astype(jnp.bfloat16), d_context, preferred_element_type=jnp.float32
    )
    inner = jnp.sum(probs * d_probs, -1, keepdims=True)
    d_scores = (probs * (d_probs - inner)).astype(jnp.bfloat16)
    scale = query.shape[-1] ** (-0.5)
    d_query = (
        jnp.einsum("shqk,skhd->sqhd", d_scores, keyed, preferred_element_type=jnp.float32) * scale
    )
    d_keyed = (
        jnp.einsum("shqk,sqhd->skhd", d_scores, query, preferred_element_type=jnp.float32) * scale
    )
    d_joint = (
        jnp.stack([d_query, d_keyed, d_valued], 2)
        .astype(jnp.bfloat16)
        .reshape(row_count, 3 * model_width)
    )
    d_joint_w = jnp.dot(normed.T, d_joint, preferred_element_type=jnp.float32)
    d_normed = jnp.dot(d_joint, joint_w.T, preferred_element_type=jnp.float32).reshape(stream.shape)
    norm_pull = jax.vjp(layer_norm, stream, gain_one)[1]
    d_stream, d_gain_one = norm_pull(d_normed)
    return (d_stream + d_middle, (d_joint_w, d_output, d_expand, d_reduce), d_gain_one, d_gain_two)


def adamw(master, moment, square, grad, rate, decay):
    moment = BETA_ONE * moment + (1.0 - BETA_ONE) * grad
    square = BETA_TWO * square + (1.0 - BETA_TWO) * grad * grad
    fixed_moment = moment / (1.0 - BETA_ONE**STEP)
    fixed_square = square / (1.0 - BETA_TWO**STEP)
    return (
        moment,
        square,
        master - rate * (fixed_moment / (jnp.sqrt(fixed_square) + ADAM_EPS) + decay * master),
    )


def weight_rates():
    fan_ins = (MEL, KS * (D // GROUPS), D, D // 8, D, FF, 2 * D, D)
    return [RATE_SCALE * fan_in ** (-0.5) for fan_in in fan_ins] + [GAIN_RATE]


def shards(
    spectra,
    gaussian,
    flow_times,
    lengths,
    span_flags,
    phone_ids,
    input_master,
    input_moment,
    input_square,
    kernel_master,
    kernel_moment,
    kernel_square,
    joint_master,
    joint_moment,
    joint_square,
    output_master,
    output_moment,
    output_square,
    expand_master,
    expand_moment,
    expand_square,
    reduce_master,
    reduce_moment,
    reduce_square,
    bridge_master,
    bridge_moment,
    bridge_square,
    readout_master,
    readout_moment,
    readout_square,
    gains_master,
    gains_moment,
    gains_square,
):
    low_type = jnp.bfloat16
    wide_dtype = jnp.float32
    input_wide, kernel_full, bridge_full, readout_full, gains_full = (
        lax.all_gather(input_master.astype(low_type), ("dp", "fsdp"), axis=1, tiled=True),
        lax.all_gather(kernel_master.astype(low_type), ("dp", "fsdp"), axis=1, tiled=True),
        lax.all_gather(bridge_master.astype(low_type), ("dp", "fsdp"), axis=0, tiled=True),
        lax.all_gather(readout_master.astype(low_type), ("dp", "fsdp"), axis=0, tiled=True),
        lax.all_gather(gains_master.astype(low_type), ("dp", "fsdp"), axis=1, tiled=True),
    )
    gains_full = gains_full.astype(wide_dtype)

    def fetch(layer_index):
        return (
            lax.all_gather(
                joint_master[layer_index].astype(low_type), ("dp", "fsdp"), axis=0, tiled=True
            ),
            lax.all_gather(
                output_master[layer_index].astype(low_type), ("dp", "fsdp"), axis=0, tiled=True
            ),
            lax.all_gather(
                expand_master[layer_index].astype(low_type), ("dp", "fsdp"), axis=0, tiled=True
            ),
            lax.all_gather(
                reduce_master[layer_index].astype(low_type), ("dp", "fsdp"), axis=0, tiled=True
            ),
        )

    def share(grads):
        return (
            lax.psum_scatter(grads[0], ("dp", "fsdp"), scatter_dimension=0, tiled=True),
            lax.psum_scatter(grads[1], ("dp", "fsdp"), scatter_dimension=0, tiled=True),
            lax.psum_scatter(grads[2], ("dp", "fsdp"), scatter_dimension=0, tiled=True),
            lax.psum_scatter(grads[3], ("dp", "fsdp"), scatter_dimension=0, tiled=True),
        )

    seq_count, mel_count, frame_count = spectra.shape
    row_count = seq_count * frame_count
    valid = jnp.arange(frame_count)[None, :] < lengths[:, None]
    valid_float = valid.astype(wide_dtype)
    flags = span_flags.astype(wide_dtype)
    clean = spectra.astype(wide_dtype)
    noise_full = gaussian.astype(wide_dtype)
    scaled = flow_times[:, None, None]
    noisy = (1.0 - (1.0 - SIGMA_MIN) * scaled) * noise_full + scaled * clean
    context = clean * (1.0 - flags[:, None, :])
    onehot = (phone_ids[:, None, :] == jnp.arange(VOCAB)[None, :, None]).astype(low_type)
    feature_rows = jnp.concatenate([noisy.astype(low_type), context.astype(low_type), onehot], 1)
    initial_state = (
        jnp.einsum("nzv,zr->nvr", feature_rows, input_wide, preferred_element_type=wide_dtype)
        * valid_float[:, :, None]
    )
    conv_out, conv_pull = jax.vjp(
        conv_mix, initial_state.astype(low_type).astype(wide_dtype), kernel_full.astype(wide_dtype)
    )
    embedded = initial_state + jax.nn.gelu(conv_out)
    alibi = alibi_bias(frame_count)
    mats_zero = fetch(0)
    encoded, kept_zero = layer_forward(
        embedded, mats_zero, gains_full[0], gains_full[1], valid, alibi
    )
    model_width = encoded.shape[-1]
    joined = (
        jnp.concatenate([encoded, embedded], -1)
        .astype(low_type)
        .reshape(row_count, 2 * model_width)
    )
    bridged = jnp.dot(joined, bridge_full, preferred_element_type=wide_dtype).reshape(encoded.shape)
    mats_one = fetch(1)
    decoded, kept_one = layer_forward(bridged, mats_one, gains_full[2], gains_full[3], valid, alibi)
    final_low = layer_norm(decoded, gains_full[4]).astype(low_type).reshape(row_count, model_width)
    predict = jnp.dot(final_low, readout_full, preferred_element_type=wide_dtype)
    target = jnp.swapaxes(clean - (1.0 - SIGMA_MIN) * noise_full, 1, 2).reshape(
        row_count, mel_count
    )
    weight = (flags * valid_float).reshape(row_count, 1)
    missed = predict - target
    loss_local = jnp.sum(weight * missed * missed)
    count_local = jnp.sum(weight)
    loss_sum, frame_total = lax.psum((loss_local, count_local), ("dp", "fsdp"))
    d_predict = (2.0 * weight * missed).astype(low_type)
    d_readout = jnp.dot(final_low.T, d_predict, preferred_element_type=wide_dtype)
    d_final = jnp.dot(d_predict, readout_full.T, preferred_element_type=wide_dtype).reshape(
        decoded.shape
    )
    final_pull = jax.vjp(layer_norm, decoded, gains_full[4])[1]
    d_decoded, d_gain_last = final_pull(d_final)
    mats_back = mats_one
    d_bridged, grads_one, d_gain_two, d_gain_three = layer_backward(
        d_decoded, kept_one, mats_back, gains_full[2], gains_full[3], valid, alibi
    )
    shard_one = share(grads_one)
    d_bridged_low = d_bridged.reshape(row_count, model_width).astype(low_type)
    d_bridge = jnp.dot(joined.T, d_bridged_low, preferred_element_type=wide_dtype)
    d_joined = jnp.dot(d_bridged_low, bridge_full.T, preferred_element_type=wide_dtype).reshape(
        seq_count, frame_count, 2 * model_width
    )
    mats_back = mats_zero
    d_embedded, grads_zero, d_gain_zero, d_gain_one = layer_backward(
        d_joined[:, :, :model_width],
        kept_zero,
        mats_back,
        gains_full[0],
        gains_full[1],
        valid,
        alibi,
    )
    shard_zero = share(grads_zero)
    d_embedded = d_embedded + d_joined[:, :, model_width:]
    gelu_pull = jax.vjp(jax.nn.gelu, conv_out)[1]
    d_conv = gelu_pull(d_embedded)[0].astype(low_type).astype(wide_dtype)
    d_conv_in, d_kernel = conv_pull(d_conv)
    initial_gradient = ((d_embedded + d_conv_in) * valid_float[:, :, None]).astype(low_type)
    input_gradient = jnp.einsum(
        "fpk,fkq->pq", feature_rows, initial_gradient, preferred_element_type=wide_dtype
    )
    d_gains = jnp.stack([d_gain_zero, d_gain_one, d_gain_two, d_gain_three, d_gain_last])
    edge_input, edge_kernel, edge_bridge, edge_readout, edge_gains = (
        lax.psum_scatter(input_gradient, ("dp", "fsdp"), scatter_dimension=1, tiled=True),
        lax.psum_scatter(d_kernel, ("dp", "fsdp"), scatter_dimension=1, tiled=True),
        lax.psum_scatter(d_bridge, ("dp", "fsdp"), scatter_dimension=0, tiled=True),
        lax.psum_scatter(d_readout, ("dp", "fsdp"), scatter_dimension=0, tiled=True),
        lax.psum_scatter(d_gains, ("dp", "fsdp"), scatter_dimension=1, tiled=True),
    )
    layer_shards = [
        jnp.stack([zero_part, one_part]) for zero_part, one_part in zip(shard_zero, shard_one)
    ]
    grads = [edge_input, edge_kernel] + layer_shards + [edge_bridge, edge_readout, edge_gains]
    squares_local = sum((jnp.sum(item * item) for item in grads))
    squared = lax.psum(squares_local, ("dp", "fsdp"))
    grad_norm = jnp.sqrt(squared) / frame_total
    factor = jnp.minimum(1.0, CLIP_LIMIT / grad_norm) / frame_total
    masters = (
        input_master,
        kernel_master,
        joint_master,
        output_master,
        expand_master,
        reduce_master,
        bridge_master,
        readout_master,
        gains_master,
    )
    moments = (
        input_moment,
        kernel_moment,
        joint_moment,
        output_moment,
        expand_moment,
        reduce_moment,
        bridge_moment,
        readout_moment,
        gains_moment,
    )
    squares = (
        input_square,
        kernel_square,
        joint_square,
        output_square,
        expand_square,
        reduce_square,
        bridge_square,
        readout_square,
        gains_square,
    )
    decays = [DECAY_RATE] * 8 + [0.0]
    results = []
    for master, moment, square, grad, rate, decay in zip(
        masters, moments, squares, grads, weight_rates(), decays
    ):
        results.extend(adamw(master, moment, square, factor * grad, rate, decay))
    return (loss_sum, frame_total, grad_norm, *results)


LOW = jnp.bfloat16
WIDE = jnp.float32
BOTH = ("dp", "fsdp")
VMEM_GRANT = 24 * 2**20
GRANT = pltpu.CompilerParams(vmem_limit_bytes=VMEM_GRANT)
TAPS_OUT = 8
GELU_SCALE = 0.7978845608028654
SHORT = pl.CostEstimate(flops=1000, bytes_accessed=1000, transcendentals=0)
LANES = 512
Z_LINES = [[half + 2 * i for i in range(4)] for half in range(2)]


def swap_x(item):
    return lax.ppermute(item, "dp", [(i, i ^ 1) for i in range(4)])


def swap_y(item):
    return lax.ppermute(item, "dp", [(i, i ^ 2) for i in range(4)])


def swap_core(item):
    return lax.ppermute(item, "fsdp", [(i, i ^ 1) for i in range(8)])


def shift_z(item, hops):
    return lax.ppermute(item, "fsdp", [(i, (i + 2 * hops) % 8) for i in range(8)])


def pick(stacked, index):
    return lax.dynamic_index_in_dim(stacked, index, 0, keepdims=False)


def in_order(core, mine, other):
    first = core == 0
    return jnp.where(first, mine, other), jnp.where(first, other, mine)


def side_by_side(core, mine):
    return jnp.concatenate(in_order(core, mine, swap_core(mine)), -1)


def z_line(own, z):
    parts = [own] + [shift_z(own, hops) for hops in (1, 2, 3)]
    line = jnp.zeros((4,) + own.shape, own.dtype)
    for hops, part in enumerate(parts):
        line = lax.dynamic_update_index_in_dim(line, part, (z - hops) % 4, 0)
    return line


def laid_out(weights_ref, places_ref, whole_ref, part):
    for slot in range(16):
        start = pl.multiple_of(places_ref[slot] * part, 16)
        whole_ref[pl.ds(start, part), :] = weights_ref[slot]


def piece_dot(rows, weights, base, part, count, low=False, with_gelu=False):
    gathered, places = weights
    row_count, depth = rows.shape
    out_type = LOW if low else WIDE
    width = count * LANES

    def body(places_ref, rows_ref, weights_ref, *refs):
        whole_ref = refs[-1]
        laid_out(weights_ref, places_ref, whole_ref, part)
        total = jnp.dot(rows_ref[...], whole_ref[...], preferred_element_type=WIDE)
        refs[0][...] = total.astype(out_type)
        if with_gelu:
            refs[1][...] = jax.nn.gelu(total).astype(LOW)

    out_spec = pl.BlockSpec((row_count, LANES), lambda j, s: (0, j))
    shape = jax.ShapeDtypeStruct((row_count, width), out_type)
    low_shape = jax.ShapeDtypeStruct((row_count, width), LOW)
    return pl.pallas_call(
        body,
        grid_spec=pltpu.PrefetchScalarGridSpec(
            num_scalar_prefetch=1,
            grid=(count,),
            in_specs=[
                pl.BlockSpec((row_count, depth), lambda j, s: (0, 0)),
                pl.BlockSpec((16, part, LANES), lambda j, s: (0, j + base // part, 0)),
            ],
            out_specs=[out_spec, out_spec] if with_gelu else out_spec,
            scratch_shapes=[pltpu.VMEM((depth, LANES), LOW)],
        ),
        out_shape=[shape, low_shape] if with_gelu else shape,
        compiler_params=GRANT,
        cost_estimate=SHORT,
    )(places, rows, gathered)


def gelu_slope(values):
    cubic = 0.044715 * values * values
    bent = jnp.tanh(GELU_SCALE * values * (1.0 + cubic))
    return 0.5 * (1.0 + bent) + 0.5 * values * (1.0 - bent * bent) * GELU_SCALE * (
        1.0 + 3.0 * cubic
    )


def piece_dot_back(grads, weights, base, part, upper=None, split=False):
    gathered, places = weights
    row_count, width = grads.shape
    depth, steps = 16 * part, grads.shape[1] // LANES
    half = depth // 2

    def body(places_ref, grads_ref, weights_ref, *refs):
        total_ref, whole_ref = refs[-2:]
        laid_out(weights_ref, places_ref, whole_ref, part)
        product = lax.dot_general(
            grads_ref[...],
            whole_ref[...],
            (((1,), (1,)), ((), ())),
            preferred_element_type=WIDE,
        )

        @pl.when(pl.program_id(0) == 0)
        def _():
            total_ref[...] = product

        @pl.when(pl.program_id(0) > 0)
        def _():
            total_ref[...] += product

        @pl.when(pl.program_id(0) == steps - 1)
        def _():
            if upper is not None:
                refs[1][...] = (total_ref[...] * gelu_slope(refs[0][...])).astype(LOW)
            elif split:
                core = places_ref[16]
                refs[0][...] = total_ref[:, pl.ds(pl.multiple_of(core * half, 128), half)]
                refs[1][...] = total_ref[:, pl.ds(pl.multiple_of((1 - core) * half, 128), half)]
            else:
                refs[0][...] = total_ref[...]

    def fixed(shape):
        return pl.BlockSpec(shape, lambda j, s: (0, 0))

    if split:
        shapes = [jax.ShapeDtypeStruct((row_count, half), WIDE)] * 2
    else:
        shapes = [jax.ShapeDtypeStruct((row_count, depth), WIDE if upper is None else LOW)]
    extra = [] if upper is None else [upper]
    out = pl.pallas_call(
        body,
        grid_spec=pltpu.PrefetchScalarGridSpec(
            num_scalar_prefetch=1,
            grid=(steps,),
            in_specs=[
                pl.BlockSpec((row_count, LANES), lambda j, s: (0, j)),
                pl.BlockSpec((16, part, LANES), lambda j, s: (0, j + base // part, 0)),
            ]
            + [fixed(item.shape) for item in extra],
            out_specs=[fixed(item.shape) for item in shapes],
            scratch_shapes=[
                pltpu.VMEM((row_count, depth), WIDE),
                pltpu.VMEM((depth, LANES), LOW),
            ],
        ),
        out_shape=shapes,
        compiler_params=GRANT,
        cost_estimate=SHORT,
    )(places, grads, gathered, *extra)
    return out if split else out[0]


def whole_blocks(items):
    return [pl.BlockSpec(item.shape, lambda s, n=len(item.shape): (0,) * n) for item in items]


def one_step(body, scalars, operands, shapes, scratch=()):
    return pl.pallas_call(
        body,
        grid_spec=pltpu.PrefetchScalarGridSpec(
            num_scalar_prefetch=1,
            grid=(),
            in_specs=[pl.BlockSpec(memory_space=pltpu.VMEM)] * len(operands),
            out_specs=[pl.BlockSpec(memory_space=pltpu.VMEM)] * len(shapes),
            scratch_shapes=list(scratch),
        ),
        out_shape=shapes,
        compiler_params=GRANT,
        cost_estimate=SHORT,
    )(scalars, *operands)


def norm_forward(base, mine, other, gain, scalars, halves):
    addends = [] if mine is None else [mine, other]
    bases = [] if base is None else [base]
    rows = (mine if base is None else base).shape[0]
    width = gain.shape[1]
    half = width // 2

    def body(scalars_ref, *refs):
        gain_ref, stream_ref, normed_ref = refs[-3:]
        base_ref = None if base is None else refs[0]
        if mine is None:
            stream_ref[...] = base_ref[...]
        elif halves:
            mine_ref, other_ref = refs[len(bases) : len(bases) + 2]
            core = scalars_ref[16]
            for ref, side in ((mine_ref, core), (other_ref, 1 - core)):
                lanes = pl.ds(pl.multiple_of(side * half, 128), half)
                part = ref[...]
                stream_ref[:, lanes] = part if base is None else base_ref[:, lanes] + part
        else:
            mine_ref, other_ref = refs[len(bases) : len(bases) + 2]
            stream_ref[...] = base_ref[...] + (mine_ref[...] + other_ref[...])
        normed_ref[...] = (norm_parts(stream_ref[...]) * gain_ref[...]).astype(LOW)

    shapes = [jax.ShapeDtypeStruct((rows, width), WIDE), jax.ShapeDtypeStruct((rows, width), LOW)]
    return one_step(body, scalars, (*bases, *addends, gain), shapes)


def norm_backward(mine, other, values, gain, incoming, scalars):
    rows, width = values.shape
    half = width // 2

    def body(scalars_ref, mine_ref, other_ref, values_ref, gain_ref, incoming_ref, *refs):
        total_ref, low_ref, low_half_ref, row_ref, terms_ref = refs
        core = scalars_ref[16]
        back, terms = norm_back(values_ref[...], gain_ref[...], mine_ref[...] + other_ref[...])
        total = incoming_ref[...] + back
        total_ref[...] = total
        low_ref[...] = total.astype(LOW)
        low_half_ref[...] = low_ref[:, pl.ds(pl.multiple_of(core * half, 128), half)]
        terms_ref[...] = terms
        own = terms_ref[pl.ds(pl.multiple_of(core * (rows // 2), 8), rows // 2), :]
        row_ref[...] = jnp.sum(own, 0, keepdims=True)

    shapes = [
        jax.ShapeDtypeStruct((rows, width), WIDE),
        jax.ShapeDtypeStruct((rows, width), LOW),
        jax.ShapeDtypeStruct((rows, half), LOW),
        jax.ShapeDtypeStruct((1, width), WIDE),
    ]
    scratch = [pltpu.VMEM((rows, width), WIDE)]
    return one_step(
        body, scalars, (mine, other, values, gain, incoming), shapes, scratch
    )


def head_probs(joint_ref, head, size, slope, valid, distance):
    third = joint_ref.shape[1] // 3
    query = joint_ref[:, head * size : (head + 1) * size]
    keyed = joint_ref[:, third + head * size : third + (head + 1) * size]
    scores = lax.dot_general(
        query, keyed, (((1,), (1,)), ((), ())), preferred_element_type=WIDE
    )
    scores = jnp.where(valid, scores * size ** (-0.5) - slope * distance, MASKED)
    raised = jnp.exp(scores - jnp.max(scores, -1, keepdims=True))
    return query, keyed, raised / jnp.sum(raised, -1, keepdims=True)


def frame_distance(frames):
    ahead = lax.broadcasted_iota(jnp.int32, (frames, frames), 0)
    return jnp.abs(ahead - lax.broadcasted_iota(jnp.int32, (frames, frames), 1)).astype(WIDE)


def attend(joint, slopes, valid, size):
    rows, triple = joint.shape
    frames, third = rows // 2, triple // 3

    def body(slopes_ref, joint_ref, valid_ref, out_ref):
        distance = frame_distance(frames)
        mask = jnp.broadcast_to(valid_ref[0] > 0.5, (frames, frames))
        for head in range(third // size):
            _, _, probs = head_probs(joint_ref, head, size, slopes_ref[head], mask, distance)
            value = joint_ref[:, 2 * third + head * size : 2 * third + (head + 1) * size]
            mixed = jnp.dot(probs.astype(LOW), value, preferred_element_type=WIDE)
            out_ref[:, head * size : (head + 1) * size] = mixed.astype(LOW)

    return pl.pallas_call(
        body,
        grid_spec=pltpu.PrefetchScalarGridSpec(
            num_scalar_prefetch=1,
            grid=(2,),
            in_specs=[
                pl.BlockSpec((frames, triple), lambda u, s: (u, 0)),
                pl.BlockSpec((1, 1, frames), lambda u, s: (u, 0, 0)),
            ],
            out_specs=pl.BlockSpec((frames, third), lambda u, s: (u, 0)),
        ),
        out_shape=jax.ShapeDtypeStruct((rows, third), LOW),
        compiler_params=GRANT,
        cost_estimate=SHORT,
    )(slopes, joint, valid)


def attend_back(joint, mine, other, slopes, valid, size):
    rows, triple = joint.shape
    frames, third = rows // 2, triple // 3

    def body(slopes_ref, joint_ref, mine_ref, other_ref, valid_ref, out_ref):
        distance = frame_distance(frames)
        mask = jnp.broadcast_to(valid_ref[0] > 0.5, (frames, frames))
        scale = size ** (-0.5)
        for head in range(third // size):
            cut = slice(head * size, (head + 1) * size)
            query, keyed, probs = head_probs(
                joint_ref, head, size, slopes_ref[head], mask, distance
            )
            value = joint_ref[:, 2 * third + head * size : 2 * third + (head + 1) * size]
            grad = (mine_ref[:, cut] + other_ref[:, cut]).astype(LOW)
            d_probs = lax.dot_general(
                grad, value, (((1,), (1,)), ((), ())), preferred_element_type=WIDE
            )
            inner = jnp.sum(probs * d_probs, -1, keepdims=True)
            d_scores = (probs * (d_probs - inner)).astype(LOW)
            d_query = jnp.dot(d_scores, keyed, preferred_element_type=WIDE) * scale
            d_keyed = jnp.dot(d_scores.T, query, preferred_element_type=WIDE) * scale
            d_value = jnp.dot(probs.astype(LOW).T, grad, preferred_element_type=WIDE)
            for spot, item in enumerate((d_query, d_keyed, d_value)):
                start = spot * third + head * size
                out_ref[:, start : start + size] = item.astype(LOW)

    def utterance(width):
        return pl.BlockSpec((frames, width), lambda u, s: (u, 0))

    return pl.pallas_call(
        body,
        grid_spec=pltpu.PrefetchScalarGridSpec(
            num_scalar_prefetch=1,
            grid=(2,),
            in_specs=[
                utterance(triple),
                utterance(third),
                utterance(third),
                pl.BlockSpec((1, 1, frames), lambda u, s: (u, 0, 0)),
            ],
            out_specs=utterance(triple),
        ),
        out_shape=jax.ShapeDtypeStruct((rows, triple), LOW),
        compiler_params=GRANT,
        cost_estimate=SHORT,
    )(slopes, joint, mine, other, valid)


def packed_tokens(left, right, numbers):
    rows, depth = left.shape
    quarter, width = depth // 4, right.shape[1]

    def body(numbers_ref, left_ref, right_ref, out_ref):
        for spot in range(2):
            start = pl.multiple_of(numbers_ref[spot] * quarter, 128)
            out_ref[:, spot * quarter : (spot + 1) * quarter] = left_ref[:, pl.ds(start, quarter)]
        out_ref[:, 2 * quarter :] = right_ref[...]

    shapes = [jax.ShapeDtypeStruct((rows, 2 * quarter + width), LOW)]
    return one_step(body, numbers, (left, right), shapes)[0]


def outer_sum(left, right, got, number, second, out_type):
    rows, depth = left.shape
    quarter, width = depth // 4, right.shape[1]

    def body(number_ref, left_ref, right_ref, far_left_ref, far_right_ref, out_ref):
        dims = (((0,), (0,)), ((), ()))
        total = lax.dot_general(
            left_ref[...], right_ref[...], dims, preferred_element_type=WIDE
        )
        total = total + lax.dot_general(
            far_left_ref[...], far_right_ref[...], dims, preferred_element_type=WIDE
        )
        out_ref[...] = total.astype(out_type)

    return pl.pallas_call(
        body,
        grid_spec=pltpu.PrefetchScalarGridSpec(
            num_scalar_prefetch=1,
            grid=(width // LANES,),
            in_specs=[
                pl.BlockSpec((rows, quarter), lambda j, s: (0, s[0])),
                pl.BlockSpec((rows, LANES), lambda j, s: (0, j)),
                pl.BlockSpec((rows, quarter), lambda j, s: (0, second)),
                pl.BlockSpec((rows, LANES), lambda j, s: (0, j + 2 * quarter // LANES)),
            ],
            out_specs=pl.BlockSpec((quarter, LANES), lambda j, s: (0, j)),
        ),
        out_shape=jax.ShapeDtypeStruct((quarter, width), out_type),
        compiler_params=GRANT,
        cost_estimate=SHORT,
    )(number, left, right, got, got)


def banded_kernel(body, operands, blocks, out_block, shape, sums):
    def summed(*refs):
        if not sums:
            refs[-1][...] = body(*refs[:-1])
            return

        @pl.when(pl.program_id(0) == 0)
        def _():
            refs[-1][...] = jnp.zeros_like(refs[-1])

        refs[-1][...] += body(*refs[:-1])

    return pl.pallas_call(
        summed,
        grid=(5,),
        in_specs=blocks,
        out_specs=out_block,
        out_shape=jax.ShapeDtypeStruct(shape, WIDE),
        compiler_params=GRANT,
        cost_estimate=SHORT,
    )(*operands)


def banded_dot(windows, banded):
    rows, (_, depth, width) = windows.shape[0], banded.shape
    return banded_kernel(
        lambda left, right: jnp.dot(left[...], right[0], preferred_element_type=WIDE),
        (windows, banded),
        [
            pl.BlockSpec((rows, depth), lambda i: (0, i)),
            pl.BlockSpec((1, depth, width), lambda i: (i, 0, 0)),
        ],
        pl.BlockSpec((rows, width), lambda i: (0, 0)),
        (rows, width),
        True,
    )


def banded_back(own, conv_out, windows, banded, scalars):
    rows, width = own.shape
    count, depth, _ = banded.shape
    blocks = rows // 32
    half = depth // 2

    def body(scalars_ref, own_ref, conv_ref, windows_ref, banded_ref, *refs):
        mine_ref, other_ref, outer_ref, padded_ref, low_ref, total_ref = refs
        step = pl.program_id(0)

        @pl.when(step == 0)
        def _():
            grads = own_ref[...].astype(WIDE) * gelu_slope(conv_ref[...])
            low_ref[...] = grads.astype(LOW)
            padded_ref[...] = jnp.zeros_like(padded_ref)
            padded_ref[:, 8 : 8 + blocks, :] = low_ref[...].astype(WIDE).reshape(32, blocks, width)
            total_ref[...] = jnp.zeros_like(total_ref)

        for number in range(count):

            @pl.when(step == number)
            def _():
                shifted = padded_ref[:, 10 - number : 10 - number + blocks, :]
                total_ref[...] += lax.dot_general(
                    shifted.reshape(rows, width).astype(LOW),
                    banded_ref[0],
                    (((1,), (1,)), ((), ())),
                    preferred_element_type=WIDE,
                )

        outer_ref[...] = lax.dot_general(
            windows_ref[...], low_ref[...], (((0,), (0,)), ((), ())), preferred_element_type=WIDE
        )

        @pl.when(step == count - 1)
        def _():
            core = scalars_ref[16]
            mine_ref[...] = total_ref[:, pl.ds(pl.multiple_of(core * half, 128), half)]
            other_ref[...] = total_ref[:, pl.ds(pl.multiple_of((1 - core) * half, 128), half)]

    def fixed(shape):
        return pl.BlockSpec(shape, lambda i, s: (0, 0))

    return pl.pallas_call(
        body,
        grid_spec=pltpu.PrefetchScalarGridSpec(
            num_scalar_prefetch=1,
            grid=(count,),
            in_specs=[
                fixed((rows, width)),
                fixed((rows, width)),
                pl.BlockSpec((rows, depth), lambda i, s: (0, i)),
                pl.BlockSpec((1, depth, width), lambda i, s: (i, 0, 0)),
            ],
            out_specs=[
                fixed((rows, half)),
                fixed((rows, half)),
                pl.BlockSpec((depth, width), lambda i, s: (i, 0)),
            ],
            scratch_shapes=[
                pltpu.VMEM((32, blocks + 16, width), WIDE),
                pltpu.VMEM((rows, width), LOW),
                pltpu.VMEM((rows, depth), WIDE),
            ],
        ),
        out_shape=[
            jax.ShapeDtypeStruct((rows, half), WIDE),
            jax.ShapeDtypeStruct((rows, half), WIDE),
            jax.ShapeDtypeStruct((count * depth, width), WIDE),
        ],
        compiler_params=GRANT,
        cost_estimate=SHORT,
    )(scalars, own, conv_out, windows, banded)


def input_grad(own, mine, other, valid, strided, scalars):
    frames, channels, _ = strided.shape
    outs = own.shape[1] // frames

    def body(scalars_ref, own_ref, mine_ref, other_ref, valid_ref, strided_ref, out_ref):
        total = None
        grads = own_ref[...].astype(WIDE) + mine_ref[...] + other_ref[...]
        for frame in range(frames):
            part = grads[:, frame * outs : (frame + 1) * outs] * valid_ref[:, frame : frame + 1]
            product = jnp.dot(
                strided_ref[frame], part.astype(LOW), preferred_element_type=WIDE
            )
            total = product if total is None else total + product
        out_ref[...] = total.T

    shapes = [jax.ShapeDtypeStruct((outs, channels), WIDE)]
    return one_step(body, scalars, (own, mine, other, valid, strided), shapes)[0]


def kernel_grad(spread, taps, outs, scalars):
    count = spread.shape[0] // (2 * TAPS_OUT * outs)

    def body(scalars_ref, spread_ref, out_ref):
        for tap in range(taps):
            for side in range(2):
                total = None
                for frame in range(TAPS_OUT):
                    block, spot = divmod(tap + frame + 1, TAPS_OUT)
                    row = ((block * 2 + side) * TAPS_OUT + spot) * outs
                    part = spread_ref[row : row + outs, frame * outs : (frame + 1) * outs]
                    total = part if total is None else total + part
                out_ref[tap, :, side * outs : (side + 1) * outs] = total.T

    shapes = [jax.ShapeDtypeStruct((taps, outs, 2 * outs), WIDE)]
    return one_step(body, scalars, (spread,), shapes)[0]


def packed_exchange(stream, joined, readout, gains, scalars):
    rows, width = stream.shape
    frames, outs = rows // 2, width // 32
    blocks = frames // TAPS_OUT
    mel_count, gain_count = readout.shape[1], gains.shape[0]

    def body(scalars_ref, stream_ref, joined_ref, readout_ref, gains_ref, out_ref, own_ref):
        first = pl.multiple_of(scalars_ref[16] * frames, 8)
        for lanes in range(width // 128):
            cut = pl.ds(lanes * 128, 128)
            beyond = pl.ds(width + lanes * 128, 128)
            own_ref[lanes] = (
                stream_ref[pl.ds(first, frames), cut] + joined_ref[pl.ds(first, frames), beyond]
            )
        out_ref[:, blocks:, :] = jnp.zeros((32, blocks, TAPS_OUT * outs), LOW)
        each = 128 // outs
        for frame in range(TAPS_OUT):
            for lanes in range(width // 128):
                part = own_ref[lanes, pl.ds(frame, blocks, stride=TAPS_OUT), :].astype(LOW)
                for spot in range(each):
                    piece = part[:, spot * outs : (spot + 1) * outs]
                    device = lanes * each + spot
                    out_ref[device, :blocks, frame * outs : (frame + 1) * outs] = piece
        for device in range(32):
            for side in range(2):
                row = device * outs + side * blocks
                piece = readout_ref[row : row + blocks, :].astype(LOW)
                out_ref[device, blocks:, side * 128 : side * 128 + mel_count] = piece
            piece = gains_ref[:, device * outs : (device + 1) * outs].astype(LOW)
            out_ref[device, blocks : blocks + gain_count, 96 : 96 + outs] = piece

    shapes = [jax.ShapeDtypeStruct((32, 2 * blocks, TAPS_OUT * outs), LOW)]
    scratch = [pltpu.VMEM((width // 128, frames, 128), WIDE)]
    return one_step(body, scalars, (stream, joined, readout, gains), shapes, scratch)[0]


def squares_of(items, scalars, extras=()):
    def body(scalars_ref, *refs):
        out_ref = refs[-1]
        out_ref[...] = refs[len(items)][...] if extras else jnp.zeros_like(out_ref)
        for ref in refs[: len(items)]:
            values = ref[...].astype(WIDE)
            values = values * values
            while values.ndim > 2:
                values = jnp.sum(values, 0)
            row = jnp.sum(values, 0, keepdims=True)
            width = row.shape[1]
            for start in range(0, width, 128):
                stop = min(start + 128, width)
                out_ref[0:1, : stop - start] += row[:, start:stop]

    shapes = [jax.ShapeDtypeStruct((8, 128), WIDE)]
    return one_step(body, scalars, (*items, *extras), shapes)[0]


def all_updates(totals, weights, scalars):
    rates, decays = weight_rates(), [DECAY_RATE] * 8 + [0.0]
    count = len(weights)

    steps = 8

    def split(item):
        return item.shape[-1] % (steps * 128) == 0

    def block(item):
        if not split(item):
            return pl.BlockSpec(item.shape, lambda j, s, n=item.ndim: (0,) * n)
        lead = item.ndim - 1
        shape = item.shape[:-1] + (item.shape[-1] // steps,)
        return pl.BlockSpec(shape, lambda j, s, n=lead: (0,) * n + (j,))

    def body(scalars_ref, totals_ref, *refs):
        ins, stats_ref, outs = refs[: 4 * count], refs[4 * count], refs[4 * count + 1 :]
        whole = jnp.sum(totals_ref[...].reshape(32, 8, 128), 0)
        squared, loss, frames = [
            jnp.sum(whole[row : row + 1], 1, keepdims=True) for row in range(3)
        ]
        norm = jnp.sqrt(squared) / frames
        factor = jnp.minimum(1.0, CLIP_LIMIT / norm) / frames

        def update(number):
            master, moment, square, grad = [
                ref[...].astype(WIDE) for ref in ins[4 * number : 4 * number + 4]
            ]
            scale = factor.reshape((1,) * grad.ndim)
            grad = scale * grad
            moment = BETA_ONE * moment + (1.0 - BETA_ONE) * grad
            square = BETA_TWO * square + (1.0 - BETA_TWO) * grad * grad
            root = jnp.sqrt(square * (1.0 / (1.0 - BETA_TWO**STEP))) + ADAM_EPS
            step = moment * (1.0 / (1.0 - BETA_ONE**STEP)) / root
            new = (moment, square, master - rates[number] * (step + decays[number] * master))
            for ref, item in zip(outs[3 * number : 3 * number + 3], new):
                ref[...] = item

        @pl.when(pl.program_id(0) == 0)
        def _():
            for row, item in enumerate((loss, frames, norm)):
                stats_ref[row : row + 1, :] = jnp.broadcast_to(item, (1, 128))
            for number, (master, *_) in enumerate(weights):
                if not split(master):
                    update(number)

        for number, (master, *_) in enumerate(weights):
            if split(master):
                update(number)

    stats_shape = jax.ShapeDtypeStruct((8, 128), WIDE)
    shapes, out_specs = [stats_shape], [pl.BlockSpec((8, 128), lambda j, s: (0, 0))]
    for master, *_ in weights:
        shapes += [jax.ShapeDtypeStruct(master.shape, WIDE)] * 3
        out_specs += [block(master)] * 3
    operands = (totals, *[item for weight in weights for item in weight])
    stats, *new = pl.pallas_call(
        body,
        grid_spec=pltpu.PrefetchScalarGridSpec(
            num_scalar_prefetch=1,
            grid=(steps,),
            in_specs=[block(item) for item in operands],
            out_specs=out_specs,
        ),
        out_shape=shapes,
        compiler_params=pltpu.CompilerParams(vmem_limit_bytes=60 * 2**20),
        cost_estimate=SHORT,
    )(scalars, *operands)
    return stats, new


def norm_parts(values):
    center = values - jnp.mean(values, -1, keepdims=True)
    spread = jnp.mean(center * center, -1, keepdims=True)
    return center * lax.rsqrt(spread + NORM_EPS)


def norm_back(values, gain_row, grads):
    center = values - jnp.mean(values, -1, keepdims=True)
    spread = jnp.mean(center * center, -1, keepdims=True)
    inverse = lax.rsqrt(spread + NORM_EPS)
    unit = center * inverse
    scaled = grads * gain_row
    back = inverse * (
        scaled
        - jnp.mean(scaled, -1, keepdims=True)
        - unit * jnp.mean(scaled * unit, -1, keepdims=True)
    )
    return back, grads * unit


def tp_forward(stream, normed, mats, gain_two, slopes, valid, scalars, beside=None):
    (joint_out, jo), (expand, ex), (reduce, re) = mats
    width = stream.shape[1]
    joint = piece_dot(normed, joint_out, jo, 64, 3, low=True)
    context = attend(joint, slopes, valid, width // HEADS)
    context = side_by_side(scalars[16], context)
    mixed = piece_dot(context, joint_out, jo + 192, 64, 1)
    if beside is not None:
        mixed, _ = tie((mixed, beside))
    middle, normed_two = norm_forward(stream, mixed, swap_core(mixed), gain_two, scalars, True)
    upper, hidden = piece_dot(normed_two, expand, ex, 64, 4, with_gelu=True)
    lowered = piece_dot(hidden, reduce, re, 128, 2)
    kept = (stream, normed, joint, context, middle, normed_two, upper, hidden)
    return middle, lowered, kept


tie = lax.optimization_barrier


class Share:
    def __init__(self, left, right, spot, by_y):
        y, x = spot
        self.left, self.right = left, right
        if by_y:
            self.hops = [swap_y, swap_x]
            passed, theirs = (y, 1 - x), ((1 - y, 1 - x), (1 - y, x))
        else:
            self.hops = [swap_x, swap_y]
            passed, theirs = (1 - y, x), ((1 - y, 1 - x), (y, 1 - x))
        numbers = [2 * row + column for row, column in (passed, (y, x), *theirs)]
        self.passed, self.own, *theirs = [number.astype(jnp.int32) for number in numbers]
        self.made = packed_tokens(left, right, jnp.stack(theirs))
        self.flying = self.total = self.beside = None
        self.turns = 0

    def send(self):
        if self.hops:
            self.flying = self.hops.pop(0)(self.made)
        else:
            self.flying = None
            self.total = lax.psum_scatter(
                self.made, "fsdp", scatter_dimension=0, axis_index_groups=Z_LINES, tiled=True
            )

    def land(self, landed):
        terms = (self.left, self.right, landed)
        if self.hops:
            self.made = outer_sum(*terms, self.passed[None], 0, LOW)
            self.kept = outer_sum(*terms, self.own[None], 1, WIDE)
        else:
            self.made = (self.kept + landed.astype(WIDE)).astype(LOW)


class Flow:
    def __init__(self):
        self.shares = []

    def add(self, values, *terms):
        added = [Share(*term) for term in terms]
        values, made = tie((values, [share.made for share in added]))
        for share, item in zip(added, made):
            share.made = item
            share.send()
        self.shares += added
        return (*values, *added)

    def turn(self, *values):
        flying = [share for share in self.shares if share.flying is not None]
        summed = [share for share in self.shares if share.total is not None]
        for share in summed:
            share.turns += 1
        summed = [share for share in summed if share.turns == 2]
        values, landed, totals = tie(
            (values, [share.flying for share in flying], [share.total for share in summed])
        )
        for share, item in zip(summed, totals):
            share.total = item
        for share, item in zip(flying, landed):
            share.land(item)
        for share in [share for share in flying if share.beside is not None]:
            if not share.hops:
                share.made = jnp.concatenate([share.made, share.beside.made], 1)
                share.beside.flying = None
                flying.remove(share.beside)
        values, made = tie((values, [share.made for share in flying]))
        for share, item in zip(flying, made):
            share.made = item
            share.send()
        return values


def own_rows(total, core):
    halves = total.reshape(2, total.shape[0] // 2, total.shape[1])
    mine, other = pick(halves, core), swap_core(pick(halves, 1 - core))
    return jnp.stack(in_order(core, mine, other))


def tp_backward(
    incoming, incoming_low, kept, mats, gain_one, gain_two, slopes, valid, spot, scalars, flow
):
    stream, normed, joint, context, middle, normed_two, upper, hidden = kept
    (joint_out, jo), (expand, ex), (reduce, re) = mats
    d_upper = piece_dot_back(incoming_low, reduce, re, 128, upper=upper)
    d_normed = piece_dot_back(d_upper, expand, ex, 64)
    incoming, d_upper, d_normed = flow.turn(incoming, d_upper, d_normed)
    d_normed, g_reduce, g_expand = flow.add(
        (d_normed,), (hidden, incoming_low, spot, False), (normed_two, d_upper, spot, True)
    )
    d_middle, _, d_middle_low, d_gain_two = norm_backward(
        d_normed, swap_core(d_normed), middle, gain_two, incoming, scalars
    )
    mine, other = piece_dot_back(d_middle_low, joint_out, jo + 192, 64, split=True)
    mine, other, d_middle, d_middle_low = flow.turn(mine, other, d_middle, d_middle_low)
    d_joint = attend_back(
        joint, mine, swap_core(other), slopes, valid, stream.shape[1] // HEADS
    )
    d_normed = piece_dot_back(d_joint, joint_out, jo, 64)
    d_joint, d_normed = flow.turn(d_joint, d_normed)
    d_normed, g_output, g_joint = flow.add(
        (d_normed,), (context, d_middle_low, spot, False), (normed, d_joint, spot, True)
    )
    g_joint.beside = g_output
    result = norm_backward(d_normed, swap_core(d_normed), stream, gain_one, d_middle, scalars)
    return result, (g_joint, g_expand, g_reduce), d_gain_two


def paired_shards(
    spectra,
    gaussian,
    flow_times,
    lengths,
    span_flags,
    phone_ids,
    input_master,
    input_moment,
    input_square,
    kernel_master,
    kernel_moment,
    kernel_square,
    joint_master,
    joint_moment,
    joint_square,
    output_master,
    output_moment,
    output_square,
    expand_master,
    expand_moment,
    expand_square,
    reduce_master,
    reduce_moment,
    reduce_square,
    bridge_master,
    bridge_moment,
    bridge_square,
    readout_master,
    readout_moment,
    readout_square,
    gains_master,
    gains_moment,
    gains_square,
):
    dp_index, fsdp_index = lax.axis_index("dp"), lax.axis_index("fsdp")
    y, x = dp_index // 2, dp_index % 2
    z, core = fsdp_index // 2, fsdp_index % 2
    spot = (y, x)
    corners = [2 * y + x, 2 * y + 1 - x, 2 * (1 - y) + x, 2 * (1 - y) + 1 - x]
    behind = [(z - hops) % 4 for hops in range(4)]
    in_place = jnp.stack([*range(16), core]).astype(jnp.int32)
    all_shifted = [4 * corner + line for corner in corners for line in behind]
    all_shifted = jnp.stack([*all_shifted, core]).astype(jnp.int32)
    both_shifted = [4 * corner + line for line in behind for corner in corners]
    both_shifted = jnp.stack([*both_shifted, core]).astype(jnp.int32)
    chip = 8 * y + 4 * x + z
    mel_count, frame_count = spectra.shape[1:]
    taps, outs, group = kernel_master.shape
    width = outs * 32
    blocks = frame_count // TAPS_OUT

    with jax.named_scope("features"):
        flags = span_flags[0].astype(WIDE)
        valid_own = (jnp.arange(frame_count) < lengths[0]).astype(WIDE)
        clean, noise = spectra[0].astype(WIDE), gaussian[0].astype(WIDE)
        time = flow_times[0]
        noisy = (1.0 - (1.0 - SIGMA_MIN) * time) * noise + time * clean
        shown = clean * (1.0 - flags[None, :])
        small = jnp.concatenate(
            [readout_master.astype(LOW), gains_master.astype(LOW).T], 1
        )
        small = jnp.pad(small, ((0, 0), (0, frame_count - small.shape[1])))
        packed = jnp.concatenate(
            [
                noisy.astype(LOW),
                shown.astype(LOW),
                phone_ids.astype(LOW),
                valid_own[None].astype(LOW),
                jnp.zeros((14, frame_count), LOW),
                small,
            ],
            0,
        )
        line = z_line(packed, z)
        beside, across = swap_x(line), swap_y(line)
        corner = swap_y(beside)
        whole = jnp.zeros((4,) + line.shape, LOW)
        for number, part in enumerate((line, beside, across, corner)):
            whole = lax.dynamic_update_index_in_dim(whole, part, corners[number], 0)
        whole = whole.reshape((16,) + packed.shape)
        whole = jnp.stack(in_order(core, whole, swap_core(whole)), 1)
        whole = whole.reshape((32,) + packed.shape)
        mels = whole[:, : 2 * mel_count]
        onehot = (whole[:, 2 * mel_count][:, None, :] == jnp.arange(VOCAB, dtype=LOW)[None, :, None]).astype(LOW)
        features = jnp.concatenate([mels, onehot], 1)
        valid_all = whole[:, 2 * mel_count + 1].astype(WIDE)
        small = whole[:, 2 * mel_count + 16 :].reshape(width, frame_count)
        readout_full = small[:, :mel_count]
        gains_full = small[:, mel_count : mel_count + 5].T.astype(WIDE)

    with jax.named_scope("weights"):
        layers, rows = joint_master.shape[:2]
        tiles = expand_master.shape[2] // (2 * 128 * 4)
        cut_joint = joint_master.astype(LOW).reshape(layers, rows, 3, 2, LANES)
        cut_output = output_master.astype(LOW).reshape(layers, rows, 1, 2, LANES)
        cut_expand = expand_master.astype(LOW).reshape(layers, rows, tiles, 4, 2, 128)
        cut_bridge = bridge_master.astype(LOW).reshape(2, rows, 2, LANES)

        def columns_of(which):
            joint = lax.dynamic_index_in_dim(cut_joint, which, 3, keepdims=False)
            out = lax.dynamic_index_in_dim(cut_output, which, 3, keepdims=False)
            expand = lax.dynamic_index_in_dim(cut_expand, which, 4, keepdims=False)
            expand = expand.reshape(layers, rows, tiles, LANES)
            bridge = lax.dynamic_index_in_dim(cut_bridge, which, 2, keepdims=False)
            blocks = jnp.concatenate([joint, out, expand], 2).transpose(0, 2, 1, 3)
            blocks = blocks.reshape(layers * (4 + tiles), rows, LANES)
            return jnp.concatenate([blocks, bridge], 0)

        mine, other = in_order(core, columns_of(core), swap_core(columns_of(1 - core)))
        blocks = layers * (4 + tiles)
        paired = jnp.stack([mine[:blocks], other[:blocks]], 1)
        paired = paired.reshape(layers, 4 + tiles, 2 * rows, LANES)
        bridge = jnp.concatenate([mine[blocks:], other[blocks:]], 0).reshape(-1, LANES)
        lowered = reduce_master.astype(LOW).reshape(layers, -1, 2, LANES)
        lowered = lowered.transpose(0, 2, 1, 3).reshape(layers, -1, LANES)

        def flat(item):
            return item.reshape(-1, LANES)

        def along_z(own):
            parts = [own]
            for _ in range(3):
                parts.append(shift_z(parts[-1], 1))
            return parts

        def by_permutes(own, after_line, after_square, x_first):
            line = jnp.concatenate(along_z(tie((own, after_line))[0]), 0)
            line = tie((line, after_square))[0]
            beside, across = swap_x(line), swap_y(line)
            corner = swap_y(beside) if x_first else swap_x(across)
            whole = jnp.concatenate([line, beside, across, corner], 0)
            return line, (beside, across), (whole.reshape((16,) + own.shape), all_shifted)

        same_core = [[half + 2 * i for i in range(16)] for half in range(2)]

        def in_background(*parts):
            own = jnp.concatenate(parts, 0)
            whole = lax.all_gather(own, BOTH, axis=0, axis_index_groups=same_core)
            return whole, in_place

        third = in_background(lowered[0], bridge, flat(paired[1, :4]))
        fourth = in_background(lowered[1])
        first_line, first_square, first = by_permutes(flat(paired[0, :4]), line, line, True)
        last_own = tie((flat(paired[1, 4:]), line))[0]
        beside, across = swap_x(last_own), swap_y(last_own)
        square = jnp.concatenate([last_own, beside, across, swap_y(beside)], 0)
        second_line, _, second = by_permutes(
            flat(paired[0, 4:]), first_line, first_square, False
        )
        last = along_z(tie((square, second_line))[0])
        fifth = (jnp.concatenate(last, 0).reshape((16,) + last_own.shape), both_shifted)
        mats_zero = ((first, 0), (second, 0), (third, 0))
        mats_one = ((third, lowered.shape[1] + bridge.shape[0]), (fifth, 0), (fourth, 0))
        bridge_mat = (third, lowered.shape[1])

    with jax.named_scope("embedding"):
        columns = input_master.astype(LOW)
        columns = jnp.concatenate(in_order(core, columns, swap_core(columns)), -1)
        start = jnp.einsum("nzv,zr->nvr", features, columns, preferred_element_type=WIDE)
        start = start * valid_all[:, :, None]
        padded = start.astype(LOW).reshape(32, blocks, TAPS_OUT, 2, outs)
        padded = padded.transpose(0, 1, 3, 2, 4).reshape(32, blocks, TAPS_OUT * group)
        padded = jnp.pad(padded, ((0, 0), (2, 2), (0, 0)))
        windows = jnp.concatenate([padded[:, i : i + blocks] for i in range(5)], -1)
        windows = windows.reshape(32 * blocks, 5 * TAPS_OUT * group)
        turned = jnp.pad(
            kernel_master.astype(LOW).transpose(0, 2, 1), ((TAPS_OUT, TAPS_OUT), (0, 0), (0, 0))
        )
        banded = jnp.stack([turned[7 - j : 47 - j] for j in range(TAPS_OUT)], 2)
        banded = banded.reshape(5, TAPS_OUT, 2, outs, TAPS_OUT * outs).transpose(0, 2, 1, 3, 4)
        banded = banded.reshape(5, TAPS_OUT * group, TAPS_OUT * outs)
        conv_out = banded_dot(windows, banded)
        strided = features.reshape(32, -1, blocks, TAPS_OUT).transpose(3, 1, 0, 2)
        strided = strided.reshape(TAPS_OUT, -1, 32 * blocks)
        valid_rows = valid_all.reshape(32 * blocks, TAPS_OUT)
        conv_out, strided, valid_rows = tie((conv_out, strided, valid_rows))
        start_own = lax.dynamic_slice_in_dim(start, core * outs, outs, 2)
        start_own = start_own.reshape(32 * blocks, TAPS_OUT * outs)
        embedded = start_own + jax.nn.gelu(conv_out)
        embedded = lax.all_to_all(embedded.astype(LOW), BOTH, 0, 0, tiled=True)
        embedded = embedded.reshape(32, frame_count, outs).transpose(1, 0, 2)
        embedded = embedded.reshape(frame_count, width)
        embedded = jnp.concatenate(in_order(core, embedded, swap_core(embedded)), 0)
        embedded = embedded.astype(WIDE)

    slopes = 2.0 ** (
        -8.0 * (jnp.arange(HEADS // 2) + core * (HEADS // 2) + 1.0).astype(WIDE) / HEADS
    )
    valid = lax.dynamic_slice_in_dim(valid_all, 2 * chip, 2, 0)[:, None, :]
    scalars = in_place
    gain = [gains_full[row : row + 1] for row in range(5)]

    with jax.named_scope("forward_layers"):
        embedded, normed = norm_forward(embedded, None, None, gain[0], scalars, False)
        middle, lowered, kept_zero = tp_forward(
            embedded, normed, mats_zero, gain[1], slopes, valid, scalars, last[2]
        )
        encoded = middle + (lowered + swap_core(lowered))
        joined = jnp.concatenate([encoded, embedded], -1).astype(LOW)
        joined, _ = tie((joined, last[3]))
        bridged = piece_dot(joined, *bridge_mat, 128, 1)
        bridged, normed = norm_forward(
            None, bridged, swap_core(bridged), gain[2], scalars, True
        )
        middle, lowered, kept_one = tp_forward(
            bridged, normed, mats_one, gain[3], slopes, valid, scalars
        )
        decoded = middle + (lowered + swap_core(lowered))

    with jax.named_scope("readout_loss"):
        last = pick(decoded.reshape(2, frame_count, width), core)
        final_low = (norm_parts(last) * gains_full[4]).astype(LOW)
        predict = jnp.dot(final_low, readout_full, preferred_element_type=WIDE)
        target = (clean - (1.0 - SIGMA_MIN) * noise).T
        weight = (flags * valid_own)[:, None]
        missed = predict - target
        loss_local = jnp.sum(weight * missed * missed)
        count_local = jnp.sum(weight)
        d_predict = (2.0 * weight * missed).astype(LOW)
        d_readout = lax.dot_general(
            final_low, d_predict, (((0,), (0,)), ((), ())), preferred_element_type=WIDE
        )
        d_final = lax.dot_general(
            d_predict, readout_full, (((1,), (1,)), ((), ())), preferred_element_type=WIDE
        )
        back, gain_terms = norm_back(last, gains_full[4], d_final)
        d_gain_last = jnp.sum(gain_terms, 0)
        d_decoded = jnp.concatenate(in_order(core, back, swap_core(back)), 0)

    with jax.named_scope("backward_layers"):
        flow = Flow()
        parts = (slopes, valid, spot, scalars, flow)
        result, shares_one, d_gain_three = tp_backward(
            d_decoded, d_decoded.astype(LOW), kept_one, mats_one, gain[2], gain[3], *parts
        )
        d_gain_two = result[3]
        d_joined = piece_dot_back(result[2], *bridge_mat, 128)
        d_joined, d_bridged_low = flow.turn(d_joined, result[2])
        d_joined, g_bridge = flow.add((d_joined,), (joined, d_bridged_low, spot, True))
        d_joined = d_joined + swap_core(d_joined)
        d_encoded = d_joined[:, :width]
        result, shares_zero, d_gain_one = tp_backward(
            d_encoded, d_encoded.astype(LOW), kept_zero, mats_zero, gain[0], gain[1], *parts
        )
        d_stream, d_gain_zero = result[0], result[3]

    with jax.named_scope("embedding_back"):
        d_gains = jnp.concatenate(
            [d_gain_zero, d_gain_one, d_gain_two, d_gain_three, d_gain_last[None]], 0
        )
        d_gains = jnp.pad(d_gains, ((0, 3), (0, 0)))
        both = packed_exchange(d_stream, d_joined, d_readout, d_gains, scalars)
        (both,) = flow.turn(both)
        (both,) = flow.turn(both)
        own_sent = both = both.reshape(64 * blocks, TAPS_OUT * outs)
        both = lax.all_to_all(both, BOTH, 0, 0, tiled=True)
        both = both.reshape(32, 2 * blocks, TAPS_OUT * outs)
        own = both[:, :blocks].reshape(32 * blocks, TAPS_OUT * outs)
        mine, other, spread = banded_back(own, conv_out, windows, banded, scalars)
        small = tie((both[:, blocks:], mine))[0]
        grad_kernel = kernel_grad(spread, taps, outs, scalars)
        mine, other, grad_kernel, shares_zero[0].total = tie(
            (mine, other, grad_kernel, shares_zero[0].total)
        )
        grad_input = input_grad(own, mine, swap_core(other), valid_rows, strided, scalars)
        small = jnp.sum(small.astype(WIDE), 0)
        grad_readout = jnp.concatenate([small[:, :mel_count], small[:, 128 : 128 + mel_count]], 0)
        grad_gains = small[:5, 96 : 96 + outs]

    with jax.named_scope("own_grads"):
        shares = [*shares_zero, *shares_one, g_bridge]
        for share in shares:
            share.total = tie((share.total, own_sent))[0]

        def unfolded(both, count):
            cut = both.reshape(2, both.shape[1], count, both.shape[2] // count)
            return jnp.moveaxis(cut, 0, 2).reshape(both.shape[1], 2 * both.shape[2])

        layer_grads = []
        last_total = tie((shares_zero[0].total, grad_input))[0]
        for joint_share, expand_share, reduce_share in (shares_zero, shares_one):
            joint_total = last_total if joint_share is shares_zero[0] else joint_share.total
            both = own_rows(joint_total, core)
            layer_grads.append(
                (
                    unfolded(both[:, :, : 3 * LANES], 3),
                    unfolded(both[:, :, 3 * LANES :], 1),
                    unfolded(own_rows(expand_share.total, core), 4 * tiles),
                    reduce_share.total,
                )
            )
        grads = [
            grad_input,
            grad_kernel,
            *[jnp.stack(pair) for pair in zip(*layer_grads)],
            unfolded(own_rows(g_bridge.total, core), 1),
            grad_readout,
            grad_gains,
        ]

    with jax.named_scope("clip_and_update"):
        early = squares_of([share.total for share in shares[1:]], scalars)
        row = lax.broadcasted_iota(jnp.int32, (8, 128), 0)
        lane = lax.broadcasted_iota(jnp.int32, (8, 128), 1)
        told = jnp.where(row == 1, loss_local, jnp.where(row == 2, count_local, 0.0))
        early = early + jnp.where(lane == 0, told, 0.0)
        late = [shares[0].total, grad_input, grad_kernel, grad_readout, grad_gains]
        totals = squares_of(late, scalars, (early,))
        totals = jnp.broadcast_to(totals[None], (32, 8, 128)).reshape(256, 128)
        totals = lax.all_to_all(totals, BOTH, 0, 0, tiled=True)
        masters = (
            input_master.T,
            kernel_master,
            joint_master,
            output_master,
            expand_master,
            reduce_master,
            bridge_master,
            readout_master,
            gains_master,
        )
        moments = (
            input_moment.T,
            kernel_moment,
            joint_moment,
            output_moment,
            expand_moment,
            reduce_moment,
            bridge_moment,
            readout_moment,
            gains_moment,
        )
        squares = (
            input_square.T,
            kernel_square,
            joint_square,
            output_square,
            expand_square,
            reduce_square,
            bridge_square,
            readout_square,
            gains_square,
        )
        stats, results = all_updates(
            totals, list(zip(masters, moments, squares, grads)), scalars
        )
        results[:3] = [item.T for item in results[:3]]
        loss_sum, frame_total, grad_norm = stats[0, 0], stats[1, 0], stats[2, 0]
    return (loss_sum, frame_total, grad_norm, *results)


def solution(mesh):
    in_specs = (
        P(("dp", "fsdp"), None, None),
        P(("dp", "fsdp"), None, None),
        P(("dp", "fsdp")),
        P(("dp", "fsdp")),
        P(("dp", "fsdp"), None),
        P(("dp", "fsdp"), None),
        P(None, ("dp", "fsdp")),
        P(None, ("dp", "fsdp")),
        P(None, ("dp", "fsdp")),
        P(None, ("dp", "fsdp"), None),
        P(None, ("dp", "fsdp"), None),
        P(None, ("dp", "fsdp"), None),
        P(None, ("dp", "fsdp"), None),
        P(None, ("dp", "fsdp"), None),
        P(None, ("dp", "fsdp"), None),
        P(None, ("dp", "fsdp"), None),
        P(None, ("dp", "fsdp"), None),
        P(None, ("dp", "fsdp"), None),
        P(None, ("dp", "fsdp"), None),
        P(None, ("dp", "fsdp"), None),
        P(None, ("dp", "fsdp"), None),
        P(None, ("dp", "fsdp"), None),
        P(None, ("dp", "fsdp"), None),
        P(None, ("dp", "fsdp"), None),
        P(("dp", "fsdp"), None),
        P(("dp", "fsdp"), None),
        P(("dp", "fsdp"), None),
        P(("dp", "fsdp"), None),
        P(("dp", "fsdp"), None),
        P(("dp", "fsdp"), None),
        P(None, ("dp", "fsdp")),
        P(None, ("dp", "fsdp")),
        P(None, ("dp", "fsdp")),
    )
    out_specs = (
        P(),
        P(),
        P(),
        P(None, ("dp", "fsdp")),
        P(None, ("dp", "fsdp")),
        P(None, ("dp", "fsdp")),
        P(None, ("dp", "fsdp"), None),
        P(None, ("dp", "fsdp"), None),
        P(None, ("dp", "fsdp"), None),
        P(None, ("dp", "fsdp"), None),
        P(None, ("dp", "fsdp"), None),
        P(None, ("dp", "fsdp"), None),
        P(None, ("dp", "fsdp"), None),
        P(None, ("dp", "fsdp"), None),
        P(None, ("dp", "fsdp"), None),
        P(None, ("dp", "fsdp"), None),
        P(None, ("dp", "fsdp"), None),
        P(None, ("dp", "fsdp"), None),
        P(None, ("dp", "fsdp"), None),
        P(None, ("dp", "fsdp"), None),
        P(None, ("dp", "fsdp"), None),
        P(("dp", "fsdp"), None),
        P(("dp", "fsdp"), None),
        P(("dp", "fsdp"), None),
        P(("dp", "fsdp"), None),
        P(("dp", "fsdp"), None),
        P(("dp", "fsdp"), None),
        P(None, ("dp", "fsdp")),
        P(None, ("dp", "fsdp")),
        P(None, ("dp", "fsdp")),
    )
    paired = mesh.shape["dp"] == 4 and mesh.shape["fsdp"] == 8
    step = paired_shards if paired else shards
    return jax.shard_map(step, mesh=mesh, in_specs=in_specs, out_specs=out_specs, check_vma=False)
```

```python
import jax
import jax.numpy as jnp
from jax import lax
from jax.experimental import pallas as pl
from jax.experimental.pallas import tpu as pltpu
from jax.sharding import PartitionSpec as P

D = 1024
HEADS = 16
FF = 4096
MEL = 80
VOCAB = 96
KS = 31
GROUPS = 16
STEP = 10


SIGMA_MIN = 1e-05
NORM_EPS = 1e-05
MASKED = -1e30
BETA_ONE = 0.9
BETA_TWO = 0.95
ADAM_EPS = 1e-08
DECAY_RATE = 0.01
CLIP_LIMIT = 0.2
RATE_SCALE = 0.5
GAIN_RATE = 0.25


def layer_norm(values, gain_row):
    center = values - jnp.mean(values, -1, keepdims=True)
    spread = jnp.mean(center * center, -1, keepdims=True)
    return center * lax.rsqrt(spread + NORM_EPS) * gain_row


def alibi_bias(frames):
    slopes = 2.0 ** (-8.0 * (jnp.arange(HEADS, dtype=jnp.float32) + 1.0) / HEADS)
    places = jnp.arange(frames, dtype=jnp.float32)
    return -slopes[:, None, None] * jnp.abs(places[:, None] - places[None, :])


def conv_mix(hidden, kernel):
    tap_count = kernel.shape[0]
    margin = tap_count // 2
    seq_count, frame_count, model_width = hidden.shape
    per_group = model_width // GROUPS
    padded = jnp.pad(hidden, ((0, 0), (margin, margin), (0, 0)))
    stacked = jnp.stack([padded[:, tap : tap + frame_count] for tap in range(tap_count)], 1)
    stacked = stacked.reshape(seq_count, tap_count, frame_count, GROUPS, per_group)
    weights = kernel.reshape(tap_count, GROUPS, per_group, per_group)
    mixed = jnp.einsum("bklgc,kgoc->blgo", stacked, weights)
    return mixed.reshape(seq_count, frame_count, model_width)


def score_block(query, keyed, valid, alibi):
    scale = query.shape[-1] ** (-0.5)
    scores = (
        jnp.einsum("sqhd,skhd->shqk", query, keyed, preferred_element_type=jnp.float32) * scale
        + alibi[None]
    )
    return jnp.where(valid[:, None, None, :], scores, MASKED)


def layer_forward(stream, mats, gain_one, gain_two, valid, alibi):
    joint_w, output_w, expand_w, reduce_w = mats
    seq_count, frame_count, model_width = stream.shape
    row_count = seq_count * frame_count
    normed = layer_norm(stream, gain_one).astype(jnp.bfloat16).reshape(row_count, model_width)
    joint = jnp.dot(normed, joint_w, preferred_element_type=jnp.float32).astype(jnp.bfloat16)
    joint = joint.reshape(seq_count, frame_count, 3, HEADS, model_width // HEADS)
    scores = score_block(joint[:, :, 0], joint[:, :, 1], valid, alibi)
    highest = jnp.max(scores, -1, keepdims=True)
    raised = jnp.exp(scores - highest)
    totals = jnp.sum(raised, -1, keepdims=True)
    probs = raised / totals
    log_total = highest + jnp.log(totals)
    context = jnp.einsum(
        "shqk,skhd->sqhd",
        probs.astype(jnp.bfloat16),
        joint[:, :, 2],
        preferred_element_type=jnp.float32,
    )
    context = context.astype(jnp.bfloat16).reshape(row_count, model_width)
    middle = stream + jnp.dot(context, output_w, preferred_element_type=jnp.float32).reshape(
        stream.shape
    )
    normed_two = layer_norm(middle, gain_two).astype(jnp.bfloat16).reshape(row_count, model_width)
    upper = jnp.dot(normed_two, expand_w, preferred_element_type=jnp.float32)
    hidden = jax.nn.gelu(upper).astype(jnp.bfloat16)
    result = middle + jnp.dot(hidden, reduce_w, preferred_element_type=jnp.float32).reshape(
        stream.shape
    )
    return (result, (stream, normed, joint, log_total, context, middle, normed_two, upper, hidden))


def layer_backward(incoming, kept, mats, gain_one, gain_two, valid, alibi):
    stream, normed, joint, log_total, context, middle, normed_two, upper, hidden = kept
    joint_w, output_w, expand_w, reduce_w = mats
    seq_count, frame_count, model_width = stream.shape
    row_count = seq_count * frame_count
    incoming_low = incoming.reshape(row_count, model_width).astype(jnp.bfloat16)
    d_reduce = jnp.dot(hidden.T, incoming_low, preferred_element_type=jnp.float32)
    d_hidden = jnp.dot(incoming_low, reduce_w.T, preferred_element_type=jnp.float32)
    gelu_pull = jax.vjp(jax.nn.gelu, upper)[1]
    d_upper = gelu_pull(d_hidden)[0].astype(jnp.bfloat16)
    d_expand = jnp.dot(normed_two.T, d_upper, preferred_element_type=jnp.float32)
    d_normed = jnp.dot(d_upper, expand_w.T, preferred_element_type=jnp.float32).reshape(
        stream.shape
    )
    norm_pull = jax.vjp(layer_norm, middle, gain_two)[1]
    d_middle, d_gain_two = norm_pull(d_normed)
    d_middle = d_middle + incoming
    d_middle_low = d_middle.reshape(row_count, model_width).astype(jnp.bfloat16)
    d_output = jnp.dot(context.T, d_middle_low, preferred_element_type=jnp.float32)
    d_context = jnp.dot(d_middle_low, output_w.T, preferred_element_type=jnp.float32).astype(
        jnp.bfloat16
    )
    d_context = d_context.reshape(seq_count, frame_count, HEADS, model_width // HEADS)
    query, keyed, valued = (joint[:, :, 0], joint[:, :, 1], joint[:, :, 2])
    probs = jnp.exp(score_block(query, keyed, valid, alibi) - log_total)
    d_probs = jnp.einsum("sqhd,skhd->shqk", d_context, valued, preferred_element_type=jnp.float32)
    d_valued = jnp.einsum(
        "shqk,sqhd->skhd", probs.astype(jnp.bfloat16), d_context, preferred_element_type=jnp.float32
    )
    inner = jnp.sum(probs * d_probs, -1, keepdims=True)
    d_scores = (probs * (d_probs - inner)).astype(jnp.bfloat16)
    scale = query.shape[-1] ** (-0.5)
    d_query = (
        jnp.einsum("shqk,skhd->sqhd", d_scores, keyed, preferred_element_type=jnp.float32) * scale
    )
    d_keyed = (
        jnp.einsum("shqk,sqhd->skhd", d_scores, query, preferred_element_type=jnp.float32) * scale
    )
    d_joint = (
        jnp.stack([d_query, d_keyed, d_valued], 2)
        .astype(jnp.bfloat16)
        .reshape(row_count, 3 * model_width)
    )
    d_joint_w = jnp.dot(normed.T, d_joint, preferred_element_type=jnp.float32)
    d_normed = jnp.dot(d_joint, joint_w.T, preferred_element_type=jnp.float32).reshape(stream.shape)
    norm_pull = jax.vjp(layer_norm, stream, gain_one)[1]
    d_stream, d_gain_one = norm_pull(d_normed)
    return (d_stream + d_middle, (d_joint_w, d_output, d_expand, d_reduce), d_gain_one, d_gain_two)


def adamw(master, moment, square, grad, rate, decay):
    moment = BETA_ONE * moment + (1.0 - BETA_ONE) * grad
    square = BETA_TWO * square + (1.0 - BETA_TWO) * grad * grad
    fixed_moment = moment / (1.0 - BETA_ONE**STEP)
    fixed_square = square / (1.0 - BETA_TWO**STEP)
    return (
        moment,
        square,
        master - rate * (fixed_moment / (jnp.sqrt(fixed_square) + ADAM_EPS) + decay * master),
    )


def weight_rates():
    fan_ins = (MEL, KS * (D // GROUPS), D, D // 8, D, FF, 2 * D, D)
    return [RATE_SCALE * fan_in ** (-0.5) for fan_in in fan_ins] + [GAIN_RATE]


def shards(
    spectra,
    gaussian,
    flow_times,
    lengths,
    span_flags,
    phone_ids,
    input_master,
    input_moment,
    input_square,
    kernel_master,
    kernel_moment,
    kernel_square,
    joint_master,
    joint_moment,
    joint_square,
    output_master,
    output_moment,
    output_square,
    expand_master,
    expand_moment,
    expand_square,
    reduce_master,
    reduce_moment,
    reduce_square,
    bridge_master,
    bridge_moment,
    bridge_square,
    readout_master,
    readout_moment,
    readout_square,
    gains_master,
    gains_moment,
    gains_square,
):
    low_type = jnp.bfloat16
    wide_dtype = jnp.float32
    input_wide, kernel_full, bridge_full, readout_full, gains_full = (
        lax.all_gather(input_master.astype(low_type), ("dp", "fsdp"), axis=1, tiled=True),
        lax.all_gather(kernel_master.astype(low_type), ("dp", "fsdp"), axis=1, tiled=True),
        lax.all_gather(bridge_master.astype(low_type), ("dp", "fsdp"), axis=0, tiled=True),
        lax.all_gather(readout_master.astype(low_type), ("dp", "fsdp"), axis=0, tiled=True),
        lax.all_gather(gains_master.astype(low_type), ("dp", "fsdp"), axis=1, tiled=True),
    )
    gains_full = gains_full.astype(wide_dtype)

    def fetch(layer_index):
        return (
            lax.all_gather(
                joint_master[layer_index].astype(low_type), ("dp", "fsdp"), axis=0, tiled=True
            ),
            lax.all_gather(
                output_master[layer_index].astype(low_type), ("dp", "fsdp"), axis=0, tiled=True
            ),
            lax.all_gather(
                expand_master[layer_index].astype(low_type), ("dp", "fsdp"), axis=0, tiled=True
            ),
            lax.all_gather(
                reduce_master[layer_index].astype(low_type), ("dp", "fsdp"), axis=0, tiled=True
            ),
        )

    def share(grads):
        return (
            lax.psum_scatter(grads[0], ("dp", "fsdp"), scatter_dimension=0, tiled=True),
            lax.psum_scatter(grads[1], ("dp", "fsdp"), scatter_dimension=0, tiled=True),
            lax.psum_scatter(grads[2], ("dp", "fsdp"), scatter_dimension=0, tiled=True),
            lax.psum_scatter(grads[3], ("dp", "fsdp"), scatter_dimension=0, tiled=True),
        )

    seq_count, mel_count, frame_count = spectra.shape
    row_count = seq_count * frame_count
    valid = jnp.arange(frame_count)[None, :] < lengths[:, None]
    valid_float = valid.astype(wide_dtype)
    flags = span_flags.astype(wide_dtype)
    clean = spectra.astype(wide_dtype)
    noise_full = gaussian.astype(wide_dtype)
    scaled = flow_times[:, None, None]
    noisy = (1.0 - (1.0 - SIGMA_MIN) * scaled) * noise_full + scaled * clean
    context = clean * (1.0 - flags[:, None, :])
    onehot = (phone_ids[:, None, :] == jnp.arange(VOCAB)[None, :, None]).astype(low_type)
    feature_rows = jnp.concatenate([noisy.astype(low_type), context.astype(low_type), onehot], 1)
    initial_state = (
        jnp.einsum("nzv,zr->nvr", feature_rows, input_wide, preferred_element_type=wide_dtype)
        * valid_float[:, :, None]
    )
    conv_out, conv_pull = jax.vjp(
        conv_mix, initial_state.astype(low_type).astype(wide_dtype), kernel_full.astype(wide_dtype)
    )
    embedded = initial_state + jax.nn.gelu(conv_out)
    alibi = alibi_bias(frame_count)
    mats_zero = fetch(0)
    encoded, kept_zero = layer_forward(
        embedded, mats_zero, gains_full[0], gains_full[1], valid, alibi
    )
    model_width = encoded.shape[-1]
    joined = (
        jnp.concatenate([encoded, embedded], -1)
        .astype(low_type)
        .reshape(row_count, 2 * model_width)
    )
    bridged = jnp.dot(joined, bridge_full, preferred_element_type=wide_dtype).reshape(encoded.shape)
    mats_one = fetch(1)
    decoded, kept_one = layer_forward(bridged, mats_one, gains_full[2], gains_full[3], valid, alibi)
    final_low = layer_norm(decoded, gains_full[4]).astype(low_type).reshape(row_count, model_width)
    predict = jnp.dot(final_low, readout_full, preferred_element_type=wide_dtype)
    target = jnp.swapaxes(clean - (1.0 - SIGMA_MIN) * noise_full, 1, 2).reshape(
        row_count, mel_count
    )
    weight = (flags * valid_float).reshape(row_count, 1)
    missed = predict - target
    loss_local = jnp.sum(weight * missed * missed)
    count_local = jnp.sum(weight)
    loss_sum, frame_total = lax.psum((loss_local, count_local), ("dp", "fsdp"))
    d_predict = (2.0 * weight * missed).astype(low_type)
    d_readout = jnp.dot(final_low.T, d_predict, preferred_element_type=wide_dtype)
    d_final = jnp.dot(d_predict, readout_full.T, preferred_element_type=wide_dtype).reshape(
        decoded.shape
    )
    final_pull = jax.vjp(layer_norm, decoded, gains_full[4])[1]
    d_decoded, d_gain_last = final_pull(d_final)
    mats_back = mats_one
    d_bridged, grads_one, d_gain_two, d_gain_three = layer_backward(
        d_decoded, kept_one, mats_back, gains_full[2], gains_full[3], valid, alibi
    )
    shard_one = share(grads_one)
    d_bridged_low = d_bridged.reshape(row_count, model_width).astype(low_type)
    d_bridge = jnp.dot(joined.T, d_bridged_low, preferred_element_type=wide_dtype)
    d_joined = jnp.dot(d_bridged_low, bridge_full.T, preferred_element_type=wide_dtype).reshape(
        seq_count, frame_count, 2 * model_width
    )
    mats_back = mats_zero
    d_embedded, grads_zero, d_gain_zero, d_gain_one = layer_backward(
        d_joined[:, :, :model_width],
        kept_zero,
        mats_back,
        gains_full[0],
        gains_full[1],
        valid,
        alibi,
    )
    shard_zero = share(grads_zero)
    d_embedded = d_embedded + d_joined[:, :, model_width:]
    gelu_pull = jax.vjp(jax.nn.gelu, conv_out)[1]
    d_conv = gelu_pull(d_embedded)[0].astype(low_type).astype(wide_dtype)
    d_conv_in, d_kernel = conv_pull(d_conv)
    initial_gradient = ((d_embedded + d_conv_in) * valid_float[:, :, None]).astype(low_type)
    input_gradient = jnp.einsum(
        "fpk,fkq->pq", feature_rows, initial_gradient, preferred_element_type=wide_dtype
    )
    d_gains = jnp.stack([d_gain_zero, d_gain_one, d_gain_two, d_gain_three, d_gain_last])
    edge_input, edge_kernel, edge_bridge, edge_readout, edge_gains = (
        lax.psum_scatter(input_gradient, ("dp", "fsdp"), scatter_dimension=1, tiled=True),
        lax.psum_scatter(d_kernel, ("dp", "fsdp"), scatter_dimension=1, tiled=True),
        lax.psum_scatter(d_bridge, ("dp", "fsdp"), scatter_dimension=0, tiled=True),
        lax.psum_scatter(d_readout, ("dp", "fsdp"), scatter_dimension=0, tiled=True),
        lax.psum_scatter(d_gains, ("dp", "fsdp"), scatter_dimension=1, tiled=True),
    )
    layer_shards = [
        jnp.stack([zero_part, one_part]) for zero_part, one_part in zip(shard_zero, shard_one)
    ]
    grads = [edge_input, edge_kernel] + layer_shards + [edge_bridge, edge_readout, edge_gains]
    squares_local = sum((jnp.sum(item * item) for item in grads))
    squared = lax.psum(squares_local, ("dp", "fsdp"))
    grad_norm = jnp.sqrt(squared) / frame_total
    factor = jnp.minimum(1.0, CLIP_LIMIT / grad_norm) / frame_total
    masters = (
        input_master,
        kernel_master,
        joint_master,
        output_master,
        expand_master,
        reduce_master,
        bridge_master,
        readout_master,
        gains_master,
    )
    moments = (
        input_moment,
        kernel_moment,
        joint_moment,
        output_moment,
        expand_moment,
        reduce_moment,
        bridge_moment,
        readout_moment,
        gains_moment,
    )
    squares = (
        input_square,
        kernel_square,
        joint_square,
        output_square,
        expand_square,
        reduce_square,
        bridge_square,
        readout_square,
        gains_square,
    )
    decays = [DECAY_RATE] * 8 + [0.0]
    results = []
    for master, moment, square, grad, rate, decay in zip(
        masters, moments, squares, grads, weight_rates(), decays
    ):
        results.extend(adamw(master, moment, square, factor * grad, rate, decay))
    return (loss_sum, frame_total, grad_norm, *results)


LOW = jnp.bfloat16
WIDE = jnp.float32
BOTH = ("dp", "fsdp")
VMEM_GRANT = 24 * 2**20
GRANT = pltpu.CompilerParams(vmem_limit_bytes=VMEM_GRANT)
TAPS_OUT = 8
GELU_SCALE = 0.7978845608028654
SHORT = pl.CostEstimate(flops=1000, bytes_accessed=1000, transcendentals=0)
LANES = 512
Z_LINES = [[half + 2 * i for i in range(4)] for half in range(2)]


def swap_x(item):
    return lax.ppermute(item, "dp", [(i, i ^ 1) for i in range(4)])


def swap_y(item):
    return lax.ppermute(item, "dp", [(i, i ^ 2) for i in range(4)])


def swap_core(item):
    return lax.ppermute(item, "fsdp", [(i, i ^ 1) for i in range(8)])


def shift_z(item, hops):
    return lax.ppermute(item, "fsdp", [(i, (i + 2 * hops) % 8) for i in range(8)])


def pick(stacked, index):
    return lax.dynamic_index_in_dim(stacked, index, 0, keepdims=False)


def in_order(core, mine, other):
    first = core == 0
    return jnp.where(first, mine, other), jnp.where(first, other, mine)


def side_by_side(core, mine):
    return jnp.concatenate(in_order(core, mine, swap_core(mine)), -1)


def z_line(own, z):
    parts = [own] + [shift_z(own, hops) for hops in (1, 2, 3)]
    line = jnp.zeros((4,) + own.shape, own.dtype)
    for hops, part in enumerate(parts):
        line = lax.dynamic_update_index_in_dim(line, part, (z - hops) % 4, 0)
    return line


def laid_out(weights_ref, places_ref, whole_ref, part):
    for slot in range(16):
        start = pl.multiple_of(places_ref[slot] * part, 16)
        whole_ref[pl.ds(start, part), :] = weights_ref[slot]


def piece_dot(rows, weights, base, part, count, low=False, with_gelu=False):
    gathered, places = weights
    row_count, depth = rows.shape
    out_type = LOW if low else WIDE
    width = count * LANES

    def body(places_ref, rows_ref, weights_ref, *refs):
        whole_ref = refs[-1]
        laid_out(weights_ref, places_ref, whole_ref, part)
        total = jnp.dot(rows_ref[...], whole_ref[...], preferred_element_type=WIDE)
        refs[0][...] = total.astype(out_type)
        if with_gelu:
            refs[1][...] = jax.nn.gelu(total).astype(LOW)

    out_spec = pl.BlockSpec((row_count, LANES), lambda j, s: (0, j))
    shape = jax.ShapeDtypeStruct((row_count, width), out_type)
    low_shape = jax.ShapeDtypeStruct((row_count, width), LOW)
    return pl.pallas_call(
        body,
        grid_spec=pltpu.PrefetchScalarGridSpec(
            num_scalar_prefetch=1,
            grid=(count,),
            in_specs=[
                pl.BlockSpec((row_count, depth), lambda j, s: (0, 0)),
                pl.BlockSpec((16, part, LANES), lambda j, s: (0, j + base // part, 0)),
            ],
            out_specs=[out_spec, out_spec] if with_gelu else out_spec,
            scratch_shapes=[pltpu.VMEM((depth, LANES), LOW)],
        ),
        out_shape=[shape, low_shape] if with_gelu else shape,
        compiler_params=GRANT,
        cost_estimate=SHORT,
    )(places, rows, gathered)


def gelu_slope(values):
    cubic = 0.044715 * values * values
    bent = jnp.tanh(GELU_SCALE * values * (1.0 + cubic))
    return 0.5 * (1.0 + bent) + 0.5 * values * (1.0 - bent * bent) * GELU_SCALE * (
        1.0 + 3.0 * cubic
    )


def piece_dot_back(grads, weights, base, part, upper=None, split=False):
    gathered, places = weights
    row_count, width = grads.shape
    depth, steps = 16 * part, grads.shape[1] // LANES
    half = depth // 2

    def body(places_ref, grads_ref, weights_ref, *refs):
        total_ref, whole_ref = refs[-2:]
        laid_out(weights_ref, places_ref, whole_ref, part)
        product = lax.dot_general(
            grads_ref[...],
            whole_ref[...],
            (((1,), (1,)), ((), ())),
            preferred_element_type=WIDE,
        )

        @pl.when(pl.program_id(0) == 0)
        def _():
            total_ref[...] = product

        @pl.when(pl.program_id(0) > 0)
        def _():
            total_ref[...] += product

        @pl.when(pl.program_id(0) == steps - 1)
        def _():
            if upper is not None:
                refs[1][...] = (total_ref[...] * gelu_slope(refs[0][...])).astype(LOW)
            elif split:
                core = places_ref[16]
                refs[0][...] = total_ref[:, pl.ds(pl.multiple_of(core * half, 128), half)]
                refs[1][...] = total_ref[:, pl.ds(pl.multiple_of((1 - core) * half, 128), half)]
            else:
                refs[0][...] = total_ref[...]

    def fixed(shape):
        return pl.BlockSpec(shape, lambda j, s: (0, 0))

    if split:
        shapes = [jax.ShapeDtypeStruct((row_count, half), WIDE)] * 2
    else:
        shapes = [jax.ShapeDtypeStruct((row_count, depth), WIDE if upper is None else LOW)]
    extra = [] if upper is None else [upper]
    out = pl.pallas_call(
        body,
        grid_spec=pltpu.PrefetchScalarGridSpec(
            num_scalar_prefetch=1,
            grid=(steps,),
            in_specs=[
                pl.BlockSpec((row_count, LANES), lambda j, s: (0, j)),
                pl.BlockSpec((16, part, LANES), lambda j, s: (0, j + base // part, 0)),
            ]
            + [fixed(item.shape) for item in extra],
            out_specs=[fixed(item.shape) for item in shapes],
            scratch_shapes=[
                pltpu.VMEM((row_count, depth), WIDE),
                pltpu.VMEM((depth, LANES), LOW),
            ],
        ),
        out_shape=shapes,
        compiler_params=GRANT,
        cost_estimate=SHORT,
    )(places, grads, gathered, *extra)
    return out if split else out[0]


def whole_blocks(items):
    return [pl.BlockSpec(item.shape, lambda s, n=len(item.shape): (0,) * n) for item in items]


def one_step(body, scalars, operands, shapes, scratch=()):
    return pl.pallas_call(
        body,
        grid_spec=pltpu.PrefetchScalarGridSpec(
            num_scalar_prefetch=1,
            grid=(),
            in_specs=[pl.BlockSpec(memory_space=pltpu.VMEM)] * len(operands),
            out_specs=[pl.BlockSpec(memory_space=pltpu.VMEM)] * len(shapes),
            scratch_shapes=list(scratch),
        ),
        out_shape=shapes,
        compiler_params=GRANT,
        cost_estimate=SHORT,
    )(scalars, *operands)


def norm_forward(base, mine, other, gain, scalars, halves):
    addends = [] if mine is None else [mine, other]
    bases = [] if base is None else [base]
    rows = (mine if base is None else base).shape[0]
    width = gain.shape[1]
    half = width // 2

    def body(scalars_ref, *refs):
        gain_ref, stream_ref, normed_ref = refs[-3:]
        base_ref = None if base is None else refs[0]
        if mine is None:
            stream_ref[...] = base_ref[...]
        elif halves:
            mine_ref, other_ref = refs[len(bases) : len(bases) + 2]
            core = scalars_ref[16]
            for ref, side in ((mine_ref, core), (other_ref, 1 - core)):
                lanes = pl.ds(pl.multiple_of(side * half, 128), half)
                part = ref[...]
                stream_ref[:, lanes] = part if base is None else base_ref[:, lanes] + part
        else:
            mine_ref, other_ref = refs[len(bases) : len(bases) + 2]
            stream_ref[...] = base_ref[...] + (mine_ref[...] + other_ref[...])
        normed_ref[...] = (norm_parts(stream_ref[...]) * gain_ref[...]).astype(LOW)

    shapes = [jax.ShapeDtypeStruct((rows, width), WIDE), jax.ShapeDtypeStruct((rows, width), LOW)]
    return one_step(body, scalars, (*bases, *addends, gain), shapes)


def norm_backward(mine, other, values, gain, incoming, scalars):
    rows, width = values.shape
    half = width // 2

    def body(scalars_ref, mine_ref, other_ref, values_ref, gain_ref, incoming_ref, *refs):
        total_ref, low_ref, low_half_ref, row_ref, terms_ref = refs
        core = scalars_ref[16]
        back, terms = norm_back(values_ref[...], gain_ref[...], mine_ref[...] + other_ref[...])
        total = incoming_ref[...] + back
        total_ref[...] = total
        low_ref[...] = total.astype(LOW)
        low_half_ref[...] = low_ref[:, pl.ds(pl.multiple_of(core * half, 128), half)]
        terms_ref[...] = terms
        own = terms_ref[pl.ds(pl.multiple_of(core * (rows // 2), 8), rows // 2), :]
        row_ref[...] = jnp.sum(own, 0, keepdims=True)

    shapes = [
        jax.ShapeDtypeStruct((rows, width), WIDE),
        jax.ShapeDtypeStruct((rows, width), LOW),
        jax.ShapeDtypeStruct((rows, half), LOW),
        jax.ShapeDtypeStruct((1, width), WIDE),
    ]
    scratch = [pltpu.VMEM((rows, width), WIDE)]
    return one_step(
        body, scalars, (mine, other, values, gain, incoming), shapes, scratch
    )


def head_probs(joint_ref, head, size, slope, valid, distance):
    third = joint_ref.shape[1] // 3
    query = joint_ref[:, head * size : (head + 1) * size]
    keyed = joint_ref[:, third + head * size : third + (head + 1) * size]
    scores = lax.dot_general(
        query, keyed, (((1,), (1,)), ((), ())), preferred_element_type=WIDE
    )
    scores = jnp.where(valid, scores * size ** (-0.5) - slope * distance, MASKED)
    raised = jnp.exp(scores - jnp.max(scores, -1, keepdims=True))
    return query, keyed, raised / jnp.sum(raised, -1, keepdims=True)


def frame_distance(frames):
    ahead = lax.broadcasted_iota(jnp.int32, (frames, frames), 0)
    return jnp.abs(ahead - lax.broadcasted_iota(jnp.int32, (frames, frames), 1)).astype(WIDE)


def attend(joint, slopes, valid, size):
    rows, triple = joint.shape
    frames, third = rows // 2, triple // 3

    def body(slopes_ref, joint_ref, valid_ref, out_ref):
        distance = frame_distance(frames)
        mask = jnp.broadcast_to(valid_ref[0] > 0.5, (frames, frames))
        for head in range(third // size):
            _, _, probs = head_probs(joint_ref, head, size, slopes_ref[head], mask, distance)
            value = joint_ref[:, 2 * third + head * size : 2 * third + (head + 1) * size]
            mixed = jnp.dot(probs.astype(LOW), value, preferred_element_type=WIDE)
            out_ref[:, head * size : (head + 1) * size] = mixed.astype(LOW)

    return pl.pallas_call(
        body,
        grid_spec=pltpu.PrefetchScalarGridSpec(
            num_scalar_prefetch=1,
            grid=(2,),
            in_specs=[
                pl.BlockSpec((frames, triple), lambda u, s: (u, 0)),
                pl.BlockSpec((1, 1, frames), lambda u, s: (u, 0, 0)),
            ],
            out_specs=pl.BlockSpec((frames, third), lambda u, s: (u, 0)),
        ),
        out_shape=jax.ShapeDtypeStruct((rows, third), LOW),
        compiler_params=GRANT,
        cost_estimate=SHORT,
    )(slopes, joint, valid)


def attend_back(joint, mine, other, slopes, valid, size):
    rows, triple = joint.shape
    frames, third = rows // 2, triple // 3

    def body(slopes_ref, joint_ref, mine_ref, other_ref, valid_ref, out_ref):
        distance = frame_distance(frames)
        mask = jnp.broadcast_to(valid_ref[0] > 0.5, (frames, frames))
        scale = size ** (-0.5)
        for head in range(third // size):
            cut = slice(head * size, (head + 1) * size)
            query, keyed, probs = head_probs(
                joint_ref, head, size, slopes_ref[head], mask, distance
            )
            value = joint_ref[:, 2 * third + head * size : 2 * third + (head + 1) * size]
            grad = (mine_ref[:, cut] + other_ref[:, cut]).astype(LOW)
            d_probs = lax.dot_general(
                grad, value, (((1,), (1,)), ((), ())), preferred_element_type=WIDE
            )
            inner = jnp.sum(probs * d_probs, -1, keepdims=True)
            d_scores = (probs * (d_probs - inner)).astype(LOW)
            d_query = jnp.dot(d_scores, keyed, preferred_element_type=WIDE) * scale
            d_keyed = jnp.dot(d_scores.T, query, preferred_element_type=WIDE) * scale
            d_value = jnp.dot(probs.astype(LOW).T, grad, preferred_element_type=WIDE)
            for spot, item in enumerate((d_query, d_keyed, d_value)):
                start = spot * third + head * size
                out_ref[:, start : start + size] = item.astype(LOW)

    def utterance(width):
        return pl.BlockSpec((frames, width), lambda u, s: (u, 0))

    return pl.pallas_call(
        body,
        grid_spec=pltpu.PrefetchScalarGridSpec(
            num_scalar_prefetch=1,
            grid=(2,),
            in_specs=[
                utterance(triple),
                utterance(third),
                utterance(third),
                pl.BlockSpec((1, 1, frames), lambda u, s: (u, 0, 0)),
            ],
            out_specs=utterance(triple),
        ),
        out_shape=jax.ShapeDtypeStruct((rows, triple), LOW),
        compiler_params=GRANT,
        cost_estimate=SHORT,
    )(slopes, joint, mine, other, valid)


def packed_tokens(left, right, numbers):
    rows, depth = left.shape
    quarter, width = depth // 4, right.shape[1]

    def body(numbers_ref, left_ref, right_ref, out_ref):
        for spot in range(2):
            start = pl.multiple_of(numbers_ref[spot] * quarter, 128)
            out_ref[:, spot * quarter : (spot + 1) * quarter] = left_ref[:, pl.ds(start, quarter)]
        out_ref[:, 2 * quarter :] = right_ref[...]

    shapes = [jax.ShapeDtypeStruct((rows, 2 * quarter + width), LOW)]
    return one_step(body, numbers, (left, right), shapes)[0]


def outer_sum(left, right, got, number, second, out_type):
    rows, depth = left.shape
    quarter, width = depth // 4, right.shape[1]

    def body(number_ref, left_ref, right_ref, far_left_ref, far_right_ref, out_ref):
        dims = (((0,), (0,)), ((), ()))
        total = lax.dot_general(
            left_ref[...], right_ref[...], dims, preferred_element_type=WIDE
        )
        total = total + lax.dot_general(
            far_left_ref[...], far_right_ref[...], dims, preferred_element_type=WIDE
        )
        out_ref[...] = total.astype(out_type)

    return pl.pallas_call(
        body,
        grid_spec=pltpu.PrefetchScalarGridSpec(
            num_scalar_prefetch=1,
            grid=(width // LANES,),
            in_specs=[
                pl.BlockSpec((rows, quarter), lambda j, s: (0, s[0])),
                pl.BlockSpec((rows, LANES), lambda j, s: (0, j)),
                pl.BlockSpec((rows, quarter), lambda j, s: (0, second)),
                pl.BlockSpec((rows, LANES), lambda j, s: (0, j + 2 * quarter // LANES)),
            ],
            out_specs=pl.BlockSpec((quarter, LANES), lambda j, s: (0, j)),
        ),
        out_shape=jax.ShapeDtypeStruct((quarter, width), out_type),
        compiler_params=GRANT,
        cost_estimate=SHORT,
    )(number, left, right, got, got)


def banded_kernel(body, operands, blocks, out_block, shape, sums):
    def summed(*refs):
        if not sums:
            refs[-1][...] = body(*refs[:-1])
            return

        @pl.when(pl.program_id(0) == 0)
        def _():
            refs[-1][...] = jnp.zeros_like(refs[-1])

        refs[-1][...] += body(*refs[:-1])

    return pl.pallas_call(
        summed,
        grid=(5,),
        in_specs=blocks,
        out_specs=out_block,
        out_shape=jax.ShapeDtypeStruct(shape, WIDE),
        compiler_params=GRANT,
        cost_estimate=SHORT,
    )(*operands)


def banded_dot(windows, banded):
    rows, (_, depth, width) = windows.shape[0], banded.shape
    return banded_kernel(
        lambda left, right: jnp.dot(left[...], right[0], preferred_element_type=WIDE),
        (windows, banded),
        [
            pl.BlockSpec((rows, depth), lambda i: (0, i)),
            pl.BlockSpec((1, depth, width), lambda i: (i, 0, 0)),
        ],
        pl.BlockSpec((rows, width), lambda i: (0, 0)),
        (rows, width),
        True,
    )


def banded_back(own, conv_out, windows, banded, scalars):
    rows, width = own.shape
    count, depth, _ = banded.shape
    blocks = rows // 32
    half = depth // 2

    def body(scalars_ref, own_ref, conv_ref, windows_ref, banded_ref, *refs):
        mine_ref, other_ref, outer_ref, padded_ref, low_ref, total_ref = refs
        step = pl.program_id(0)

        @pl.when(step == 0)
        def _():
            grads = own_ref[...].astype(WIDE) * gelu_slope(conv_ref[...])
            low_ref[...] = grads.astype(LOW)
            padded_ref[...] = jnp.zeros_like(padded_ref)
            padded_ref[:, 8 : 8 + blocks, :] = low_ref[...].astype(WIDE).reshape(32, blocks, width)
            total_ref[...] = jnp.zeros_like(total_ref)

        for number in range(count):

            @pl.when(step == number)
            def _():
                shifted = padded_ref[:, 10 - number : 10 - number + blocks, :]
                total_ref[...] += lax.dot_general(
                    shifted.reshape(rows, width).astype(LOW),
                    banded_ref[0],
                    (((1,), (1,)), ((), ())),
                    preferred_element_type=WIDE,
                )

        outer_ref[...] = lax.dot_general(
            windows_ref[...], low_ref[...], (((0,), (0,)), ((), ())), preferred_element_type=WIDE
        )

        @pl.when(step == count - 1)
        def _():
            core = scalars_ref[16]
            mine_ref[...] = total_ref[:, pl.ds(pl.multiple_of(core * half, 128), half)]
            other_ref[...] = total_ref[:, pl.ds(pl.multiple_of((1 - core) * half, 128), half)]

    def fixed(shape):
        return pl.BlockSpec(shape, lambda i, s: (0, 0))

    return pl.pallas_call(
        body,
        grid_spec=pltpu.PrefetchScalarGridSpec(
            num_scalar_prefetch=1,
            grid=(count,),
            in_specs=[
                fixed((rows, width)),
                fixed((rows, width)),
                pl.BlockSpec((rows, depth), lambda i, s: (0, i)),
                pl.BlockSpec((1, depth, width), lambda i, s: (i, 0, 0)),
            ],
            out_specs=[
                fixed((rows, half)),
                fixed((rows, half)),
                pl.BlockSpec((depth, width), lambda i, s: (i, 0)),
            ],
            scratch_shapes=[
                pltpu.VMEM((32, blocks + 16, width), WIDE),
                pltpu.VMEM((rows, width), LOW),
                pltpu.VMEM((rows, depth), WIDE),
            ],
        ),
        out_shape=[
            jax.ShapeDtypeStruct((rows, half), WIDE),
            jax.ShapeDtypeStruct((rows, half), WIDE),
            jax.ShapeDtypeStruct((count * depth, width), WIDE),
        ],
        compiler_params=GRANT,
        cost_estimate=SHORT,
    )(scalars, own, conv_out, windows, banded)


def input_grad(own, mine, other, valid, strided, scalars):
    frames, channels, _ = strided.shape
    outs = own.shape[1] // frames

    def body(scalars_ref, own_ref, mine_ref, other_ref, valid_ref, strided_ref, out_ref):
        total = None
        grads = own_ref[...].astype(WIDE) + mine_ref[...] + other_ref[...]
        for frame in range(frames):
            part = grads[:, frame * outs : (frame + 1) * outs] * valid_ref[:, frame : frame + 1]
            product = jnp.dot(
                strided_ref[frame], part.astype(LOW), preferred_element_type=WIDE
            )
            total = product if total is None else total + product
        out_ref[...] = total.T

    shapes = [jax.ShapeDtypeStruct((outs, channels), WIDE)]
    return one_step(body, scalars, (own, mine, other, valid, strided), shapes)[0]


def kernel_grad(spread, taps, outs, scalars):
    count = spread.shape[0] // (2 * TAPS_OUT * outs)

    def body(scalars_ref, spread_ref, out_ref):
        for tap in range(taps):
            for side in range(2):
                total = None
                for frame in range(TAPS_OUT):
                    block, spot = divmod(tap + frame + 1, TAPS_OUT)
                    row = ((block * 2 + side) * TAPS_OUT + spot) * outs
                    part = spread_ref[row : row + outs, frame * outs : (frame + 1) * outs]
                    total = part if total is None else total + part
                out_ref[tap, :, side * outs : (side + 1) * outs] = total.T

    shapes = [jax.ShapeDtypeStruct((taps, outs, 2 * outs), WIDE)]
    return one_step(body, scalars, (spread,), shapes)[0]


def packed_exchange(stream, joined, readout, gains, scalars):
    rows, width = stream.shape
    frames, outs = rows // 2, width // 32
    blocks = frames // TAPS_OUT
    mel_count, gain_count = readout.shape[1], gains.shape[0]

    def body(scalars_ref, stream_ref, joined_ref, readout_ref, gains_ref, out_ref, own_ref):
        first = pl.multiple_of(scalars_ref[16] * frames, 8)
        for lanes in range(width // 128):
            cut = pl.ds(lanes * 128, 128)
            beyond = pl.ds(width + lanes * 128, 128)
            own_ref[lanes] = (
                stream_ref[pl.ds(first, frames), cut] + joined_ref[pl.ds(first, frames), beyond]
            )
        out_ref[:, blocks:, :] = jnp.zeros((32, blocks, TAPS_OUT * outs), LOW)
        each = 128 // outs
        for frame in range(TAPS_OUT):
            for lanes in range(width // 128):
                part = own_ref[lanes, pl.ds(frame, blocks, stride=TAPS_OUT), :].astype(LOW)
                for spot in range(each):
                    piece = part[:, spot * outs : (spot + 1) * outs]
                    device = lanes * each + spot
                    out_ref[device, :blocks, frame * outs : (frame + 1) * outs] = piece
        for device in range(32):
            for side in range(2):
                row = device * outs + side * blocks
                piece = readout_ref[row : row + blocks, :].astype(LOW)
                out_ref[device, blocks:, side * 128 : side * 128 + mel_count] = piece
            piece = gains_ref[:, device * outs : (device + 1) * outs].astype(LOW)
            out_ref[device, blocks : blocks + gain_count, 96 : 96 + outs] = piece

    shapes = [jax.ShapeDtypeStruct((32, 2 * blocks, TAPS_OUT * outs), LOW)]
    scratch = [pltpu.VMEM((width // 128, frames, 128), WIDE)]
    return one_step(body, scalars, (stream, joined, readout, gains), shapes, scratch)[0]


def squares_of(items, scalars, extras=()):
    def body(scalars_ref, *refs):
        out_ref = refs[-1]
        out_ref[...] = refs[len(items)][...] if extras else jnp.zeros_like(out_ref)
        for ref in refs[: len(items)]:
            values = ref[...].astype(WIDE)
            values = values * values
            while values.ndim > 2:
                values = jnp.sum(values, 0)
            row = jnp.sum(values, 0, keepdims=True)
            width = row.shape[1]
            for start in range(0, width, 128):
                stop = min(start + 128, width)
                out_ref[0:1, : stop - start] += row[:, start:stop]

    shapes = [jax.ShapeDtypeStruct((8, 128), WIDE)]
    return one_step(body, scalars, (*items, *extras), shapes)[0]


def all_updates(totals, weights, scalars):
    rates, decays = weight_rates(), [DECAY_RATE] * 8 + [0.0]
    count = len(weights)

    steps = 4

    def split(item):
        return item.shape[-1] % (steps * 128) == 0

    def block(item):
        if not split(item):
            return pl.BlockSpec(item.shape, lambda j, s, n=item.ndim: (0,) * n)
        lead = item.ndim - 1
        shape = item.shape[:-1] + (item.shape[-1] // steps,)
        return pl.BlockSpec(shape, lambda j, s, n=lead: (0,) * n + (j,))

    def body(scalars_ref, totals_ref, *refs):
        ins, stats_ref, outs = refs[: 4 * count], refs[4 * count], refs[4 * count + 1 :]
        whole = jnp.sum(totals_ref[...].reshape(32, 8, 128), 0)
        squared, loss, frames = [
            jnp.sum(whole[row : row + 1], 1, keepdims=True) for row in range(3)
        ]
        norm = jnp.sqrt(squared) / frames
        factor = jnp.minimum(1.0, CLIP_LIMIT / norm) / frames

        def update(number):
            master, moment, square, grad = [
                ref[...].astype(WIDE) for ref in ins[4 * number : 4 * number + 4]
            ]
            scale = factor.reshape((1,) * grad.ndim)
            grad = scale * grad
            moment = BETA_ONE * moment + (1.0 - BETA_ONE) * grad
            square = BETA_TWO * square + (1.0 - BETA_TWO) * grad * grad
            root = jnp.sqrt(square * (1.0 / (1.0 - BETA_TWO**STEP))) + ADAM_EPS
            step = moment * (1.0 / (1.0 - BETA_ONE**STEP)) / root
            new = (moment, square, master - rates[number] * (step + decays[number] * master))
            for ref, item in zip(outs[3 * number : 3 * number + 3], new):
                ref[...] = item

        @pl.when(pl.program_id(0) == 0)
        def _():
            for row, item in enumerate((loss, frames, norm)):
                stats_ref[row : row + 1, :] = jnp.broadcast_to(item, (1, 128))
            for number, (master, *_) in enumerate(weights):
                if not split(master):
                    update(number)

        for number, (master, *_) in enumerate(weights):
            if split(master):
                update(number)

    stats_shape = jax.ShapeDtypeStruct((8, 128), WIDE)
    shapes, out_specs = [stats_shape], [pl.BlockSpec((8, 128), lambda j, s: (0, 0))]
    for master, *_ in weights:
        shapes += [jax.ShapeDtypeStruct(master.shape, WIDE)] * 3
        out_specs += [block(master)] * 3
    operands = (totals, *[item for weight in weights for item in weight])
    stats, *new = pl.pallas_call(
        body,
        grid_spec=pltpu.PrefetchScalarGridSpec(
            num_scalar_prefetch=1,
            grid=(steps,),
            in_specs=[block(item) for item in operands],
            out_specs=out_specs,
        ),
        out_shape=shapes,
        compiler_params=pltpu.CompilerParams(vmem_limit_bytes=60 * 2**20),
        cost_estimate=SHORT,
    )(scalars, *operands)
    return stats, new


def norm_parts(values):
    center = values - jnp.mean(values, -1, keepdims=True)
    spread = jnp.mean(center * center, -1, keepdims=True)
    return center * lax.rsqrt(spread + NORM_EPS)


def norm_back(values, gain_row, grads):
    center = values - jnp.mean(values, -1, keepdims=True)
    spread = jnp.mean(center * center, -1, keepdims=True)
    inverse = lax.rsqrt(spread + NORM_EPS)
    unit = center * inverse
    scaled = grads * gain_row
    back = inverse * (
        scaled
        - jnp.mean(scaled, -1, keepdims=True)
        - unit * jnp.mean(scaled * unit, -1, keepdims=True)
    )
    return back, grads * unit


def tp_forward(stream, normed, mats, gain_two, slopes, valid, scalars, beside=None):
    (joint_out, jo), (expand, ex), (reduce, re) = mats
    width = stream.shape[1]
    joint = piece_dot(normed, joint_out, jo, 64, 3, low=True)
    context = attend(joint, slopes, valid, width // HEADS)
    context = side_by_side(scalars[16], context)
    mixed = piece_dot(context, joint_out, jo + 192, 64, 1)
    if beside is not None:
        mixed, _ = tie((mixed, beside))
    middle, normed_two = norm_forward(stream, mixed, swap_core(mixed), gain_two, scalars, True)
    upper, hidden = piece_dot(normed_two, expand, ex, 64, 4, with_gelu=True)
    lowered = piece_dot(hidden, reduce, re, 128, 2)
    kept = (stream, normed, joint, context, middle, normed_two, upper, hidden)
    return middle, lowered, kept


tie = lax.optimization_barrier


class Share:
    def __init__(self, left, right, spot, by_y):
        y, x = spot
        self.left, self.right = left, right
        if by_y:
            self.hops = [swap_y, swap_x]
            passed, theirs = (y, 1 - x), ((1 - y, 1 - x), (1 - y, x))
        else:
            self.hops = [swap_x, swap_y]
            passed, theirs = (1 - y, x), ((1 - y, 1 - x), (y, 1 - x))
        numbers = [2 * row + column for row, column in (passed, (y, x), *theirs)]
        self.passed, self.own, *theirs = [number.astype(jnp.int32) for number in numbers]
        self.made = packed_tokens(left, right, jnp.stack(theirs))
        self.flying = self.total = self.beside = None
        self.turns = 0

    def send(self):
        if self.hops:
            self.flying = self.hops.pop(0)(self.made)
        else:
            self.flying = None
            self.total = lax.psum_scatter(
                self.made, "fsdp", scatter_dimension=0, axis_index_groups=Z_LINES, tiled=True
            )

    def land(self, landed):
        terms = (self.left, self.right, landed)
        if self.hops:
            self.made = outer_sum(*terms, self.passed[None], 0, LOW)
            self.kept = outer_sum(*terms, self.own[None], 1, WIDE)
        else:
            self.made = (self.kept + landed.astype(WIDE)).astype(LOW)


class Flow:
    def __init__(self):
        self.shares = []

    def add(self, values, *terms):
        added = [Share(*term) for term in terms]
        values, made = tie((values, [share.made for share in added]))
        for share, item in zip(added, made):
            share.made = item
            share.send()
        self.shares += added
        return (*values, *added)

    def turn(self, *values):
        flying = [share for share in self.shares if share.flying is not None]
        summed = [share for share in self.shares if share.total is not None]
        for share in summed:
            share.turns += 1
        summed = [share for share in summed if share.turns == 2]
        values, landed, totals = tie(
            (values, [share.flying for share in flying], [share.total for share in summed])
        )
        for share, item in zip(summed, totals):
            share.total = item
        for share, item in zip(flying, landed):
            share.land(item)
        for share in [share for share in flying if share.beside is not None]:
            if not share.hops:
                share.made = jnp.concatenate([share.made, share.beside.made], 1)
                share.beside.flying = None
                flying.remove(share.beside)
        values, made = tie((values, [share.made for share in flying]))
        for share, item in zip(flying, made):
            share.made = item
            share.send()
        return values


def own_rows(total, core):
    halves = total.reshape(2, total.shape[0] // 2, total.shape[1])
    mine, other = pick(halves, core), swap_core(pick(halves, 1 - core))
    return jnp.stack(in_order(core, mine, other))


def tp_backward(
    incoming, incoming_low, kept, mats, gain_one, gain_two, slopes, valid, spot, scalars, flow
):
    stream, normed, joint, context, middle, normed_two, upper, hidden = kept
    (joint_out, jo), (expand, ex), (reduce, re) = mats
    d_upper = piece_dot_back(incoming_low, reduce, re, 128, upper=upper)
    d_normed = piece_dot_back(d_upper, expand, ex, 64)
    incoming, d_upper, d_normed = flow.turn(incoming, d_upper, d_normed)
    d_normed, g_reduce, g_expand = flow.add(
        (d_normed,), (hidden, incoming_low, spot, False), (normed_two, d_upper, spot, True)
    )
    d_middle, _, d_middle_low, d_gain_two = norm_backward(
        d_normed, swap_core(d_normed), middle, gain_two, incoming, scalars
    )
    mine, other = piece_dot_back(d_middle_low, joint_out, jo + 192, 64, split=True)
    mine, other, d_middle, d_middle_low = flow.turn(mine, other, d_middle, d_middle_low)
    d_joint = attend_back(
        joint, mine, swap_core(other), slopes, valid, stream.shape[1] // HEADS
    )
    d_normed = piece_dot_back(d_joint, joint_out, jo, 64)
    d_joint, d_normed = flow.turn(d_joint, d_normed)
    d_normed, g_output, g_joint = flow.add(
        (d_normed,), (context, d_middle_low, spot, False), (normed, d_joint, spot, True)
    )
    g_joint.beside = g_output
    result = norm_backward(d_normed, swap_core(d_normed), stream, gain_one, d_middle, scalars)
    return result, (g_joint, g_expand, g_reduce), d_gain_two


def paired_shards(
    spectra,
    gaussian,
    flow_times,
    lengths,
    span_flags,
    phone_ids,
    input_master,
    input_moment,
    input_square,
    kernel_master,
    kernel_moment,
    kernel_square,
    joint_master,
    joint_moment,
    joint_square,
    output_master,
    output_moment,
    output_square,
    expand_master,
    expand_moment,
    expand_square,
    reduce_master,
    reduce_moment,
    reduce_square,
    bridge_master,
    bridge_moment,
    bridge_square,
    readout_master,
    readout_moment,
    readout_square,
    gains_master,
    gains_moment,
    gains_square,
):
    dp_index, fsdp_index = lax.axis_index("dp"), lax.axis_index("fsdp")
    y, x = dp_index // 2, dp_index % 2
    z, core = fsdp_index // 2, fsdp_index % 2
    spot = (y, x)
    corners = [2 * y + x, 2 * y + 1 - x, 2 * (1 - y) + x, 2 * (1 - y) + 1 - x]
    behind = [(z - hops) % 4 for hops in range(4)]
    in_place = jnp.stack([*range(16), core]).astype(jnp.int32)
    all_shifted = [4 * corner + line for corner in corners for line in behind]
    all_shifted = jnp.stack([*all_shifted, core]).astype(jnp.int32)
    both_shifted = [4 * corner + line for line in behind for corner in corners]
    both_shifted = jnp.stack([*both_shifted, core]).astype(jnp.int32)
    chip = 8 * y + 4 * x + z
    mel_count, frame_count = spectra.shape[1:]
    taps, outs, group = kernel_master.shape
    width = outs * 32
    blocks = frame_count // TAPS_OUT

    with jax.named_scope("features"):
        flags = span_flags[0].astype(WIDE)
        valid_own = (jnp.arange(frame_count) < lengths[0]).astype(WIDE)
        clean, noise = spectra[0].astype(WIDE), gaussian[0].astype(WIDE)
        time = flow_times[0]
        noisy = (1.0 - (1.0 - SIGMA_MIN) * time) * noise + time * clean
        shown = clean * (1.0 - flags[None, :])
        small = jnp.concatenate(
            [readout_master.astype(LOW), gains_master.astype(LOW).T], 1
        )
        small = jnp.pad(small, ((0, 0), (0, frame_count - small.shape[1])))
        packed = jnp.concatenate(
            [
                noisy.astype(LOW),
                shown.astype(LOW),
                phone_ids.astype(LOW),
                valid_own[None].astype(LOW),
                jnp.zeros((14, frame_count), LOW),
                small,
            ],
            0,
        )
        line = z_line(packed, z)
        beside, across = swap_x(line), swap_y(line)
        corner = swap_y(beside)
        whole = jnp.zeros((4,) + line.shape, LOW)
        for number, part in enumerate((line, beside, across, corner)):
            whole = lax.dynamic_update_index_in_dim(whole, part, corners[number], 0)
        whole = whole.reshape((16,) + packed.shape)
        whole = jnp.stack(in_order(core, whole, swap_core(whole)), 1)
        whole = whole.reshape((32,) + packed.shape)
        mels = whole[:, : 2 * mel_count]
        onehot = (whole[:, 2 * mel_count][:, None, :] == jnp.arange(VOCAB, dtype=LOW)[None, :, None]).astype(LOW)
        features = jnp.concatenate([mels, onehot], 1)
        valid_all = whole[:, 2 * mel_count + 1].astype(WIDE)
        small = whole[:, 2 * mel_count + 16 :].reshape(width, frame_count)
        readout_full = small[:, :mel_count]
        gains_full = small[:, mel_count : mel_count + 5].T.astype(WIDE)

    with jax.named_scope("weights"):
        layers, rows = joint_master.shape[:2]
        tiles = expand_master.shape[2] // (2 * 128 * 4)
        cut_joint = joint_master.astype(LOW).reshape(layers, rows, 3, 2, LANES)
        cut_output = output_master.astype(LOW).reshape(layers, rows, 1, 2, LANES)
        cut_expand = expand_master.astype(LOW).reshape(layers, rows, tiles, 4, 2, 128)
        cut_bridge = bridge_master.astype(LOW).reshape(2, rows, 2, LANES)

        def columns_of(which):
            joint = lax.dynamic_index_in_dim(cut_joint, which, 3, keepdims=False)
            out = lax.dynamic_index_in_dim(cut_output, which, 3, keepdims=False)
            expand = lax.dynamic_index_in_dim(cut_expand, which, 4, keepdims=False)
            expand = expand.reshape(layers, rows, tiles, LANES)
            bridge = lax.dynamic_index_in_dim(cut_bridge, which, 2, keepdims=False)
            blocks = jnp.concatenate([joint, out, expand], 2).transpose(0, 2, 1, 3)
            blocks = blocks.reshape(layers * (4 + tiles), rows, LANES)
            return jnp.concatenate([blocks, bridge], 0)

        mine, other = in_order(core, columns_of(core), swap_core(columns_of(1 - core)))
        blocks = layers * (4 + tiles)
        paired = jnp.stack([mine[:blocks], other[:blocks]], 1)
        paired = paired.reshape(layers, 4 + tiles, 2 * rows, LANES)
        bridge = jnp.concatenate([mine[blocks:], other[blocks:]], 0).reshape(-1, LANES)
        lowered = reduce_master.astype(LOW).reshape(layers, -1, 2, LANES)
        lowered = lowered.transpose(0, 2, 1, 3).reshape(layers, -1, LANES)

        def flat(item):
            return item.reshape(-1, LANES)

        def along_z(own):
            parts = [own]
            for _ in range(3):
                parts.append(shift_z(parts[-1], 1))
            return parts

        def by_permutes(own, after_line, after_square, x_first):
            line = jnp.concatenate(along_z(tie((own, after_line))[0]), 0)
            line = tie((line, after_square))[0]
            beside, across = swap_x(line), swap_y(line)
            corner = swap_y(beside) if x_first else swap_x(across)
            whole = jnp.concatenate([line, beside, across, corner], 0)
            return line, (beside, across), (whole.reshape((16,) + own.shape), all_shifted)

        same_core = [[half + 2 * i for i in range(16)] for half in range(2)]

        def in_background(*parts):
            own = jnp.concatenate(parts, 0)
            whole = lax.all_gather(own, BOTH, axis=0, axis_index_groups=same_core)
            return whole, in_place

        third = in_background(lowered[0], bridge, flat(paired[1, :4]))
        fourth = in_background(lowered[1])
        first_line, first_square, first = by_permutes(flat(paired[0, :4]), line, line, True)
        last_own = tie((flat(paired[1, 4:]), line))[0]
        beside, across = swap_x(last_own), swap_y(last_own)
        square = jnp.concatenate([last_own, beside, across, swap_y(beside)], 0)
        second_line, _, second = by_permutes(
            flat(paired[0, 4:]), first_line, first_square, False
        )
        last = along_z(tie((square, second_line))[0])
        fifth = (jnp.concatenate(last, 0).reshape((16,) + last_own.shape), both_shifted)
        mats_zero = ((first, 0), (second, 0), (third, 0))
        mats_one = ((third, lowered.shape[1] + bridge.shape[0]), (fifth, 0), (fourth, 0))
        bridge_mat = (third, lowered.shape[1])

    with jax.named_scope("embedding"):
        columns = input_master.astype(LOW)
        columns = jnp.concatenate(in_order(core, columns, swap_core(columns)), -1)
        start = jnp.einsum("nzv,zr->nvr", features, columns, preferred_element_type=WIDE)
        start = start * valid_all[:, :, None]
        padded = start.astype(LOW).reshape(32, blocks, TAPS_OUT, 2, outs)
        padded = padded.transpose(0, 1, 3, 2, 4).reshape(32, blocks, TAPS_OUT * group)
        padded = jnp.pad(padded, ((0, 0), (2, 2), (0, 0)))
        windows = jnp.concatenate([padded[:, i : i + blocks] for i in range(5)], -1)
        windows = windows.reshape(32 * blocks, 5 * TAPS_OUT * group)
        turned = jnp.pad(
            kernel_master.astype(LOW).transpose(0, 2, 1), ((TAPS_OUT, TAPS_OUT), (0, 0), (0, 0))
        )
        banded = jnp.stack([turned[7 - j : 47 - j] for j in range(TAPS_OUT)], 2)
        banded = banded.reshape(5, TAPS_OUT, 2, outs, TAPS_OUT * outs).transpose(0, 2, 1, 3, 4)
        banded = banded.reshape(5, TAPS_OUT * group, TAPS_OUT * outs)
        conv_out = banded_dot(windows, banded)
        strided = features.reshape(32, -1, blocks, TAPS_OUT).transpose(3, 1, 0, 2)
        strided = strided.reshape(TAPS_OUT, -1, 32 * blocks)
        valid_rows = valid_all.reshape(32 * blocks, TAPS_OUT)
        conv_out, strided, valid_rows = tie((conv_out, strided, valid_rows))
        start_own = lax.dynamic_slice_in_dim(start, core * outs, outs, 2)
        start_own = start_own.reshape(32 * blocks, TAPS_OUT * outs)
        embedded = start_own + jax.nn.gelu(conv_out)
        embedded = lax.all_to_all(embedded.astype(LOW), BOTH, 0, 0, tiled=True)
        embedded = embedded.reshape(32, frame_count, outs).transpose(1, 0, 2)
        embedded = embedded.reshape(frame_count, width)
        embedded = jnp.concatenate(in_order(core, embedded, swap_core(embedded)), 0)
        embedded = embedded.astype(WIDE)

    slopes = 2.0 ** (
        -8.0 * (jnp.arange(HEADS // 2) + core * (HEADS // 2) + 1.0).astype(WIDE) / HEADS
    )
    valid = lax.dynamic_slice_in_dim(valid_all, 2 * chip, 2, 0)[:, None, :]
    scalars = in_place
    gain = [gains_full[row : row + 1] for row in range(5)]

    with jax.named_scope("forward_layers"):
        embedded, normed = norm_forward(embedded, None, None, gain[0], scalars, False)
        middle, lowered, kept_zero = tp_forward(
            embedded, normed, mats_zero, gain[1], slopes, valid, scalars, last[2]
        )
        encoded = middle + (lowered + swap_core(lowered))
        joined = jnp.concatenate([encoded, embedded], -1).astype(LOW)
        joined, _ = tie((joined, last[3]))
        bridged = piece_dot(joined, *bridge_mat, 128, 1)
        bridged, normed = norm_forward(
            None, bridged, swap_core(bridged), gain[2], scalars, True
        )
        middle, lowered, kept_one = tp_forward(
            bridged, normed, mats_one, gain[3], slopes, valid, scalars
        )
        decoded = middle + (lowered + swap_core(lowered))

    with jax.named_scope("readout_loss"):
        last = pick(decoded.reshape(2, frame_count, width), core)
        final_low = (norm_parts(last) * gains_full[4]).astype(LOW)
        predict = jnp.dot(final_low, readout_full, preferred_element_type=WIDE)
        target = (clean - (1.0 - SIGMA_MIN) * noise).T
        weight = (flags * valid_own)[:, None]
        missed = predict - target
        loss_local = jnp.sum(weight * missed * missed)
        count_local = jnp.sum(weight)
        d_predict = (2.0 * weight * missed).astype(LOW)
        d_readout = lax.dot_general(
            final_low, d_predict, (((0,), (0,)), ((), ())), preferred_element_type=WIDE
        )
        d_final = lax.dot_general(
            d_predict, readout_full, (((1,), (1,)), ((), ())), preferred_element_type=WIDE
        )
        back, gain_terms = norm_back(last, gains_full[4], d_final)
        d_gain_last = jnp.sum(gain_terms, 0)
        d_decoded = jnp.concatenate(in_order(core, back, swap_core(back)), 0)

    with jax.named_scope("backward_layers"):
        flow = Flow()
        parts = (slopes, valid, spot, scalars, flow)
        result, shares_one, d_gain_three = tp_backward(
            d_decoded, d_decoded.astype(LOW), kept_one, mats_one, gain[2], gain[3], *parts
        )
        d_gain_two = result[3]
        d_joined = piece_dot_back(result[2], *bridge_mat, 128)
        d_joined, d_bridged_low = flow.turn(d_joined, result[2])
        d_joined, g_bridge = flow.add((d_joined,), (joined, d_bridged_low, spot, True))
        d_joined = d_joined + swap_core(d_joined.astype(LOW)).astype(WIDE)
        d_encoded = d_joined[:, :width]
        result, shares_zero, d_gain_one = tp_backward(
            d_encoded, d_encoded.astype(LOW), kept_zero, mats_zero, gain[0], gain[1], *parts
        )
        d_stream, d_gain_zero = result[0], result[3]

    with jax.named_scope("embedding_back"):
        d_gains = jnp.concatenate(
            [d_gain_zero, d_gain_one, d_gain_two, d_gain_three, d_gain_last[None]], 0
        )
        d_gains = jnp.pad(d_gains, ((0, 3), (0, 0)))
        both = packed_exchange(d_stream, d_joined, d_readout, d_gains, scalars)
        (both,) = flow.turn(both)
        (both,) = flow.turn(both)
        own_sent = both = both.reshape(64 * blocks, TAPS_OUT * outs)
        both = lax.all_to_all(both, BOTH, 0, 0, tiled=True)
        both = both.reshape(32, 2 * blocks, TAPS_OUT * outs)
        own = both[:, :blocks].reshape(32 * blocks, TAPS_OUT * outs)
        mine, other, spread = banded_back(own, conv_out, windows, banded, scalars)
        small = tie((both[:, blocks:], mine))[0]
        grad_kernel = kernel_grad(spread, taps, outs, scalars)
        mine, other, grad_kernel, shares_zero[0].total = tie(
            (mine, other, grad_kernel, shares_zero[0].total)
        )
        grad_input = input_grad(own, mine, swap_core(other), valid_rows, strided, scalars)
        small = jnp.sum(small.astype(WIDE), 0)
        grad_readout = jnp.concatenate([small[:, :mel_count], small[:, 128 : 128 + mel_count]], 0)
        grad_gains = small[:5, 96 : 96 + outs]

    with jax.named_scope("own_grads"):
        shares = [*shares_zero, *shares_one, g_bridge]
        for share in shares:
            share.total = tie((share.total, own_sent))[0]

        def unfolded(both, count):
            cut = both.reshape(2, both.shape[1], count, both.shape[2] // count)
            return jnp.moveaxis(cut, 0, 2).reshape(both.shape[1], 2 * both.shape[2])

        layer_grads = []
        last_total = tie((shares_zero[0].total, grad_input))[0]
        for joint_share, expand_share, reduce_share in (shares_zero, shares_one):
            joint_total = last_total if joint_share is shares_zero[0] else joint_share.total
            both = own_rows(joint_total, core)
            layer_grads.append(
                (
                    unfolded(both[:, :, : 3 * LANES], 3),
                    unfolded(both[:, :, 3 * LANES :], 1),
                    unfolded(own_rows(expand_share.total, core), 4 * tiles),
                    reduce_share.total,
                )
            )
        grads = [
            grad_input,
            grad_kernel,
            *[jnp.stack(pair) for pair in zip(*layer_grads)],
            unfolded(own_rows(g_bridge.total, core), 1),
            grad_readout,
            grad_gains,
        ]

    with jax.named_scope("clip_and_update"):
        early = squares_of([share.total for share in shares[1:]], scalars)
        row = lax.broadcasted_iota(jnp.int32, (8, 128), 0)
        lane = lax.broadcasted_iota(jnp.int32, (8, 128), 1)
        told = jnp.where(row == 1, loss_local, jnp.where(row == 2, count_local, 0.0))
        early = early + jnp.where(lane == 0, told, 0.0)
        late = [shares[0].total, grad_input, grad_kernel, grad_readout, grad_gains]
        totals = squares_of(late, scalars, (early,))
        totals = jnp.broadcast_to(totals[None], (32, 8, 128)).reshape(256, 128)
        totals = lax.all_to_all(totals, BOTH, 0, 0, tiled=True)
        masters = (
            input_master.T,
            kernel_master,
            joint_master,
            output_master,
            expand_master,
            reduce_master,
            bridge_master,
            readout_master,
            gains_master,
        )
        moments = (
            input_moment.T,
            kernel_moment,
            joint_moment,
            output_moment,
            expand_moment,
            reduce_moment,
            bridge_moment,
            readout_moment,
            gains_moment,
        )
        squares = (
            input_square.T,
            kernel_square,
            joint_square,
            output_square,
            expand_square,
            reduce_square,
            bridge_square,
            readout_square,
            gains_square,
        )
        stats, results = all_updates(
            totals, list(zip(masters, moments, squares, grads)), scalars
        )
        results[:3] = [item.T for item in results[:3]]
        loss_sum, frame_total, grad_norm = stats[0, 0], stats[1, 0], stats[2, 0]
    return (loss_sum, frame_total, grad_norm, *results)


def solution(mesh):
    in_specs = (
        P(("dp", "fsdp"), None, None),
        P(("dp", "fsdp"), None, None),
        P(("dp", "fsdp")),
        P(("dp", "fsdp")),
        P(("dp", "fsdp"), None),
        P(("dp", "fsdp"), None),
        P(None, ("dp", "fsdp")),
        P(None, ("dp", "fsdp")),
        P(None, ("dp", "fsdp")),
        P(None, ("dp", "fsdp"), None),
        P(None, ("dp", "fsdp"), None),
        P(None, ("dp", "fsdp"), None),
        P(None, ("dp", "fsdp"), None),
        P(None, ("dp", "fsdp"), None),
        P(None, ("dp", "fsdp"), None),
        P(None, ("dp", "fsdp"), None),
        P(None, ("dp", "fsdp"), None),
        P(None, ("dp", "fsdp"), None),
        P(None, ("dp", "fsdp"), None),
        P(None, ("dp", "fsdp"), None),
        P(None, ("dp", "fsdp"), None),
        P(None, ("dp", "fsdp"), None),
        P(None, ("dp", "fsdp"), None),
        P(None, ("dp", "fsdp"), None),
        P(("dp", "fsdp"), None),
        P(("dp", "fsdp"), None),
        P(("dp", "fsdp"), None),
        P(("dp", "fsdp"), None),
        P(("dp", "fsdp"), None),
        P(("dp", "fsdp"), None),
        P(None, ("dp", "fsdp")),
        P(None, ("dp", "fsdp")),
        P(None, ("dp", "fsdp")),
    )
    out_specs = (
        P(),
        P(),
        P(),
        P(None, ("dp", "fsdp")),
        P(None, ("dp", "fsdp")),
        P(None, ("dp", "fsdp")),
        P(None, ("dp", "fsdp"), None),
        P(None, ("dp", "fsdp"), None),
        P(None, ("dp", "fsdp"), None),
        P(None, ("dp", "fsdp"), None),
        P(None, ("dp", "fsdp"), None),
        P(None, ("dp", "fsdp"), None),
        P(None, ("dp", "fsdp"), None),
        P(None, ("dp", "fsdp"), None),
        P(None, ("dp", "fsdp"), None),
        P(None, ("dp", "fsdp"), None),
        P(None, ("dp", "fsdp"), None),
        P(None, ("dp", "fsdp"), None),
        P(None, ("dp", "fsdp"), None),
        P(None, ("dp", "fsdp"), None),
        P(None, ("dp", "fsdp"), None),
        P(("dp", "fsdp"), None),
        P(("dp", "fsdp"), None),
        P(("dp", "fsdp"), None),
        P(("dp", "fsdp"), None),
        P(("dp", "fsdp"), None),
        P(("dp", "fsdp"), None),
        P(None, ("dp", "fsdp")),
        P(None, ("dp", "fsdp")),
        P(None, ("dp", "fsdp")),
    )
    paired = mesh.shape["dp"] == 4 and mesh.shape["fsdp"] == 8
    step = paired_shards if paired else shards
    return jax.shard_map(step, mesh=mesh, in_specs=in_specs, out_specs=out_specs, check_vma=False)
```
